32 devices in a mesh: dp: 16 (over z, y, core), shard: 2 (over x).
Axes of the slice: x: 2, y: 2, z: 4, core: 2. Of those that a mesh axis runs over, the one named last changes fastest.
Arguments:
- tokens: bfloat16 [2, 32, 577, 768], P(None, ('dp', 'shard')), may hold values from -6 to 6
- lengths: int32 [2, 32], P(None, ('dp', 'shard')), may hold values from 197 to 577, as said below
- selected: int32 [2, 32, 288], P(None, ('dp', 'shard')), may hold values from 0 to 576, as said below
- cotangent: bfloat16 [2, 32, 577, 768], P(None, ('dp', 'shard')), may hold values from -6 to 6
- attn_gain: bfloat16 [768], P(('dp', 'shard')), may hold values from 0.5 to 1.5
- attn_shift: bfloat16 [768], P(('dp', 'shard')), may hold values from -3 to 3
- mlp_gain: bfloat16 [768], P(('dp', 'shard')), may hold values from 0.5 to 1.5
- mlp_shift: bfloat16 [768], P(('dp', 'shard')), may hold values from -3 to 3
- router_weight: bfloat16 [768], P(('dp', 'shard')), may hold values from -0.21875 to 0.21875
- qkv_weight: bfloat16 [768, 2304], P(('dp', 'shard')), may hold values from -0.21875 to 0.21875
- out_weight: bfloat16 [768, 768], P(('dp', 'shard')), may hold values from -1.75 to 1.75
- up_weight: bfloat16 [768, 3072], P(('dp', 'shard')), may hold values from -0.21875 to 0.21875
- up_bias: bfloat16 [3072], P(('dp', 'shard')), may hold values from -3 to 3
- down_weight: bfloat16 [3072, 768], P(('dp', 'shard')), may hold values from -0.109375 to 0.109375
- down_bias: bfloat16 [768], P(('dp', 'shard')), may hold values from -3 to 3
Outputs:
- layer_output: bfloat16 [2, 32, 577, 768], P(None, ('dp', 'shard'))
- input_grad: bfloat16 [2, 32, 577, 768], P(None, ('dp', 'shard'))
- attn_gain_grad: float32 [768], P(('dp', 'shard'))
- attn_shift_grad: float32 [768], P(('dp', 'shard'))
- mlp_gain_grad: float32 [768], P(('dp', 'shard'))
- mlp_shift_grad: float32 [768], P(('dp', 'shard'))
- router_weight_grad: float32 [768], P(('dp', 'shard'))
- qkv_weight_grad: float32 [768, 2304], P(('dp', 'shard'))
- out_weight_grad: float32 [768, 768], P(('dp', 'shard'))
- up_weight_grad: float32 [768, 3072], P(('dp', 'shard'))
- up_bias_grad: float32 [3072], P(('dp', 'shard'))
- down_weight_grad: float32 [3072, 768], P(('dp', 'shard'))
- down_bias_grad: float32 [768], P(('dp', 'shard'))
The draws below stay inside these ranges and needn't reach their ends.
Inputs may be any that keep to these rules, and one draw needn't show every extreme that they name: `lengths`: each image holds 197 or 577 patches; both occur in every draw. `selected`: for an image of length n the first n // 2 entries are distinct positions below n in increasing order; the remaining entries are 0; in every draw some image of 577 patches selects position 576.
All inputs are finite; a program needn't handle non-finite values.
Results may differ from the reference program's by a relative error of at most 0.0095.
Values may be sent and summed in bfloat16 or wider, within the bound.
A program may use at most 192 MiB of HBM per device.

```python
import jax
import jax.numpy as jnp
from jax import lax

D = 768
HEADS = 12
HEAD_DIM = 64
FF = 3072
LONG = 577
SHORT = 197
MICRO = 2
IMG_DEV = 1
CAP = 288
IMAGES = 32


def image_layout(key):
    total_images = MICRO * IMAGES
    key_bits, key_pick, key_perm = jax.random.split(key, 3)
    long_bits = jax.random.randint(key_bits, (total_images,), 0, 2)
    lengths_all = jnp.where(long_bits == 1, LONG, SHORT)
    indices = jnp.arange(total_images)
    picked_image = jax.random.randint(key_pick, (), 0, total_images)
    lengths_all = jnp.where(indices == picked_image, LONG, lengths_all)
    lengths_all = jnp.where(indices == (picked_image + 1) % total_images, SHORT, lengths_all)
    permuted = jax.vmap(lambda subkey: jax.random.permutation(subkey, LONG))(jax.random.split(key_perm, total_images))
    position = jnp.arange(LONG)
    ranking = jnp.where(position[None, :] < lengths_all[:, None], permuted, LONG + position[None, :])
    forced = (indices[:, None] == picked_image) & (position[None, :] == LONG - 1)
    ranking = jnp.where(forced, -1, ranking)
    ordered = jnp.argsort(ranking, axis=1, stable=True)[:, :CAP]
    counts = lengths_all // 2
    slot_index = jnp.arange(CAP)
    chosen = jnp.where(slot_index[None, :] < counts[:, None], ordered, LONG)
    chosen = jnp.sort(chosen, axis=1)
    chosen = jnp.where(slot_index[None, :] < counts[:, None], chosen, 0)
    return (lengths_all.reshape(MICRO, IMAGES).astype(jnp.int32), chosen.reshape(MICRO, IMAGES, CAP).astype(jnp.int32))


def draw_lengths(key, part):
    lengths_all, chosen = image_layout(key)
    return lengths_all


def draw_selected(key, part):
    lengths_all, chosen = image_layout(key)
    return chosen


def levels(rng, dims, cuts, least, high):
    gain, own = 1.0, jax.random.fold_in(rng, 6)
    for axis_at, blocks in cuts:
        draws = jnp.exp(jax.random.uniform(jax.random.fold_in(own, axis_at), (blocks,), jnp.float32, least / len(cuts), high / len(cuts)))
        gain = gain * jnp.repeat(draws, dims[axis_at] // blocks).reshape([-1 if axis == axis_at else 1 for axis in range(len(dims))])
    return gain


def gaussian(key, extent, spread, most, cuts=(), dtype=jnp.bfloat16):
    drawn = jax.random.normal(key, extent, jnp.float32) * spread
    if len(cuts) > 0:
        drawn = levels(key, extent, cuts, -0.22, 0.18) * drawn
    return jnp.clip(drawn, min=-most, max=most).astype(dtype)


def setup_inputs(seed: int = 0) -> dict:
    splits = jax.random.split(jax.random.key(seed), 16)
    tokens = gaussian(splits[0], (MICRO, IMAGES, LONG, D), 1.0, 6.0, ((1, 32),))
    lengths = draw_lengths(jax.random.fold_in(splits[15], 71), 0)
    selected = draw_selected(jax.random.fold_in(splits[15], 71), 0)
    cotangent = gaussian(splits[3], (MICRO, IMAGES, LONG, D), 1.0, 6.0, ((1, 32),))
    attn_gain = jnp.clip(1.0 + 0.1 * jax.random.normal(splits[4], (D,), jnp.float32), 0.5, 1.5).astype(jnp.bfloat16)
    attn_shift = gaussian(splits[5], (D,), 0.3, 3.0, ((0, 32),))
    mlp_gain = jnp.clip(1.0 + 0.1 * jax.random.normal(splits[6], (D,), jnp.float32), 0.5, 1.5).astype(jnp.bfloat16)
    mlp_shift = gaussian(splits[7], (D,), 0.3, 3.0, ((0, 32),))
    router_weight = gaussian(splits[8], (D,), D ** -0.5, 0.21875, ((0, 32),))
    qkv_weight = gaussian(splits[9], (D, 3 * D), D ** -0.5, 0.21875, ((0, 32),))
    out_weight = gaussian(splits[10], (D, D), (D // 64) ** -0.5, 1.75, ((0, 32),))
    up_weight = gaussian(splits[11], (D, FF), D ** -0.5, 0.21875, ((0, 32),))
    up_bias = gaussian(splits[12], (FF,), 0.3, 3.0, ((0, 32),))
    down_weight = gaussian(splits[13], (FF, D), FF ** -0.5, 0.109375, ((0, 32),))
    down_bias = gaussian(splits[14], (D,), 0.3, 3.0, ((0, 32),))
    return {"tokens": tokens, "lengths": lengths, "selected": selected, "cotangent": cotangent, "attn_gain": attn_gain, "attn_shift": attn_shift, "mlp_gain": mlp_gain, "mlp_shift": mlp_shift, "router_weight": router_weight, "qkv_weight": qkv_weight, "out_weight": out_weight, "up_weight": up_weight, "up_bias": up_bias, "down_weight": down_weight, "down_bias": down_bias}


@jax.custom_vjp
def low(v):
    return lax.optimization_barrier(v.astype(jnp.bfloat16)).astype(jnp.float32)

@jax.custom_vjp
def low_back(v):
    return v

def low_keep(v):
    return (low(v), None)

def low_pass(kept, grad):
    return (grad,)

def back_keep(v):
    return (v, None)

def back_low(kept, grad):
    return (low(grad),)
low.defvjp(low_keep, low_pass)
low_back.defvjp(back_keep, back_low)
highest = lax.Precision.HIGHEST
epsilon = 1e-06

def normalize(inputs, norm_gain, norm_shift):
    centered = inputs - lax.optimization_barrier(jnp.mean(inputs, axis=-1, keepdims=True))
    variance = lax.optimization_barrier(jnp.mean(centered * centered, axis=-1, keepdims=True))
    return centered * lax.rsqrt(variance + epsilon) * norm_gain + norm_shift

def image_block(group_tokens, group_lengths, group_selected, weights):
    attn_gain, attn_shift, mlp_gain, mlp_shift, router_weight, qkv_weight, out_weight, up_weight, up_bias, down_weight, down_bias = weights
    group_size, capacity = group_selected.shape
    counts = group_lengths // 2
    live_mask = (jnp.arange(capacity)[None, :] < counts[:, None]).astype(jnp.float32)
    chosen = jnp.take_along_axis(group_tokens, group_selected[:, :, None], axis=1)
    logits = jnp.einsum('bcd,d->bc', chosen, router_weight, precision=highest)
    router_gate = jax.nn.sigmoid(logits)
    normed = low(normalize(chosen, attn_gain, attn_shift))
    projected = low(low_back(jnp.einsum('bcd,de->bce', normed, qkv_weight, precision=highest)))
    projected = projected.reshape(group_size, capacity, 3, HEADS, HEAD_DIM)
    queries = projected[:, :, 0]
    key_rows = projected[:, :, 1]
    value_rows = projected[:, :, 2]
    scores = jnp.einsum('bqhe,bkhe->bhqk', queries, key_rows, precision=highest) * HEAD_DIM ** (-0.5)
    scores = low_back(jnp.where(live_mask[:, None, None, :] > 0, scores, -1000000000.0))
    row_max = lax.optimization_barrier(jnp.max(scores, axis=-1, keepdims=True))
    exponent = jnp.exp(scores - row_max)
    attention = low(exponent / lax.optimization_barrier(jnp.sum(exponent, axis=-1, keepdims=True)))
    attended = jnp.einsum('bhqk,bkhe->bqhe', attention, value_rows, precision=highest)
    attended = low(low_back(attended.reshape(group_size, capacity, HEADS * HEAD_DIM)))
    attn_out = low_back(jnp.einsum('bce,ed->bcd', attended, out_weight, precision=highest))
    hidden = chosen + attn_out
    normed_two = low(normalize(hidden, mlp_gain, mlp_shift))
    upward = low_back(jnp.einsum('bcd,df->bcf', normed_two, up_weight, precision=highest) + up_bias)
    active = low(jax.nn.gelu(upward))
    feed_out = low_back(jnp.einsum('bcf,fd->bcd', active, down_weight, precision=highest) + down_bias)
    change = (attn_out + feed_out) * (router_gate * live_mask)[:, :, None]
    image_rows = jnp.arange(group_size)[:, None]
    return group_tokens.at[image_rows, group_selected].add(change)

def reference(tokens, lengths, selected, cotangent, attn_gain, attn_shift, mlp_gain, mlp_shift, router_weight, qkv_weight, out_weight, up_weight, up_bias, down_weight, down_bias):
    weights = (attn_gain.astype(jnp.float32), attn_shift.astype(jnp.float32), mlp_gain.astype(jnp.float32), mlp_shift.astype(jnp.float32), router_weight.astype(jnp.float32), qkv_weight.astype(jnp.float32), out_weight.astype(jnp.float32), up_weight.astype(jnp.float32), up_bias.astype(jnp.float32), down_weight.astype(jnp.float32), down_bias.astype(jnp.float32))
    block_count = MICRO * IMAGES // IMG_DEV
    token_blocks = tokens.reshape(block_count, IMG_DEV, LONG, D)
    length_blocks = lengths.reshape(block_count, IMG_DEV)
    selected_blocks = selected.reshape(block_count, IMG_DEV, CAP)
    cotangent_blocks = cotangent.reshape(block_count, IMG_DEV, LONG, D)

    def scan_step(totals, pieces):
        block_tokens, block_lengths, block_selected, block_cotangent = pieces

        def forward_block(inputs, params):
            return image_block(inputs, block_lengths, block_selected, params)
        output, pullback = jax.vjp(forward_block, block_tokens.astype(jnp.float32), weights)
        token_grad, grad_terms = pullback(block_cotangent.astype(jnp.float32))
        totals = jax.tree.map(jnp.add, totals, grad_terms)
        return (totals, (output.astype(jnp.bfloat16), token_grad.astype(jnp.bfloat16)))
    starting = tuple((jnp.zeros_like(weight_item) for weight_item in weights))
    totals, (outputs, token_grads) = lax.scan(scan_step, starting, (token_blocks, length_blocks, selected_blocks, cotangent_blocks))
    return (outputs.reshape(MICRO, IMAGES, LONG, D), token_grads.reshape(MICRO, IMAGES, LONG, D), totals[0], totals[1], totals[2], totals[3], totals[4], totals[5], totals[6], totals[7], totals[8], totals[9], totals[10])
```

```python
import functools
import itertools

import jax
import jax.numpy as jnp
from jax import lax
from jax.experimental import pallas as pl
from jax.experimental.pallas import tpu as pltpu
from jax.sharding import PartitionSpec as P

HEADS = 12
HEAD_DIM = 64
MICRO = 2


epsilon = 1e-06


def normalize(inputs, norm_gain, norm_shift):
    centered = inputs - jnp.mean(inputs, axis=-1, keepdims=True)
    variance = jnp.mean(centered * centered, axis=-1, keepdims=True)
    return centered * lax.rsqrt(variance + epsilon) * norm_gain + norm_shift


def forward_pass(tokens, lengths, selected, weights):
    (
        attn_gain,
        attn_shift,
        mlp_gain,
        mlp_shift,
        router_weight,
        qkv_weight,
        out_weight,
        up_weight,
        up_bias,
        down_weight,
        down_bias,
    ) = weights
    group_size, capacity = selected.shape
    counts = lengths // 2
    live_mask = (jnp.arange(capacity)[None, :] < counts[:, None]).astype(jnp.float32)
    chosen = jnp.take_along_axis(tokens, selected[:, :, None], axis=1)
    chosen_wide = chosen.astype(jnp.float32)
    logits = jnp.einsum("bcd,d->bc", chosen, router_weight, preferred_element_type=jnp.float32)
    router_gate = jax.nn.sigmoid(logits)
    normed = normalize(
        chosen_wide, attn_gain.astype(jnp.float32), attn_shift.astype(jnp.float32)
    ).astype(jnp.bfloat16)
    projected = jnp.einsum(
        "bcd,de->bce", normed, qkv_weight, preferred_element_type=jnp.float32
    ).astype(jnp.bfloat16)
    projected = projected.reshape(group_size, capacity, 3, HEADS, HEAD_DIM)
    queries = projected[:, :, 0]
    key_rows = projected[:, :, 1]
    value_rows = projected[:, :, 2]
    score_scale = HEAD_DIM ** (-0.5)
    scores = (
        jnp.einsum("bqhe,bkhe->bhqk", queries, key_rows, preferred_element_type=jnp.float32)
        * score_scale
    )
    scores = jnp.where(live_mask[:, None, None, :] > 0, scores, -1000000000.0)
    row_max = jnp.max(scores, axis=-1, keepdims=True)
    exponent = jnp.exp(scores - row_max)
    row_total = jnp.sum(exponent, axis=-1, keepdims=True)
    attention = (exponent / row_total).astype(jnp.bfloat16)
    log_total = row_max + jnp.log(row_total)
    attended = jnp.einsum(
        "bhqk,bkhe->bqhe", attention, value_rows, preferred_element_type=jnp.float32
    ).astype(jnp.bfloat16)
    attended = attended.reshape(group_size, capacity, HEADS * HEAD_DIM)
    attn_out = jnp.einsum("bce,ed->bcd", attended, out_weight, preferred_element_type=jnp.float32)
    hidden = chosen_wide + attn_out
    normed_two = normalize(
        hidden, mlp_gain.astype(jnp.float32), mlp_shift.astype(jnp.float32)
    ).astype(jnp.bfloat16)
    upward = jnp.einsum(
        "bcd,df->bcf", normed_two, up_weight, preferred_element_type=jnp.float32
    ) + up_bias.astype(jnp.float32)
    active = jax.nn.gelu(upward).astype(jnp.bfloat16)
    feed_out = jnp.einsum(
        "bcf,fd->bcd", active, down_weight, preferred_element_type=jnp.float32
    ) + down_bias.astype(jnp.float32)
    change = (attn_out + feed_out) * (router_gate * live_mask)[:, :, None]
    image_rows = jnp.arange(group_size)[:, None]
    output = tokens.astype(jnp.float32).at[image_rows, selected].add(change).astype(jnp.bfloat16)
    kept_values = (
        chosen_wide,
        live_mask,
        router_gate,
        normed,
        projected,
        log_total,
        attended,
        attn_out,
        hidden,
        normed_two,
        upward,
        active,
        feed_out,
    )
    return (output, kept_values)


def backward_pass(cotangent, selected, weights, kept_values):
    (
        attn_gain,
        attn_shift,
        mlp_gain,
        mlp_shift,
        router_weight,
        qkv_weight,
        out_weight,
        up_weight,
        up_bias,
        down_weight,
        down_bias,
    ) = weights
    (
        chosen_wide,
        live_mask,
        router_gate,
        normed,
        projected,
        log_total,
        attended,
        attn_out,
        hidden,
        normed_two,
        upward,
        active,
        feed_out,
    ) = kept_values
    group_size, capacity = selected.shape
    out_grad = cotangent.astype(jnp.float32)
    picked = jnp.take_along_axis(out_grad, selected[:, :, None], axis=1) * live_mask[:, :, None]
    gate_grad = jnp.sum(picked * (attn_out + feed_out), axis=-1)
    logit_grad = gate_grad * router_gate * (1.0 - router_gate)
    change_grad = picked * router_gate[:, :, None]
    feed_grad = change_grad.astype(jnp.bfloat16)
    down_bias_grad = jnp.sum(feed_grad.astype(jnp.float32), axis=(0, 1))
    down_weight_grad = jnp.einsum(
        "bcf,bcd->fd", active, feed_grad, preferred_element_type=jnp.float32
    )
    active_grad = jnp.einsum(
        "bcd,fd->bcf", feed_grad, down_weight, preferred_element_type=jnp.float32
    )
    primal_out, gelu_back = jax.vjp(jax.nn.gelu, upward)
    upward_grad = gelu_back(active_grad)[0].astype(jnp.bfloat16)
    up_bias_grad = jnp.sum(upward_grad.astype(jnp.float32), axis=(0, 1))
    up_weight_grad = jnp.einsum(
        "bcd,bcf->df", normed_two, upward_grad, preferred_element_type=jnp.float32
    )
    normed_two_grad = jnp.einsum(
        "bcf,df->bcd", upward_grad, up_weight, preferred_element_type=jnp.float32
    )
    primal_two, norm_back = jax.vjp(
        normalize, hidden, mlp_gain.astype(jnp.float32), mlp_shift.astype(jnp.float32)
    )
    hidden_grad, mlp_gain_grad, mlp_shift_grad = norm_back(normed_two_grad)
    attn_grad = (change_grad + hidden_grad).astype(jnp.bfloat16)
    out_weight_grad = jnp.einsum(
        "bce,bcd->ed", attended, attn_grad, preferred_element_type=jnp.float32
    )
    attended_grad = jnp.einsum(
        "bcd,ed->bce", attn_grad, out_weight, preferred_element_type=jnp.float32
    ).astype(jnp.bfloat16)
    attended_grad = attended_grad.reshape(group_size, capacity, HEADS, HEAD_DIM)
    queries = projected[:, :, 0]
    key_rows = projected[:, :, 1]
    value_rows = projected[:, :, 2]
    score_scale = HEAD_DIM ** (-0.5)
    key_live = live_mask[:, None, None, :] > 0
    scores = (
        jnp.einsum("bqhe,bkhe->bhqk", queries, key_rows, preferred_element_type=jnp.float32)
        * score_scale
    )
    scores = jnp.where(key_live, scores, -1000000000.0)
    prob_wide = jnp.exp(scores - log_total)
    prob_low = prob_wide.astype(jnp.bfloat16)
    value_grad = jnp.einsum(
        "bhqk,bqhe->bkhe", prob_low, attended_grad, preferred_element_type=jnp.float32
    )
    prob_grad = jnp.einsum(
        "bqhe,bkhe->bhqk", attended_grad, value_rows, preferred_element_type=jnp.float32
    )
    score_grad = prob_wide * (prob_grad - jnp.sum(prob_wide * prob_grad, axis=-1, keepdims=True))
    score_grad = jnp.where(key_live, score_grad.astype(jnp.bfloat16), 0.0) * score_scale
    query_grad = jnp.einsum(
        "bhqk,bkhe->bqhe", score_grad, key_rows, preferred_element_type=jnp.float32
    )
    key_grad = jnp.einsum(
        "bhqk,bqhe->bkhe", score_grad, queries, preferred_element_type=jnp.float32
    )
    projected_grad = jnp.stack([query_grad, key_grad, value_grad], axis=2).astype(jnp.bfloat16)
    projected_grad = projected_grad.reshape(group_size, capacity, 3 * HEADS * HEAD_DIM)
    qkv_weight_grad = jnp.einsum(
        "bcd,bce->de", normed, projected_grad, preferred_element_type=jnp.float32
    )
    normed_grad = jnp.einsum(
        "bce,de->bcd", projected_grad, qkv_weight, preferred_element_type=jnp.float32
    )
    primal_one, first_back = jax.vjp(
        normalize, chosen_wide, attn_gain.astype(jnp.float32), attn_shift.astype(jnp.float32)
    )
    chosen_grad, attn_gain_grad, attn_shift_grad = first_back(normed_grad)
    chosen_grad = (
        chosen_grad + hidden_grad + logit_grad[:, :, None] * router_weight.astype(jnp.float32)
    )
    router_weight_grad = jnp.einsum(
        "bc,bcd->d", logit_grad, chosen_wide, precision=lax.Precision.HIGHEST
    )
    image_rows = jnp.arange(group_size)[:, None]
    token_grad = out_grad.at[image_rows, selected].add(chosen_grad).astype(jnp.bfloat16)
    grad_terms = (
        attn_gain_grad,
        attn_shift_grad,
        mlp_gain_grad,
        mlp_shift_grad,
        router_weight_grad,
        qkv_weight_grad,
        out_weight_grad,
        up_weight_grad,
        up_bias_grad,
        down_weight_grad,
        down_bias_grad,
    )
    return (token_grad, grad_terms)


MESH=pl.DeviceIdType.MESH
TYPES=(("ZXY",0,16),("XZY",16,32),("ZYX",48,16),("YZX",64,32))
PHASES=3; SH=32; CH=96
STRIDE=16
def events():
    out=[]
    size={"X":2,"Y":2,"Z":4}
    for p in range(PHASES):
        for t,(perm,_,_) in enumerate(TYPES):
            n1,n2=size[perm[0]],size[perm[1]]
            for a in range(3):
                for o in range(1,size[perm[a]]):
                    for combo in itertools.product(*[range(size[q]) for q in perm[:a]]):
                        e={"X":0,"Y":0,"Z":0}; e[perm[a]]=o
                        for q,v in zip(perm[:a],combo): e[q]=v
                        if a==0: pos=e[perm[0]]
                        elif a==1: pos=n1+(e[perm[1]]-1)*n1+e[perm[0]]
                        else: pos=n1*n2+(e[perm[2]]-1)*n1*n2+e[perm[1]]*n1+e[perm[0]]
                        out.append((p*STRIDE+pos+0.01*t,(p,t,e["X"],e["Y"],e["Z"],a)))
    for p in range(PHASES): out.append((p*STRIDE-2,("own",p)))
    out.sort(key=lambda q:q[0])
    return [q[1] for q in out]
class Place:
    def __init__(self):
        dp=lax.axis_index("dp"); self.x=lax.axis_index("shard"); self.dp=dp
        self.c=dp%2; self.y=(dp//2)%2; self.z=dp//4
        z=self.z
        self.mid=((z+1)//2)%2
        self.zs=[z, z+1-2*(z%2), 2-z//2, 3-3*(z//2)]
        self.zp=self.zs[1]; self.zq=3-z
        self.me=dp*2+self.x
    def dev(self,k):
        dp,x=self.dp,self.x
        if k=="C": return (dp+1-2*self.c,x)
        if k=="X": return (dp,1-x)
        if k=="Y": return (dp+2-4*self.y,x)
        if k=="P": return (self.zp*4+self.y*2+self.c,x)
        if k=="Q": return (self.zq*4+self.y*2+self.c,x)
    def src(self,xo,yo,j):
        sx=self.x if xo==0 else 1-self.x
        sy=self.y if yo==0 else 1-self.y
        sz=self.zs[j]
        chip=(sz*2+sy)*2+sx
        shard=((sz*2+sy)*2+self.c)*2+sx
        return chip,shard
def barrier(pc):
    b=pltpu.get_barrier_semaphore()
    for k in "CXYP":
        pl.semaphore_signal(b,inc=1,device_id=pc.dev(k),device_id_type=MESH)
    @pl.when(pc.mid==1)
    def _(): pl.semaphore_signal(b,inc=1,device_id=pc.dev("Q"),device_id_type=MESH)
    pl.semaphore_wait(b,4+pc.mid)
LINK={"C":0,"X":1,"Y":2,"P":3,"Q":4}
class Gather:
    def __init__(self,pc,buf,recv,crecv,send):
        self.pc,self.buf,self.recv,self.crecv,self.send=pc,buf,recv,crecv,send
        self.rows={k:0 for k in "CXY"}; self.zrows={"end":{"P":0,"Q":0},"mid":{"P":0,"Q":0}}
    def block(self,p,t,shard):
        _,r0,n=TYPES[t]
        return self.buf.at[pl.ds(pl.multiple_of((p*SH+shard)*CH+r0,16),n),:]
    def copy(self,p,t,chip,shard,k):
        b=self.block(p,t,shard)
        rs=self.crecv.at[p] if k=="C" else self.recv.at[p,t,chip]
        return pltpu.make_async_remote_copy(b,b,self.send.at[LINK[k]],rs,device_id=self.pc.dev(k),device_id_type=MESH)
    def forward(self,p,t,xo,yo,j,last):
        pc=self.pc; perm,_,n=TYPES[t]
        chip,shard=pc.src(xo,yo,j)
        if perm.index("Z")>=last:
            if j==0:
                self.copy(p,t,chip,shard,"P").start()
                self.zrows["end"]["P"]+=n; self.zrows["mid"]["P"]+=n
            k="Q" if j in(0,1) else "P"
            self.zrows["mid"][k]+=n
            @pl.when(pc.mid==1)
            def _(): self.copy(p,t,chip,shard,k).start()
        for k in "XY":
            if k in perm[last+1:]:
                self.copy(p,t,chip,shard,k).start(); self.rows[k]+=n
        self.copy(p,t,chip,shard,"C").start(); self.rows["C"]+=n
    def own(self,p):
        for t in range(len(TYPES)): self.forward(p,t,0,0,0,-1)
    def step(self,ev):
        if ev[0]=="own": return self.own(ev[1])
        p,t,xo,yo,j,a=ev
        chip,shard=self.pc.src(xo,yo,j)
        b=self.block(p,t,shard)
        pltpu.make_async_remote_copy(b,b,self.send.at[1],self.recv.at[p,t,chip],device_id=self.pc.dev("X"),device_id_type=MESH).wait_recv()
        self.forward(p,t,xo,yo,j,a)
    def phase_done(self,p):
        b=self.buf.at[pl.ds(0,16*CH),:]
        pltpu.make_async_remote_copy(b,b,self.send.at[0],self.crecv.at[p],device_id=self.pc.dev("C"),device_id_type=MESH).wait_recv()
    def wait_send(self,k,rows):
        if rows==0: return
        b=self.buf.at[pl.ds(0,rows),:]
        pltpu.make_async_remote_copy(b,b,self.send.at[LINK[k]],self.crecv.at[0],device_id=self.pc.dev(k),device_id_type=MESH).wait_send()
    def finish(self):
        for k in "CXY": self.wait_send(k,self.rows[k])
        @pl.when(self.pc.mid==1)
        def _():
            for k in "PQ": self.wait_send(k,self.zrows["mid"][k])
        @pl.when(self.pc.mid==0)
        def _():
            for k in "PQ": self.wait_send(k,self.zrows["end"][k])
def ag_kernel(x_ref,o_ref,buf,lsem,osem,recv,crecv,send):
    pc=Place()
    loc=[]
    for p in range(PHASES):
        cp=pltpu.make_async_copy(x_ref.at[p],buf.at[pl.ds(pl.multiple_of((p*SH+pc.me)*CH,16),CH),:],lsem.at[p]); cp.start(); loc.append(cp)
    barrier(pc)
    for cp in loc: cp.wait()
    g=Gather(pc,buf,recv,crecv,send)
    evs=events()
    lastev={p:max(i for i,e in enumerate(evs) if e[0]==p) for p in range(PHASES)}
    outs=[]
    for i,e in enumerate(evs):
        g.step(e)
        for p in range(PHASES):
            if lastev[p]==i:
                g.phase_done(p)
                cp=pltpu.make_async_copy(buf.at[pl.ds(p*SH*CH,SH*CH),:],o_ref.at[pl.ds(p*SH*CH,SH*CH),:],osem.at[p]); cp.start(); outs.append(cp)
    g.finish()
    for cp in outs: cp.wait()
def gather_weights(packed):
    return pl.pallas_call(ag_kernel,out_shape=jax.ShapeDtypeStruct((PHASES*SH*CH,768),jnp.bfloat16),
        in_specs=[pl.BlockSpec(memory_space=pl.ANY)],out_specs=pl.BlockSpec(memory_space=pl.ANY),
        scratch_shapes=[pltpu.VMEM((PHASES*SH*CH,768),jnp.bfloat16),pltpu.SemaphoreType.DMA((PHASES,)),pltpu.SemaphoreType.DMA((PHASES,)),
            pltpu.SemaphoreType.DMA((PHASES,len(TYPES),16)),pltpu.SemaphoreType.DMA((PHASES,)),pltpu.SemaphoreType.DMA((5,))],
        compiler_params=pltpu.CompilerParams(collective_id=0,has_side_effects=True,vmem_limit_bytes=40<<20))(packed)


class Landing:
    def __init__(self):
        self.off={}; self.n=0; self.sem={}
        for p in range(PHASES):
            for t,(perm,_,n) in enumerate(TYPES):
                for k in "XY":
                    a=perm.index(k)
                    for j in range(4):
                        for o in range(2):
                            other="Y" if k=="X" else "X"
                            if j and perm.index("Z")>a: continue
                            if o and perm.index(other)>a: continue
                            self.add((p,t,k,j,o),n)
                a=perm.index("Z")
                for xo in range(2):
                    for yo in range(2):
                        if xo and perm.index("X")>a: continue
                        if yo and perm.index("Y")>a: continue
                        for s in range(5): self.add((p,t,"Z",xo,yo,s),n)
    def add(self,key,n):
        self.off[key]=self.n; self.n+=n; self.sem[key]=len(self.sem)
class Reduce:
    def __init__(self,pc,buf,land,cland,recv,crecv,send,out):
        self.pc,self.buf,self.land,self.cland,self.recv,self.crecv,self.send,self.out=pc,buf,land,cland,recv,crecv,send,out
        self.L=Landing(); self.cdone=set()
        self.rows={k:0 for k in "CXY"}; self.zrows={"end":{"P":0,"Q":0},"mid":{"P":0,"Q":0}}
    def block(self,p,t,shard):
        _,r0,n=TYPES[t]
        return self.buf.at[pl.ds(pl.multiple_of((p*SH+shard)*CH+r0,16),n),:]
    def slot(self,off,n):
        return self.land.at[pl.ds(off if isinstance(off,int) else pl.multiple_of(off,16),n),:]
    def cslot(self,p,xo,yo,j):
        return (p*16+(j*2+yo)*2+xo)
    def csend(self,p,offsets):
        pc=self.pc
        for (xo,yo,j) in offsets:
            chip,shard=pc.src(xo,yo,j)
            other=shard+2-4*pc.c
            s=self.cslot(p,xo,yo,j)
            pltpu.make_async_remote_copy(self.buf.at[pl.ds(pl.multiple_of((p*SH+other)*CH,16),CH),:],self.cland.at[pl.ds(s*CH,CH),:],
                self.send.at[0],self.crecv.at[s],device_id=pc.dev("C"),device_id_type=MESH).start()
            self.rows["C"]+=CH
    def arrive(self,key):
        n=TYPES[key[1]][2]; r=self.slot(self.L.off[key],n)
        pltpu.make_async_remote_copy(r,r,self.send.at[1],self.recv.at[self.L.sem[key]],device_id=self.pc.dev("X"),device_id_type=MESH).wait_recv()
        return r
    def total(self,p,t,xo,yo,j,last):
        pc=self.pc; perm,r0,n=TYPES[t]
        chip,shard=pc.src(xo,yo,j)
        b=self.block(p,t,shard)
        s=self.cslot(p,xo,yo,j)
        if s not in self.cdone:
            self.cdone.add(s)
            r=self.cland.at[pl.ds(s*CH,CH),:]
            pltpu.make_async_remote_copy(r,r,self.send.at[0],self.crecv.at[s],device_id=pc.dev("C"),device_id_type=MESH).wait_recv()
        acc=b[...].astype(jnp.float32)+self.cland[s*CH+r0:s*CH+r0+n,:].astype(jnp.float32)
        for k in "XY":
            if k in perm[last+1:]:
                acc=acc+self.arrive((p,t,k,j,yo if k=="X" else xo))[...].astype(jnp.float32)
        if perm.index("Z")>=last:
            if j==0:
                acc=acc+self.arrive((p,t,"Z",xo,yo,0))[...].astype(jnp.float32)
                ms=1
            else: ms=1+j
            return acc,b,(p,t,"Z",xo,yo,ms)
        return acc,b,None
    def step(self,ev):
        pc=self.pc
        if ev[0]=="own":
            p=ev[1]
            for t in range(len(TYPES)):
                _,r0,n=TYPES[t]
                acc,b,mk=self.total(p,t,0,0,0,-1)
                self.out[p,r0:r0+n,:]=acc
                @pl.when(pc.mid==1)
                def _(): self.out[p,r0:r0+n,:]=self.out[p,r0:r0+n,:]+self.arrive(mk)[...].astype(jnp.float32)
            return
        p,t,xo,yo,j,a=ev
        perm,r0,n=TYPES[t]
        acc,b,mk=self.total(p,t,xo,yo,j,a)
        b[...]=acc.astype(jnp.bfloat16)
        if mk is not None:
            @pl.when(pc.mid==1)
            def _(): b[...]=(b[...].astype(jnp.float32)+self.arrive(mk)[...].astype(jnp.float32)).astype(jnp.bfloat16)
        L=self.L
        k=perm[a]
        def go(off,sem,link,dev):
            pltpu.make_async_remote_copy(b,self.slot(off,n),self.send.at[LINK[link]],self.recv.at[sem],device_id=dev,device_id_type=MESH).start()
        if k in "XY":
            key=(p,t,k,j,yo if k=="X" else xo)
            go(L.off[key],L.sem[key],k,pc.dev(k)); self.rows[k]+=n
        elif j==1:
            key=(p,t,"Z",xo,yo,0)
            go(L.off[key],L.sem[key],"P",pc.dev("P")); self.zrows["end"]["P"]+=n; self.zrows["mid"]["P"]+=n
        else:
            ek=(p,t,"Z",xo,yo,1+j); mk2=(p,t,"Z",xo,yo,j-1)
            @pl.when(pc.mid==0)
            def _(): go(L.off[ek],L.sem[ek],"P",pc.dev("P"))
            @pl.when(pc.mid==1)
            def _(): go(L.off[mk2],L.sem[mk2],"Q",pc.dev("Q"))
            self.zrows["end"]["P"]+=n; self.zrows["mid"]["Q"]+=n
    def wait_send(self,k,rows):
        if rows==0: return
        b=self.buf.at[pl.ds(0,rows),:]
        pltpu.make_async_remote_copy(b,b,self.send.at[LINK[k]],self.crecv.at[0],device_id=self.pc.dev(k),device_id_type=MESH).wait_send()
    def finish(self):
        for k in "CXY": self.wait_send(k,self.rows[k])
        for m,name in ((1,"mid"),(0,"end")):
            @pl.when(self.pc.mid==m)
            def _():
                for k in "PQ": self.wait_send(k,self.zrows[name][k])
def offsets_order(evs,p):
    seen=[]
    for e in evs:
        if e[0]=="own":
            o=(0,0,0) if e[1]==p else None
        else: o=(e[2],e[3],e[4]) if e[0]==p else None
        if o is not None and o not in seen: seen.append(o)
    return seen
NSEM=len(Landing().sem)
def rs_kernel(x_ref,o_ref,buf,land,cland,obuf,lsem,osem,recv,crecv,send):
    pc=Place()
    loc={}
    evs=events()[::-1]
    order=[]
    for e in evs:
        p=e[1] if e[0]=="own" else e[0]
        if p not in order: order.append(p)
    for p in order:
        cp=pltpu.make_async_copy(x_ref.at[pl.ds(p*SH*CH,SH*CH),:],buf.at[pl.ds(p*SH*CH,SH*CH),:],lsem.at[p]); cp.start(); loc[p]=cp
    barrier(pc)
    r=Reduce(pc,buf,land,cland,recv,crecv,send,obuf)
    first={p:min(i for i,e in enumerate(evs) if (e[1] if e[0]=="own" else e[0])==p) for p in order}
    for i,e in enumerate(evs):
        for p in order:
            if max(0,first[p]-20)==i:
                loc[p].wait()
                r.csend(p,offsets_order(evs,p))
        r.step(e)
    cp=pltpu.make_async_copy(obuf,o_ref,osem.at[0]); cp.start()
    r.finish()
    cp.wait()
def reduce_grads(parts):
    nl=Landing().n
    return pl.pallas_call(rs_kernel,out_shape=jax.ShapeDtypeStruct((PHASES,CH,768),jnp.float32),
        in_specs=[pl.BlockSpec(memory_space=pl.ANY)],out_specs=pl.BlockSpec(memory_space=pl.ANY),
        scratch_shapes=[pltpu.VMEM((PHASES*SH*CH,768),jnp.bfloat16),pltpu.VMEM((nl,768),jnp.bfloat16),pltpu.VMEM((PHASES*16*CH,768),jnp.bfloat16),
            pltpu.VMEM((PHASES,CH,768),jnp.float32),
            pltpu.SemaphoreType.DMA((PHASES,)),pltpu.SemaphoreType.DMA((1,)),
            pltpu.SemaphoreType.DMA((NSEM,)),pltpu.SemaphoreType.DMA((PHASES*16,)),pltpu.SemaphoreType.DMA((5,))],
        compiler_params=pltpu.CompilerParams(collective_id=1,has_side_effects=True,vmem_limit_bytes=56<<20))(parts)

SMALL = ("attn_gain", "attn_shift", "mlp_gain", "mlp_shift", "router_weight", "down_bias", "up_bias")


def slab(weight):
    rows = weight.shape[0]
    return weight.reshape(rows, 4, 768).transpose(1, 0, 2).reshape(4 * rows, 768)


def unslab(blocks):
    count, rows, width = blocks.shape
    return blocks.reshape(count, 4, rows // 4, width).transpose(0, 2, 1, 3).reshape(count * rows // 4, 4 * width)


def reslab(grad):
    rows = grad.shape[0] // 32
    return grad.reshape(32, rows, 4, 768).transpose(0, 2, 1, 3).reshape(32, 4 * rows, 768)


def on_device_fast(tokens, lengths, selected, cotangent, attn_gain, attn_shift, mlp_gain, mlp_shift, router_weight,
                   qkv_weight, out_weight, up_weight, up_bias, down_weight, down_bias):
    both = ("dp", "shard")
    packed = jnp.stack([slab(jnp.concatenate([qkv_weight, out_weight], axis=1)), slab(up_weight), down_weight])
    gathered = gather_weights(packed).reshape(PHASES, SH, CH, 768)
    small = jnp.concatenate([attn_gain, attn_shift, mlp_gain, mlp_shift, router_weight, down_bias, up_bias])
    small = lax.all_gather(small, both, axis=0, tiled=False)
    ag, ash, mg, ms, rw, db = [small[:, 24 * i : 24 * i + 24].reshape(768) for i in range(6)]
    ub = small[:, 144:].reshape(3072)
    first = unslab(gathered[0])
    weights = (ag, ash, mg, ms, rw, first[:, :2304], first[:, 2304:], unslab(gathered[1]), ub, gathered[2].reshape(3072, 768), db)
    output, kept = forward_pass(tokens[:, 0], lengths[:, 0], selected[:, 0], weights)
    token_grad, terms = backward_pass(cotangent[:, 0], selected[:, 0], weights, kept)
    gag, gash, gmg, gms, grw, gqkv, gout, gup, gub, gdown, gdb = terms
    low = jnp.bfloat16
    parts = jnp.stack([
        reslab(jnp.concatenate([gqkv.astype(low), gout.astype(low)], axis=1)),
        reslab(gup.astype(low)),
        gdown.astype(low).reshape(SH, CH, 768),
    ]).reshape(PHASES * SH * CH, 768)
    owned = reduce_grads(parts)
    tiny = jnp.concatenate([v.reshape(32, -1) for v in (gag, gash, gmg, gms, grw, gdb, gub)], axis=1)
    tiny = lax.psum_scatter(tiny, both, scatter_dimension=0, tiled=False)
    oqkv = unslab(owned[0:1])
    t = [tiny[24 * i : 24 * i + 24] for i in range(6)]
    return (output[:, None], token_grad[:, None], t[0], t[1], t[2], t[3], t[4], oqkv[:, :2304], oqkv[:, 2304:],
            unslab(owned[1:2]), tiny[144:], owned[2], t[5])


def on_device(
    tokens,
    lengths,
    selected,
    cotangent,
    attn_gain,
    attn_shift,
    mlp_gain,
    mlp_shift,
    router_weight,
    qkv_weight,
    out_weight,
    up_weight,
    up_bias,
    down_weight,
    down_bias,
):
    outputs = []
    token_grads = []
    totals = None
    for micro_step in range(MICRO):
        forward_weights = (
            lax.all_gather(attn_gain, ("dp", "shard"), axis=0, tiled=True),
            lax.all_gather(attn_shift, ("dp", "shard"), axis=0, tiled=True),
            lax.all_gather(mlp_gain, ("dp", "shard"), axis=0, tiled=True),
            lax.all_gather(mlp_shift, ("dp", "shard"), axis=0, tiled=True),
            lax.all_gather(router_weight, ("dp", "shard"), axis=0, tiled=True),
            lax.all_gather(qkv_weight, ("dp", "shard"), axis=0, tiled=True),
            lax.all_gather(out_weight, ("dp", "shard"), axis=0, tiled=True),
            lax.all_gather(up_weight, ("dp", "shard"), axis=0, tiled=True),
            lax.all_gather(up_bias, ("dp", "shard"), axis=0, tiled=True),
            lax.all_gather(down_weight, ("dp", "shard"), axis=0, tiled=True),
            lax.all_gather(down_bias, ("dp", "shard"), axis=0, tiled=True),
        )
        output, kept_values = forward_pass(
            tokens[micro_step], lengths[micro_step], selected[micro_step], forward_weights
        )
        backward_weights = (
            lax.all_gather(attn_gain, ("dp", "shard"), axis=0, tiled=True),
            lax.all_gather(attn_shift, ("dp", "shard"), axis=0, tiled=True),
            lax.all_gather(mlp_gain, ("dp", "shard"), axis=0, tiled=True),
            lax.all_gather(mlp_shift, ("dp", "shard"), axis=0, tiled=True),
            lax.all_gather(router_weight, ("dp", "shard"), axis=0, tiled=True),
            lax.all_gather(qkv_weight, ("dp", "shard"), axis=0, tiled=True),
            lax.all_gather(out_weight, ("dp", "shard"), axis=0, tiled=True),
            lax.all_gather(up_weight, ("dp", "shard"), axis=0, tiled=True),
            lax.all_gather(up_bias, ("dp", "shard"), axis=0, tiled=True),
            lax.all_gather(down_weight, ("dp", "shard"), axis=0, tiled=True),
            lax.all_gather(down_bias, ("dp", "shard"), axis=0, tiled=True),
        )
        token_grad, grad_terms = backward_pass(
            cotangent[micro_step], selected[micro_step], backward_weights, kept_values
        )
        grad_terms = (
            lax.psum_scatter(grad_terms[0], ("dp", "shard"), scatter_dimension=0, tiled=True),
            lax.psum_scatter(grad_terms[1], ("dp", "shard"), scatter_dimension=0, tiled=True),
            lax.psum_scatter(grad_terms[2], ("dp", "shard"), scatter_dimension=0, tiled=True),
            lax.psum_scatter(grad_terms[3], ("dp", "shard"), scatter_dimension=0, tiled=True),
            lax.psum_scatter(grad_terms[4], ("dp", "shard"), scatter_dimension=0, tiled=True),
            lax.psum_scatter(grad_terms[5], ("dp", "shard"), scatter_dimension=0, tiled=True),
            lax.psum_scatter(grad_terms[6], ("dp", "shard"), scatter_dimension=0, tiled=True),
            lax.psum_scatter(grad_terms[7], ("dp", "shard"), scatter_dimension=0, tiled=True),
            lax.psum_scatter(grad_terms[8], ("dp", "shard"), scatter_dimension=0, tiled=True),
            lax.psum_scatter(grad_terms[9], ("dp", "shard"), scatter_dimension=0, tiled=True),
            lax.psum_scatter(grad_terms[10], ("dp", "shard"), scatter_dimension=0, tiled=True),
        )
        totals = grad_terms if totals is None else jax.tree.map(jnp.add, totals, grad_terms)
        outputs.append(output)
        token_grads.append(token_grad)
    return (
        jnp.stack(outputs),
        jnp.stack(token_grads),
        totals[0],
        totals[1],
        totals[2],
        totals[3],
        totals[4],
        totals[5],
        totals[6],
        totals[7],
        totals[8],
        totals[9],
        totals[10],
    )


def solution(mesh):
    fits = dict(mesh.shape) == {"dp": 16, "shard": 2}
    return jax.shard_map(
        on_device_fast if fits else on_device,
        mesh=mesh,
        in_specs=(
            P(None, ("dp", "shard"), None, None),
            P(None, ("dp", "shard")),
            P(None, ("dp", "shard"), None),
            P(None, ("dp", "shard"), None, None),
            P(("dp", "shard")),
            P(("dp", "shard")),
            P(("dp", "shard")),
            P(("dp", "shard")),
            P(("dp", "shard")),
            P(("dp", "shard"), None),
            P(("dp", "shard"), None),
            P(("dp", "shard"), None),
            P(("dp", "shard")),
            P(("dp", "shard"), None),
            P(("dp", "shard")),
        ),
        out_specs=(
            P(None, ("dp", "shard"), None, None),
            P(None, ("dp", "shard"), None, None),
            P(("dp", "shard")),
            P(("dp", "shard")),
            P(("dp", "shard")),
            P(("dp", "shard")),
            P(("dp", "shard")),
            P(("dp", "shard"), None),
            P(("dp", "shard"), None),
            P(("dp", "shard"), None),
            P(("dp", "shard")),
            P(("dp", "shard"), None),
            P(("dp", "shard")),
        ),
        check_vma=False,
    )
```

```python
import functools
import itertools
import math
import types

import jax
import jax.numpy as jnp
from jax import lax
from jax.experimental import pallas as pl
from jax.experimental.pallas import tpu as pltpu
from jax.sharding import PartitionSpec as P

F32, BF16 = jnp.float32, jnp.bfloat16
D, ROWS, CAP, LONG = 768, 576, 288, 577
SH, CH = 32, 96
NN = (((1,), (0,)), ((), ()))
NT = (((1,), (1,)), ((), ()))
TN = (((0,), (0,)), ((), ()))
def dot(a, b, dims=NN):
    return lax.dot_general(a, b, dims, preferred_element_type=F32)
def ln(rows):
    centered = rows - jnp.mean(rows, axis=-1, keepdims=True)
    rstd = lax.rsqrt(jnp.mean(centered * centered, axis=-1, keepdims=True) + 1e-6)
    return centered * rstd, rstd
def spread_onehot(sel_row):
    place = lax.broadcasted_iota(jnp.int32, (LONG, CAP), 0)
    return jnp.where(place == sel_row, 1.0, 0.0).astype(BF16)
def live_rows(lens, i):
    slot = lax.broadcasted_iota(jnp.int32, (CAP, 1), 0)
    return (slot < lax.shift_right_logical(lens[i : i + 1, :], 1)).astype(F32)
def live_cols(lens, i):
    slot = lax.broadcasted_iota(jnp.int32, (1, CAP), 1)
    return slot < lax.shift_right_logical(lens[i : i + 1, :], 1)
def relayout(G, W, p, lo, hi):
    for k in range(lo, hi):
        two = [G[(p * SH + 2 * k + u) * CH : (p * SH + 2 * k + u + 1) * CH, :].astype(F32) for u in range(2)]
        for j in range(4):
            W[D * j + 48 * k : D * j + 48 * k + 48, :] = jnp.concatenate([t[24 * j : 24 * j + 24, :] for t in two], axis=0).astype(BF16)
def fwd_tiles(R):
    T = []
    def add(name, cost, dep):
        def deco(f): T.append((name, cost, dep, f)); return f
        return deco
    for i in range(2):
        sl = slice(CAP * i, CAP * i + CAP)
        @add(f"pick{i}", 1.0, "tok")
        def _(i=i, sl=sl):
            oh = spread_onehot(R.sel[i : i + 1, :])
            R.chosen[sl, :] = dot(oh, R.tok[i], TN).astype(BF16)
            R.live[sl, :] = live_rows(R.lens, i)
            R.picked[sl, :] = (dot(oh, R.ct[i], TN) * R.live[sl, :]).astype(BF16)
    B = 96
    for b in range(ROWS // B):
        sl = slice(B * b, B * b + B)
        @add(f"norm{b}", 0.4, "vec")
        def _(sl=sl):
            ch = R.chosen[sl, :].astype(F32)
            xh, _ = ln(ch)
            R.normed[sl, :] = (xh * R.vec("attn_gain") + R.vec("attn_shift")).astype(BF16)
            logit = jnp.sum(ch * R.vec("router_weight"), axis=-1, keepdims=True)
            gate = 1.0 / (1.0 + jnp.exp(-logit))
            R.gate[sl, :] = gate
            feed = (gate * R.picked[sl, :].astype(F32)).astype(BF16)
            R.feed[sl, :] = feed
    for g in range(4):
        @add(f"relay0_{g}", 0.4, 0)
        def _(g=g): relayout(R.G, R.w0, 0, 4 * g, 4 * g + 4)
    for j in range(3):
        for n in range(3):
            @add(f"qkv{j}{n}", 0.45, 0)
            def _(j=j, n=n):
                cs = slice(256 * n, 256 * n + 256)
                R.proj(j)[:, cs] = dot(R.normed[...], R.W0(j)[:, cs]).astype(BF16)
    for i in range(2):
        sl = slice(CAP * i, CAP * i + CAP)
        for h in range(6):
            @add(f"attn{i}{h}", 1.0, 0)
            def _(i=i, h=h, sl=sl):
                cs = slice(128 * h, 128 * h + 128)
                q, k, v = R.proj(0)[sl, cs], R.proj(1)[sl, cs], R.proj(2)[sl, cs]
                low = lax.broadcasted_iota(jnp.int32, (CAP, 128), 1) < 64
                lane = lax.broadcasted_iota(jnp.int32, (CAP, 128), 1)
                live = live_cols(R.lens, i)
                zero = jnp.zeros_like(q)
                outs = []
                lse = R.lse[...] if h else jnp.zeros((CAP, 128), F32)
                for u in range(2):
                    qm = jnp.where(low, q, zero) if u == 0 else jnp.where(low, zero, q)
                    s = jnp.where(live, dot(qm, k, NT) * 0.125, -1e9)
                    m = jnp.max(s, axis=-1, keepdims=True)
                    e = jnp.exp(s - m)
                    tot = jnp.sum(e, axis=-1, keepdims=True)
                    outs.append(dot((e / tot).astype(BF16), v))
                    lse = jnp.where(lane == 2 * h + u, m + jnp.log(tot), lse)
                R.lse[...] = lse
                R.attended[sl, cs] = jnp.where(low, outs[0], outs[1]).astype(BF16)
                if h == 5:
                    R.lse_row[i] = jnp.transpose(lse)[:16, :]
    for n in range(3):
        @add(f"out{n}", 0.45, 0)
        def _(n=n):
            cs = slice(256 * n, 256 * n + 256)
            R.hidden[:, cs] = R.chosen[:, cs].astype(F32) + dot(R.attended[...], R.W0(3)[:, cs])
    for b in range(ROWS // B):
        sl = slice(B * b, B * b + B)
        @add(f"norm2{b}", 0.3, 0)
        def _(sl=sl):
            xh, _ = ln(R.hidden[sl, :])
            R.normed_two[sl, :] = (xh * R.vec("mlp_gain") + R.vec("mlp_shift")).astype(BF16)
    for g in range(4):
        @add(f"relay1_{g}", 0.4, 1)
        def _(g=g): relayout(R.G, R.w1, 1, 4 * g, 4 * g + 4)
    c0 = math.sqrt(2.0 / math.pi)
    for j in range(4):
        for n in range(3):
            @add(f"up{j}{n}", 1.2, 1)
            def _(j=j, n=n):
                cs = slice(256 * n, 256 * n + 256)
                u = dot(R.normed_two[...], R.W1(j)[:, cs]) + R.vec("up_bias", D * j + 256 * n, 256)
                uu = u * u
                t = jnp.tanh(c0 * u * (1.0 + 0.044715 * uu))
                half = 0.5 * (1.0 + t)
                R.act(j)[:, cs] = (u * half).astype(BF16)
                R.gp(j)[:, cs] = (half + 0.5 * u * (1.0 - t * t) * (c0 * (1.0 + 3 * 0.044715 * uu))).astype(BF16)
    for n in range(3):
        @add(f"down{n}", 1.6, 2)
        def _(n=n):
            cs = slice(256 * n, 256 * n + 256)
            acc = R.vec("down_bias", 256 * n, 256) + dot(R.act(0)[...], R.W2(0)[:, cs])
            for j in range(1, 4): acc = acc + dot(R.act(j)[...], R.W2(j)[:, cs])
            R.tmp[:, cs] = acc + (R.hidden[:, cs] - R.chosen[:, cs].astype(F32))
    for b in range(ROWS // B):
        sl = slice(B * b, B * b + B)
        @add(f"gate{b}", 0.3, 2)
        def _(sl=sl):
            d = R.tmp[sl, :]
            gate = R.gate[sl, :]
            R.logit[sl, :] = jnp.sum(R.picked[sl, :].astype(F32) * d, axis=-1, keepdims=True) * gate * (1.0 - gate)
            R.change[sl, :] = (d * (gate * R.live[sl, :])).astype(BF16)
    for i in range(2):
        sl = slice(CAP * i, CAP * i + CAP)
        @add(f"output{i}", 1.0, 2)
        def _(i=i, sl=sl):
            oh = spread_onehot(R.sel[i : i + 1, :])
            R.output(i, (R.tok[i].astype(F32) + dot(oh, R.change[sl, :])).astype(BF16))
    return T


def bwd_tiles(R):
    T = []
    def add(name, cost, dep=None):
        def deco(f): T.append((name, cost, dep, f)); return f
        return deco
    def grow(name, v, first, off=0):
        r, w = R.VEC[name]
        n = v.shape[1]
        if first: R.vterm[r : r + 1, off : off + n] = v
        else: R.vterm[r : r + 1, off : off + n] = R.vterm[r : r + 1, off : off + n] + v
    def colsum(v): return jnp.sum(v, axis=0, keepdims=True)
    def put_pair(p, half, cs, one, two):
        for s in range(SH):
            R.part(p)[s * CH + 48 * half : s * CH + 48 * half + 48, cs] = jnp.concatenate(
                [one[24 * s : 24 * s + 24, :], two[24 * s : 24 * s + 24, :]], axis=0).astype(BF16)
    B = 96
    for j in range(4):
        for n in range(3):
            @add(f"gdown{j}{n}", 0.55)
            def _(j=j, n=n):
                cs = slice(256 * n, 256 * n + 256)
                R.part(2)[D * j + 256 * n : D * j + 256 * n + 256, :] = dot(R.act(j)[:, cs], R.feed[...], TN).astype(BF16)
    @add("bdown", 0.2)
    def _():
        grow("down_bias", colsum(R.feed[...].astype(F32)), True)
    for j in range(4):
        for n in range(3):
            @add(f"gact{j}{n}", 0.6)
            def _(j=j, n=n):
                cs = slice(256 * n, 256 * n + 256)
                g = (dot(R.feed[...], R.W2(j)[cs, :], NT) * R.gp(j)[:, cs].astype(F32)).astype(BF16)
                R.gp(j)[:, cs] = g
                grow("up_bias", colsum(g.astype(F32)), True, D * j + 256 * n)
    @add("tn2", 0.6)
    def _(): R.trans[...] = jnp.transpose(R.normed_two[...])
    for h in range(2):
        for n in range(3):
            @add(f"gup{h}{n}", 1.2)
            def _(h=h, n=n):
                cs = slice(256 * n, 256 * n + 256)
                put_pair(1, h, cs, dot(R.trans[...], R.gp(2 * h)[:, cs]), dot(R.trans[...], R.gp(2 * h + 1)[:, cs]))
    for n in range(3):
        @add(f"gn2{n}", 1.6)
        def _(n=n):
            cs = slice(256 * n, 256 * n + 256)
            acc = dot(R.gp(0)[...], R.W1(0)[cs, :], NT)
            for j in range(1, 4): acc = acc + dot(R.gp(j)[...], R.W1(j)[cs, :], NT)
            R.tmp[:, cs] = acc
    for b in range(ROWS // B):
        sl = slice(B * b, B * b + B)
        @add(f"ln2b{b}", 0.5)
        def _(sl=sl, b=b):
            g = R.tmp[sl, :]
            xh, r = ln(R.hidden[sl, :])
            grow("mlp_gain", colsum(g * xh), b == 0)
            grow("mlp_shift", colsum(g), b == 0)
            e = g * R.vec("mlp_gain")
            hg = r * (e - jnp.mean(e, axis=-1, keepdims=True) - xh * jnp.mean(e * xh, axis=-1, keepdims=True))
            R.hidden[sl, :] = hg
            R.attn_grad[sl, :] = (R.gate[sl, :] * R.picked[sl, :].astype(F32) + hg).astype(BF16)
    for n in range(3):
        @add(f"gatt{n}", 0.45)
        def _(n=n):
            cs = slice(256 * n, 256 * n + 256)
            R.datt[:, cs] = dot(R.attn_grad[...], R.W0(3)[cs, :], NT).astype(BF16)
    for i in range(2):
        sl = slice(CAP * i, CAP * i + CAP)
        for h in range(6):
            @add(f"attb{i}{h}", 1.6)
            def _(i=i, h=h, sl=sl):
                cs = slice(128 * h, 128 * h + 128)
                q, k, v, do = R.proj(0)[sl, cs], R.proj(1)[sl, cs], R.proj(2)[sl, cs], R.datt[sl, cs]
                low = lax.broadcasted_iota(jnp.int32, (CAP, 128), 1) < 64
                live = live_rows(R.lens, i) > 0
                zero = jnp.zeros_like(q)
                def own(a, u): return jnp.where(low, a, zero) if u == 0 else jnp.where(low, zero, a)
                dq = dk = dv = None
                for u in range(2):
                    qm, km, dm = own(q, u), own(k, u), own(do, u)
                    s = dot(k, qm, NT) * 0.125 - R.lse_row[i, 2 * h + u : 2 * h + u + 1, :]
                    pt = jnp.where(live, jnp.exp(s), 0.0)
                    dp = dot(v, dm, NT)
                    w = pt * dp
                    ds = ((w - pt * colsum(w)) * 0.125).astype(BF16)
                    a, b, c = dot(pt.astype(BF16), dm), dot(ds, qm), dot(ds, km, TN)
                    dv, dk, dq = (a, b, c) if u == 0 else (dv + a, dk + b, dq + c)
                R.dproj(0)[sl, cs] = dq.astype(BF16)
                R.dproj(1)[sl, cs] = dk.astype(BF16)
                R.dproj(2)[sl, cs] = dv.astype(BF16)
    @add("tn1", 0.6)
    def _(): R.trans[...] = jnp.transpose(R.normed[...])
    for n in range(3):
        @add(f"gqk{n}", 1.2)
        def _(n=n):
            cs = slice(256 * n, 256 * n + 256)
            put_pair(0, 0, cs, dot(R.trans[...], R.dproj(0)[:, cs]), dot(R.trans[...], R.dproj(1)[:, cs]))
    for n in range(3):
        @add(f"gvo{n}", 1.5)
        def _(n=n):
            cs = slice(256 * n, 256 * n + 256)
            put_pair(0, 1, cs, dot(R.trans[...], R.dproj(2)[:, cs]), dot(R.attended[...], R.attn_grad[:, cs], TN))
    for n in range(3):
        @add(f"gn1{n}", 1.3)
        def _(n=n):
            cs = slice(256 * n, 256 * n + 256)
            acc = dot(R.dproj(0)[...], R.W0(0)[cs, :], NT)
            for j in range(1, 3): acc = acc + dot(R.dproj(j)[...], R.W0(j)[cs, :], NT)
            R.tmp[:, cs] = acc
    for b in range(ROWS // B):
        sl = slice(B * b, B * b + B)
        @add(f"ln1b{b}", 0.5)
        def _(sl=sl, b=b):
            g = R.tmp[sl, :]
            ch = R.chosen[sl, :].astype(F32)
            xh, r = ln(ch)
            grow("attn_gain", colsum(g * xh), b == 0)
            grow("attn_shift", colsum(g), b == 0)
            grow("router_weight", colsum(R.logit[sl, :] * ch), b == 0)
            e = g * R.vec("attn_gain")
            cg = r * (e - jnp.mean(e, axis=-1, keepdims=True) - xh * jnp.mean(e * xh, axis=-1, keepdims=True))
            R.attn_grad[sl, :] = (cg + R.hidden[sl, :] + R.logit[sl, :] * R.vec("router_weight")).astype(BF16)
    for i in range(2):
        sl = slice(CAP * i, CAP * i + CAP)
        @add(f"ingrad{i}", 1.0)
        def _(i=i, sl=sl):
            oh = spread_onehot(R.sel[i : i + 1, :])
            R.input_grad(i, (R.ct[i].astype(F32) + dot(oh, R.attn_grad[sl, :])).astype(BF16))
    return T


PHASES = 3
TYPES = (("ZXY", 0, 16), ("XZY", 16, 32), ("ZYX", 48, 16), ("YZX", 64, 32))
MESH = pl.DeviceIdType.MESH
LINK = {"C": 0, "X": 1, "Y": 2, "P": 3, "Q": 4}
NAMES = ("attn_gain", "attn_shift", "mlp_gain", "mlp_shift", "router_weight", "down_bias")
ROW = {name: k for k, name in enumerate(NAMES)} | {"up_bias": 6}
BASE = {2: 3072, 1: 0, 0: 6144}
VSTEPS = "CXYPW"


def all_events():
    out = []
    size = {"X": 2, "Y": 2, "Z": 4}
    for p in range(PHASES):
        for t, (perm, _, _) in enumerate(TYPES):
            for a in range(3):
                for o in range(1, size[perm[a]]):
                    for combo in itertools.product(*[range(size[q]) for q in perm[:a]]):
                        e = {"X": 0, "Y": 0, "Z": 0}
                        e[perm[a]] = o
                        for q, v in zip(perm[:a], combo):
                            e[q] = v
                        out.append((p, t, e["X"], e["Y"], e["Z"], a))
    return out


class Place:
    def __init__(self):
        dp = lax.axis_index("dp")
        self.x, self.dp = lax.axis_index("shard"), dp
        self.c, self.y, self.z = dp % 2, (dp // 2) % 2, dp // 4
        z = self.z
        self.mid = ((z + 1) // 2) % 2
        self.zs = [z, z + 1 - 2 * (z % 2), 2 - z // 2, 3 - 3 * (z // 2)]
        self.me = dp * 2 + self.x

    def dev(self, k):
        dp, x = self.dp, self.x
        if k == "C":
            return (dp + 1 - 2 * self.c, x)
        if k == "X":
            return (dp, 1 - x)
        if k == "Y":
            return (dp + 2 - 4 * self.y, x)
        z = {"P": self.zs[1], "Q": 3 - self.z, "W": (self.z + 2) % 4}[k]
        return (z * 4 + self.y * 2 + self.c, x)

    def src(self, xo, yo, j):
        sx = self.x if xo == 0 else 1 - self.x
        sy = self.y if yo == 0 else 1 - self.y
        sz = self.zs[j]
        return (sz * 2 + sy) * 2 + sx, ((sz * 2 + sy) * 2 + self.c) * 2 + sx

    def signal(self, sem, kinds):
        for k in kinds:
            if k == "Q":
                @pl.when(self.mid == 1)
                def _():
                    pl.semaphore_signal(sem, inc=1, device_id=self.dev("Q"), device_id_type=MESH)
            else:
                pl.semaphore_signal(sem, inc=1, device_id=self.dev(k), device_id_type=MESH)


class Traffic:
    def __init__(self, pc, ref, send, spare):
        self.pc, self.ref, self.send, self.spare = pc, ref, send, spare
        self.rows = {}

    def note(self, k, n, where="all"):
        self.rows[(k, where)] = self.rows.get((k, where), 0) + n

    def wait(self):
        def one(k, where):
            rows = self.rows.get((k, where), 0)
            if rows:
                b = self.ref.at[pl.ds(0, rows), :]
                pltpu.make_async_remote_copy(b, b, self.send.at[LINK[k]], self.spare, device_id=self.pc.dev("C"), device_id_type=MESH).wait_send()

        for k in "CXY":
            one(k, "all")
        for m, where in ((1, "mid"), (0, "end")):
            @pl.when(self.pc.mid == m)
            def _():
                for k in "PQ":
                    one(k, where)


class Gather:
    def __init__(self, pc, buf, recv, crecv, send):
        self.pc, self.buf, self.recv, self.crecv, self.send = pc, buf, recv, crecv, send
        self.traffic = [Traffic(pc, buf, send.at[p], crecv.at[p]) for p in range(PHASES)]

    def block(self, p, t, shard):
        _, r0, n = TYPES[t]
        return self.buf.at[pl.ds(pl.multiple_of((p * SH + shard) * CH + r0, 16), n), :]

    def copy(self, p, t, chip, shard, k):
        b = self.block(p, t, shard)
        rs = self.crecv.at[p] if k == "C" else self.recv.at[p, t, chip]
        return pltpu.make_async_remote_copy(b, b, self.send.at[p, LINK[k]], rs, device_id=self.pc.dev(k), device_id_type=MESH)

    def forward(self, p, t, xo, yo, j, last):
        pc, tr = self.pc, self.traffic[p]
        perm, _, n = TYPES[t]
        chip, shard = pc.src(xo, yo, j)
        if perm.index("Z") >= last:
            if j == 0:
                self.copy(p, t, chip, shard, "P").start()
                tr.note("P", n, "end")
                tr.note("P", n, "mid")
            k = "Q" if j in (0, 1) else "P"
            tr.note(k, n, "mid")

            @pl.when(pc.mid == 1)
            def _():
                self.copy(p, t, chip, shard, k).start()
        for k in "XY":
            if k in perm[last + 1 :]:
                self.copy(p, t, chip, shard, k).start()
                tr.note(k, n)
        self.copy(p, t, chip, shard, "C").start()
        tr.note("C", n)

    def own(self, p):
        for t in range(len(TYPES)):
            self.forward(p, t, 0, 0, 0, -1)

    def step(self, ev):
        p, t, xo, yo, j, a = ev
        chip, shard = self.pc.src(xo, yo, j)
        b = self.block(p, t, shard)
        pltpu.make_async_remote_copy(b, b, self.send.at[p, 1], self.recv.at[p, t, chip], device_id=self.pc.dev("X"), device_id_type=MESH).wait_recv()
        self.forward(p, t, xo, yo, j, a)

    def phase_done(self, p):
        b = self.buf.at[pl.ds(0, 16 * CH), :]
        pltpu.make_async_remote_copy(b, b, self.send.at[p, 0], self.crecv.at[p], device_id=self.pc.dev("C"), device_id_type=MESH).wait_recv()


class Landing:
    def __init__(self):
        self.off, self.n, self.sem = {}, 0, {}
        for t, (perm, _, n) in enumerate(TYPES):
            for k in "XY":
                a = perm.index(k)
                other = "Y" if k == "X" else "X"
                for j in range(4):
                    for o in range(2):
                        if (j and perm.index("Z") > a) or (o and perm.index(other) > a):
                            continue
                        self.add((t, k, j, o), n)
            a = perm.index("Z")
            for xo in range(2):
                for yo in range(2):
                    if (xo and perm.index("X") > a) or (yo and perm.index("Y") > a):
                        continue
                    for s in range(5):
                        self.add((t, "Z", xo, yo, s), n)

    def add(self, key, n):
        self.off[key] = self.n
        self.n += n
        self.sem[key] = len(self.sem)


LAND = Landing()


class Reduce:
    def __init__(self, pc, buf, land, cland, recv, crecv, send, out):
        self.pc, self.buf, self.land, self.cland, self.recv, self.crecv, self.send, self.out = pc, buf, land, cland, recv, crecv, send, out
        self.cdone = set()
        self.traffic = Traffic(pc, buf, send, crecv.at[0])

    def block(self, p, t, shard):
        _, r0, n = TYPES[t]
        return self.buf.at[pl.ds(pl.multiple_of(BASE[p] + shard * CH + r0, 16), n), :]

    def cslot(self, xo, yo, j):
        return (j * 2 + yo) * 2 + xo

    def csend(self, p, offsets):
        pc = self.pc
        for xo, yo, j in offsets:
            _, shard = pc.src(xo, yo, j)
            other = shard + 2 - 4 * pc.c
            s = self.cslot(xo, yo, j)
            pltpu.make_async_remote_copy(
                self.buf.at[pl.ds(pl.multiple_of(BASE[p] + other * CH, 16), CH), :], self.cland(p, s * CH, CH),
                self.send.at[0], self.crecv.at[p * 16 + s], device_id=pc.dev("C"), device_id_type=MESH).start()
            self.traffic.note("C", CH)

    def arrive(self, p, key):
        r = self.land(p, LAND.off[key], TYPES[key[0]][2])
        pltpu.make_async_remote_copy(r, r, self.send.at[1], self.recv.at[p, LAND.sem[key]], device_id=self.pc.dev("X"), device_id_type=MESH).wait_recv()
        return r[...].astype(F32)

    def total(self, p, t, xo, yo, j, last):
        pc = self.pc
        perm, r0, n = TYPES[t]
        _, shard = pc.src(xo, yo, j)
        b = self.block(p, t, shard)
        s = self.cslot(xo, yo, j)
        if (p, s) not in self.cdone:
            self.cdone.add((p, s))
            r = self.cland(p, s * CH, CH)
            pltpu.make_async_remote_copy(r, r, self.send.at[0], self.crecv.at[p * 16 + s], device_id=pc.dev("C"), device_id_type=MESH).wait_recv()
        acc = b[...].astype(F32) + self.cland(p, s * CH + r0, n)[...].astype(F32)
        for k in "XY":
            if k in perm[last + 1 :]:
                acc = acc + self.arrive(p, (t, k, j, yo if k == "X" else xo))
        middle = None
        if perm.index("Z") >= last:
            if j == 0:
                acc = acc + self.arrive(p, (t, "Z", xo, yo, 0))
            middle = (t, "Z", xo, yo, 1 if j == 0 else 1 + j)
        return acc, b, middle

    def own(self, p):
        for t, (_, r0, n) in enumerate(TYPES):
            acc, _, middle = self.total(p, t, 0, 0, 0, -1)
            rows = slice(p * CH + r0, p * CH + r0 + n)
            self.out[rows, :] = acc

            @pl.when(self.pc.mid == 1)
            def _():
                self.out[rows, :] = self.out[rows, :] + self.arrive(p, middle)

    def step(self, ev):
        pc = self.pc
        p, t, xo, yo, j, a = ev
        perm, _, n = TYPES[t]
        acc, b, middle = self.total(p, t, xo, yo, j, a)
        b[...] = acc.astype(BF16)
        if middle is not None:
            @pl.when(pc.mid == 1)
            def _():
                b[...] = (b[...].astype(F32) + self.arrive(p, middle)).astype(BF16)

        def go(key, k):
            pltpu.make_async_remote_copy(b, self.land(p, LAND.off[key], n), self.send.at[LINK[k]], self.recv.at[p, LAND.sem[key]],
                                         device_id=pc.dev(k), device_id_type=MESH).start()

        k = perm[a]
        if k in "XY":
            go((t, k, j, yo if k == "X" else xo), k)
            self.traffic.note(k, n)
        elif j == 1:
            go((t, "Z", xo, yo, 0), "P")
            self.traffic.note("P", n, "end")
            self.traffic.note("P", n, "mid")
        else:
            @pl.when(pc.mid == 0)
            def _():
                go((t, "Z", xo, yo, 1 + j), "P")

            @pl.when(pc.mid == 1)
            def _():
                go((t, "Z", xo, yo, j - 1), "Q")

            self.traffic.note("P", n, "end")
            self.traffic.note("Q", n, "mid")


class SmallSum:
    def __init__(self, pc, total, out, arrived, send, recv):
        self.pc, self.total, self.out, self.arrived, self.send, self.recv = pc, total, out, arrived, send, recv

    def copy(self, k):
        return pltpu.make_async_remote_copy(self.out.at[k], self.arrived.at[k], self.send.at[k], self.recv.at[k],
                                            device_id=self.pc.dev(VSTEPS[k]), device_id_type=MESH)

    def step(self, k):
        if k:
            self.copy(k - 1).wait_recv()
            self.total[...] = self.total[...] + self.arrived[k - 1]
        if k < 5:
            self.out[k] = self.total[...]
            self.copy(k).start()

    def finish(self):
        for k in range(5):
            self.copy(k).wait_send()


def lane(rows, columns, axis):
    return lax.broadcasted_iota(jnp.int32, (rows, columns), axis)


def group24(d):
    return lax.shift_right_logical(d * 2731, 16)


def group96(f):
    return lax.shift_right_logical(f * 683, 16)


def unpack_small(total, vecs):
    v = total[...].astype(BF16)
    d = lane(256, D, 1)
    mine = group24(lane(SH, D, 1)) == lane(SH, D, 0)
    for k in range(6):
        pick = jnp.where(lane(256, D, 0) == 24 * k + d - 24 * group24(d), 1.0, 0.0).astype(BF16)
        vecs[k : k + 1, 0:D] = jnp.sum(jnp.where(mine, dot(v, pick), 0.0), axis=0, keepdims=True)
    pick = jnp.where(lane(256, D, 0) == 144 + d - 96 * group96(d), 1.0, 0.0).astype(BF16)
    wide = dot(v, pick)
    for j in range(4):
        mine = group96(lane(SH, D, 1)) + 8 * j == lane(SH, D, 0)
        vecs[6:7, D * j : D * j + D] = jnp.sum(jnp.where(mine, wide, 0.0), axis=0, keepdims=True)


def wide_dot(a, b):
    return lax.dot_general(a, b, NN, precision=lax.Precision.HIGHEST, preferred_element_type=F32)


def pack_small(vterm, total):
    d = lane(D, 128, 0)
    place = jnp.where(lane(D, 128, 1) == d - 24 * group24(d), 1.0, 0.0).astype(F32)
    mine = group24(lane(SH, D, 1)) == lane(SH, D, 0)
    rows = jnp.concatenate([jnp.where(mine, vterm[k : k + 1, 0:D], 0.0) for k in range(6)], axis=0)
    parts = wide_dot(rows, place)
    place = jnp.where(lane(D, 128, 1) == d - 96 * group96(d), 1.0, 0.0).astype(F32)
    rows = jnp.where(group96(lane(SH, D, 1)) == lane(SH, D, 0), vterm[6:7, 0:D], 0.0)
    for j in range(1, 4):
        rows = rows + jnp.where(group96(lane(SH, D, 1)) + 8 * j == lane(SH, D, 0), vterm[6:7, D * j : D * j + D], 0.0)
    last = wide_dot(rows, place)
    out = jnp.zeros((SH, 256), F32)
    for k in range(7):
        shift = jnp.where(lane(128, 256, 1) == lane(128, 256, 0) + 24 * k, 1.0, 0.0).astype(F32)
        out = out + wide_dot(parts[SH * k : SH * k + SH, :] if k < 6 else last, shift)
    total[...] = out


SCRATCH = dict(
    G=((PHASES * SH * CH, D), BF16), w0=((SH * CH, D), BF16), w1=((SH * CH, D), BF16), cl2=((16 * CH, D), BF16),
    land12=((2 * LAND.n, D), BF16), act_=((4 * ROWS, D), BF16), gp_=((4 * ROWS, D), BF16), proj_=((3 * ROWS, D), BF16),
    hidden=((ROWS, D), F32), tmp=((ROWS, D), F32), chosen=((ROWS, D), BF16), picked=((ROWS, D), BF16), normed=((ROWS, D), BF16),
    feed=((ROWS, D), BF16), attended=((ROWS, D), BF16), normed_two=((ROWS, D), BF16), attn_grad=((ROWS, D), BF16),
    trans=((D, ROWS), BF16), lse=((CAP, 128), F32), lse_row=((2, 16, CAP), F32), gate=((ROWS, 1), F32), live=((ROWS, 1), F32),
    logit=((ROWS, 1), F32), tok=((2, LONG, D), BF16), ct=((2, LONG, D), BF16), vecs=((8, 4 * D), F32), vterm=((8, 4 * D), F32),
    obuf=((PHASES * CH, D), F32), vtotal=((2, SH, 256), F32), vout=((2, 5, SH, 256), F32), varr=((2, 5, SH, 256), F32),
)
SEMS = dict(lsem=(2,), osem=(11,), arecv=(PHASES, len(TYPES), 16), acrecv=(PHASES,), asend=(PHASES, 5), rrecv=(PHASES, len(LAND.sem)),
            rcrecv=(PHASES * 16,), rsend=(5,), vsend=(2, 5), vrecv=(2, 5))
INS = ("sel", "lens", "vrow", "qkv_w", "out_w", "up_w", "down_w", "tok_h", "ct_h")
OUTS = ("out_h", "ing_h", "small", "gqkv_h", "gout_h", "gup_h", "gdown_h")


def compute_order():
    out = []

    def tiles(*names):
        out.extend(("tile", name) for name in names)

    def grid(stem, *counts):
        tiles(*[stem + "".join(map(str, at)) for at in itertools.product(*[range(n) for n in counts])])

    grid("pick", 2)
    grid("norm", 6)
    out.append(("pd", 0))
    grid("relay0_", 4)
    grid("qkv", 3, 3)
    grid("attn", 2, 6)
    grid("out", 3)
    grid("norm2", 6)
    out.append(("pd", 1))
    grid("relay1_", 4)
    grid("up", 4, 3)
    grid("gdown", 4, 3)
    out.append(("csend", 2))
    tiles("bdown")
    out.append(("pd", 2))
    grid("gact", 4, 3)
    grid("down", 3)
    out.extend([("agfin",), ("free",)])
    grid("gate", 6)
    tiles("tn2")
    grid("gup", 2, 3)
    out.append(("csend", 1))
    grid("gn2", 3)
    grid("ln2b", 6)
    grid("gatt", 3)
    grid("attb", 2, 6)
    tiles("tn1")
    grid("gqk", 3)
    grid("gvo", 3)
    out.extend([("wfree",), ("csend", 0)])
    grid("gn1", 3)
    grid("ln1b", 6)
    tiles("vecpack")
    grid("ingrad", 2)
    out.extend(("vstep", 1, k) for k in range(5))
    return out


def catalogue():
    events = all_events()
    items = [("ag", e) for e in events] + [("own", p) for p in range(PHASES)]
    items += [("rs", e) for e in events] + [("rsown", p) for p in range(PHASES)]
    items += [("vstep", 0, k) for k in range(5)]
    return items + compute_order() + [("tile", "output0"), ("tile", "output1")]


def mega_kernel(names, order, *refs):
    fields = INS + OUTS + tuple(SCRATCH) + tuple(SEMS) + ("free_c", "free_all")
    R = types.SimpleNamespace(**dict(zip(fields, refs)))
    pc = Place()
    loads = [pltpu.make_async_copy(R.tok_h, R.tok, R.lsem.at[0]), pltpu.make_async_copy(R.ct_h, R.ct, R.lsem.at[1])]
    for cp in loads:
        cp.start()
    barrier = pltpu.get_barrier_semaphore()
    pc.signal(barrier, "CXYPWQ")
    for p in range(PHASES):
        if p == 0:
            v = jnp.concatenate([R.qkv_w[:, D * j : D * j + D].astype(F32) for j in range(3)] + [R.out_w[...].astype(F32)], axis=0).astype(BF16)
        elif p == 1:
            v = jnp.concatenate([R.up_w[:, D * j : D * j + D].astype(F32) for j in range(4)], axis=0).astype(BF16)
        else:
            v = R.down_w[...]
        R.G[pl.ds(pl.multiple_of((p * SH + pc.me) * CH, 16), CH), :] = v
    R.vtotal[0] = jnp.where(lane(SH, 256, 0) == pc.me, R.vrow[...], 0.0)
    pl.semaphore_wait(barrier, 5 + pc.mid)

    ag = Gather(pc, R.G, R.arecv, R.acrecv, R.asend)

    def land(p, off, n):
        if p:
            return R.land12.at[pl.ds((2 - p) * LAND.n + off, n), :]
        if off < 16 * CH:
            return R.w1.at[pl.ds(16 * CH + off, n), :]
        return R.act_.at[pl.ds(off, n), :]

    def cland(p, off, n):
        return {2: R.cl2, 1: R.act_, 0: R.w1}[p].at[pl.ds(off, n), :]

    rs = Reduce(pc, R.G, land, cland, R.rrecv, R.rcrecv, R.rsend, R.obuf)
    sums = [SmallSum(pc, R.vtotal.at[g], R.vout.at[g], R.varr.at[g], R.vsend.at[g], R.vrecv.at[g]) for g in range(2)]

    R.VEC = {name: (k, D) for name, k in ROW.items()}
    R.VEC["up_bias"] = (ROW["up_bias"], 4 * D)

    def vec(name, off=0, n=None):
        r, w = R.VEC[name]
        return R.vecs[r : r + 1, off : off + (n or w)]

    def view(ref, rows):
        return lambda j: ref.at[pl.ds(rows * j, rows), :]

    R.vec = vec
    R.act, R.gp, R.proj, R.dproj = view(R.act_, ROWS), view(R.gp_, ROWS), view(R.proj_, ROWS), view(R.gp_, ROWS)
    R.W0, R.W1 = view(R.w0, D), view(R.w1, D)
    R.W2 = lambda j: R.G.at[pl.ds(2 * SH * CH + D * j, D), :]
    R.part = lambda p: R.G.at[pl.ds(BASE[p], SH * CH), :]
    R.change = R.datt = R.feed
    stores = []

    def store(src, dst):
        cp = pltpu.make_async_copy(src, dst, R.osem.at[len(stores)])
        cp.start()
        stores.append(cp)

    def output(i, v):
        R.tok[i] = v
        if i == 1:
            store(R.tok, R.out_h)

    def input_grad(i, v):
        R.ct[i] = v
        if i == 1:
            store(R.ct, R.ing_h)

    R.output, R.input_grad = output, input_grad
    tiles = {name: f for name, _, _, f in fwd_tiles(R) + bwd_tiles(R)}
    program = [names[k] for k in order]
    offsets = {}
    for it in program:
        if it[0] in ("rs", "rsown"):
            p, o = (it[1][0], it[1][2:5]) if it[0] == "rs" else (it[1], (0, 0, 0))
            if o not in offsets.setdefault(p, []):
                offsets[p].append(o)
    waited = set()
    for it in program:
        kind = it[0]
        if kind == "ag":
            ag.step(it[1])
        elif kind == "own":
            ag.own(it[1])
        elif kind == "pd":
            ag.phase_done(it[1])
        elif kind == "rs":
            rs.step(it[1])
        elif kind == "rsown":
            p = it[1]
            rs.own(p)
            for j in range(4 if p < 2 else 1):
                src = R.obuf.at[pl.ds(p * CH + 24 * j, 24), :]
                if p == 2:
                    store(R.obuf.at[pl.ds(p * CH, CH), :], R.gdown_h)
                elif p == 1:
                    store(src, R.gup_h.at[:, pl.ds(D * j, D)])
                elif j < 3:
                    store(src, R.gqkv_h.at[:, pl.ds(D * j, D)])
                else:
                    store(src, R.gout_h)
        elif kind == "vstep":
            sums[it[1]].step(it[2])
        elif kind == "csend":
            p = it[1]
            if p == 1:
                pl.semaphore_wait(R.free_c, 1)
            if p == 0:
                pl.semaphore_wait(R.free_all, 4 + pc.mid)
            rs.csend(p, offsets[p])
        elif kind == "tile":
            name = it[1]
            if name == "pick0":
                for cp in loads:
                    cp.wait()
            if name == "norm0":
                sums[0].step(5)
                unpack_small(R.vtotal.at[0], R.vecs)
            if name == "vecpack":
                pack_small(R.vterm, R.vtotal.at[1])
            else:
                if name == "gdown00":
                    ag.traffic[1].wait()
                if name == "gup00":
                    ag.traffic[0].wait()
                if name == "gqk0":
                    ag.traffic[2].wait()
                tiles[name]()
            if name == "down2":
                pc.signal(R.free_c, "C")
            if name == "gn22":
                pc.signal(R.free_all, "CXYPQ")
    sums[1].step(5)
    R.small[...] = R.vtotal[1, pl.ds(pc.me, 1), :]
    rs.traffic.wait()
    for s in sums:
        s.finish()
    for cp in stores:
        cp.wait()


def mega(names, order, *args):
    S = jax.ShapeDtypeStruct
    V, H = pl.BlockSpec(memory_space=pltpu.VMEM), pl.BlockSpec(memory_space=pl.ANY)
    outs = [S((2, LONG, D), BF16), S((2, LONG, D), BF16), S((1, 256), F32), S((24, 3 * D), F32), S((24, D), F32), S((24, 4 * D), F32), S((96, D), F32)]
    return pl.pallas_call(
        functools.partial(mega_kernel, names, order), out_shape=outs, in_specs=[V] * 7 + [H, H],
        out_specs=[H, H, V, H, H, H, H],
        scratch_shapes=[pltpu.VMEM(*s) for s in SCRATCH.values()] + [pltpu.SemaphoreType.DMA(s) for s in SEMS.values()] + [pltpu.SemaphoreType.REGULAR] * 2,
        compiler_params=pltpu.CompilerParams(collective_id=0, has_side_effects=True, vmem_limit_bytes=VMEM_LIMIT),
        cost_estimate=pl.CostEstimate(flops=26_000_000_000, bytes_accessed=12_000_000, transcendentals=6_000_000),
    )(*args)


ORDER = (
    180, 0, 1, 15, 30, 31, 52, 48, 46, 366, 16, 45, 4, 32, 18, 26, 371, 33, 367, 368, 50, 3, 372, 37,
    34, 17, 20, 35, 369, 7, 2, 36, 23, 181, 27, 49, 5, 370, 21, 42, 40, 6, 47, 19, 373, 22, 51, 60,
    75, 39, 13, 11, 374, 375, 8, 24, 56, 91, 43, 9, 97, 376, 112, 41, 58, 106, 377, 38, 44, 29, 63, 55,
    105, 90, 14, 82, 57, 10, 378, 12, 54, 67, 25, 93, 53, 62, 59, 28, 79, 64, 69, 76, 61, 379, 380, 381,
    382, 383, 108, 384, 385, 386, 68, 182, 387, 388, 389, 390, 391, 392, 393, 394, 109, 395, 396, 110, 65, 92, 107, 88,
    99, 397, 101, 66, 120, 78, 398, 116, 135, 77, 95, 113, 399, 150, 73, 80, 400, 86, 127, 96, 111, 165, 401, 117,
    172, 402, 94, 74, 121, 71, 98, 81, 403, 151, 146, 114, 102, 404, 72, 138, 118, 83, 166, 115, 104, 153, 405, 103,
    406, 407, 152, 84, 87, 119, 408, 154, 169, 137, 100, 89, 129, 70, 85, 142, 409, 410, 167, 124, 411, 412, 122, 413,
    123, 414, 415, 416, 136, 417, 139, 155, 418, 125, 156, 176, 419, 420, 130, 421, 422, 171, 423, 163, 424, 177, 140, 425,
    426, 128, 141, 159, 133, 143, 157, 161, 427, 126, 178, 173, 428, 168, 429, 131, 132, 147, 430, 431, 170, 432, 162, 433,
    148, 144, 158, 434, 435, 436, 149, 145, 437, 438, 439, 440, 164, 179, 175, 174, 160, 134, 441, 442, 443, 444, 445, 446,
    447, 448, 449, 450, 451, 452, 453, 454, 455, 456, 457, 458, 316, 459, 460, 461, 462, 463, 317, 341, 464, 345, 465, 466,
    467, 468, 469, 357, 470, 471, 332, 472, 473, 474, 361, 475, 476, 338, 358, 351, 315, 309, 311, 346, 477, 478, 347, 250,
    266, 302, 362, 479, 269, 257, 480, 481, 328, 482, 483, 265, 330, 344, 484, 352, 297, 270, 298, 331, 485, 272, 294, 527,
    528, 486, 356, 301, 487, 327, 354, 488, 489, 353, 490, 249, 491, 291, 300, 313, 492, 493, 264, 314, 494, 293, 268, 299,
    253, 283, 252, 322, 495, 324, 496, 285, 497, 305, 326, 254, 287, 323, 256, 281, 498, 271, 296, 499, 359, 306, 343, 360,
    349, 255, 500, 286, 263, 267, 320, 501, 502, 245, 503, 339, 334, 247, 504, 307, 259, 505, 260, 350, 336, 506, 342, 507,
    312, 261, 508, 248, 509, 282, 325, 276, 295, 290, 277, 308, 262, 289, 284, 280, 310, 510, 279, 212, 210, 242, 292, 240,
    337, 340, 208, 355, 321, 319, 237, 241, 511, 227, 238, 329, 226, 234, 192, 244, 197, 195, 335, 251, 303, 512, 225, 204,
    220, 243, 348, 222, 193, 211, 194, 224, 236, 275, 333, 196, 513, 231, 514, 515, 191, 219, 233, 278, 304, 273, 230, 318,
    516, 517, 189, 221, 518, 223, 239, 235, 258, 200, 206, 218, 232, 207, 203, 519, 274, 365, 215, 217, 288, 209, 202, 188,
    520, 521, 246, 185, 187, 522, 229, 213, 228, 523, 214, 199, 216, 186, 205, 201, 190, 198, 183, 184, 364, 524, 525, 526,
    363,
)

VMEM_LIMIT = 63 << 20


def on_device_fast(tokens, lengths, selected, cotangent, attn_gain, attn_shift, mlp_gain, mlp_shift, router_weight,
                   qkv_weight, out_weight, up_weight, up_bias, down_weight, down_bias):
    small = jnp.concatenate([attn_gain, attn_shift, mlp_gain, mlp_shift, router_weight, down_bias, up_bias, jnp.zeros((16,), BF16)])
    output, token_grad, owned, gqkv, gout, gup, gdown = mega(
        catalogue(), ORDER, selected[:, 0], lengths, small.astype(F32)[None], qkv_weight, out_weight, up_weight, down_weight,
        tokens[:, 0], cotangent[:, 0])
    owned = owned[0]
    t = [owned[24 * k : 24 * k + 24] for k in range(6)]
    return (output[:, None], token_grad[:, None], t[0], t[1], t[2], t[3], t[4], gqkv, gout, gup, owned[144:240], gdown, t[5])


HEADS = 12
HEAD_DIM = 64
MICRO = 2


epsilon = 1e-06


def normalize(inputs, norm_gain, norm_shift):
    centered = inputs - jnp.mean(inputs, axis=-1, keepdims=True)
    variance = jnp.mean(centered * centered, axis=-1, keepdims=True)
    return centered * lax.rsqrt(variance + epsilon) * norm_gain + norm_shift


def forward_pass(tokens, lengths, selected, weights):
    (
        attn_gain,
        attn_shift,
        mlp_gain,
        mlp_shift,
        router_weight,
        qkv_weight,
        out_weight,
        up_weight,
        up_bias,
        down_weight,
        down_bias,
    ) = weights
    group_size, capacity = selected.shape
    counts = lengths // 2
    live_mask = (jnp.arange(capacity)[None, :] < counts[:, None]).astype(jnp.float32)
    chosen = jnp.take_along_axis(tokens, selected[:, :, None], axis=1)
    chosen_wide = chosen.astype(jnp.float32)
    logits = jnp.einsum("bcd,d->bc", chosen, router_weight, preferred_element_type=jnp.float32)
    router_gate = jax.nn.sigmoid(logits)
    normed = normalize(
        chosen_wide, attn_gain.astype(jnp.float32), attn_shift.astype(jnp.float32)
    ).astype(jnp.bfloat16)
    projected = jnp.einsum(
        "bcd,de->bce", normed, qkv_weight, preferred_element_type=jnp.float32
    ).astype(jnp.bfloat16)
    projected = projected.reshape(group_size, capacity, 3, HEADS, HEAD_DIM)
    queries = projected[:, :, 0]
    key_rows = projected[:, :, 1]
    value_rows = projected[:, :, 2]
    score_scale = HEAD_DIM ** (-0.5)
    scores = (
        jnp.einsum("bqhe,bkhe->bhqk", queries, key_rows, preferred_element_type=jnp.float32)
        * score_scale
    )
    scores = jnp.where(live_mask[:, None, None, :] > 0, scores, -1000000000.0)
    row_max = jnp.max(scores, axis=-1, keepdims=True)
    exponent = jnp.exp(scores - row_max)
    row_total = jnp.sum(exponent, axis=-1, keepdims=True)
    attention = (exponent / row_total).astype(jnp.bfloat16)
    log_total = row_max + jnp.log(row_total)
    attended = jnp.einsum(
        "bhqk,bkhe->bqhe", attention, value_rows, preferred_element_type=jnp.float32
    ).astype(jnp.bfloat16)
    attended = attended.reshape(group_size, capacity, HEADS * HEAD_DIM)
    attn_out = jnp.einsum("bce,ed->bcd", attended, out_weight, preferred_element_type=jnp.float32)
    hidden = chosen_wide + attn_out
    normed_two = normalize(
        hidden, mlp_gain.astype(jnp.float32), mlp_shift.astype(jnp.float32)
    ).astype(jnp.bfloat16)
    upward = jnp.einsum(
        "bcd,df->bcf", normed_two, up_weight, preferred_element_type=jnp.float32
    ) + up_bias.astype(jnp.float32)
    active = jax.nn.gelu(upward).astype(jnp.bfloat16)
    feed_out = jnp.einsum(
        "bcf,fd->bcd", active, down_weight, preferred_element_type=jnp.float32
    ) + down_bias.astype(jnp.float32)
    change = (attn_out + feed_out) * (router_gate * live_mask)[:, :, None]
    image_rows = jnp.arange(group_size)[:, None]
    output = tokens.astype(jnp.float32).at[image_rows, selected].add(change).astype(jnp.bfloat16)
    kept_values = (
        chosen_wide,
        live_mask,
        router_gate,
        normed,
        projected,
        log_total,
        attended,
        attn_out,
        hidden,
        normed_two,
        upward,
        active,
        feed_out,
    )
    return (output, kept_values)


def backward_pass(cotangent, selected, weights, kept_values):
    (
        attn_gain,
        attn_shift,
        mlp_gain,
        mlp_shift,
        router_weight,
        qkv_weight,
        out_weight,
        up_weight,
        up_bias,
        down_weight,
        down_bias,
    ) = weights
    (
        chosen_wide,
        live_mask,
        router_gate,
        normed,
        projected,
        log_total,
        attended,
        attn_out,
        hidden,
        normed_two,
        upward,
        active,
        feed_out,
    ) = kept_values
    group_size, capacity = selected.shape
    out_grad = cotangent.astype(jnp.float32)
    picked = jnp.take_along_axis(out_grad, selected[:, :, None], axis=1) * live_mask[:, :, None]
    gate_grad = jnp.sum(picked * (attn_out + feed_out), axis=-1)
    logit_grad = gate_grad * router_gate * (1.0 - router_gate)
    change_grad = picked * router_gate[:, :, None]
    feed_grad = change_grad.astype(jnp.bfloat16)
    down_bias_grad = jnp.sum(feed_grad.astype(jnp.float32), axis=(0, 1))
    down_weight_grad = jnp.einsum(
        "bcf,bcd->fd", active, feed_grad, preferred_element_type=jnp.float32
    )
    active_grad = jnp.einsum(
        "bcd,fd->bcf", feed_grad, down_weight, preferred_element_type=jnp.float32
    )
    primal_out, gelu_back = jax.vjp(jax.nn.gelu, upward)
    upward_grad = gelu_back(active_grad)[0].astype(jnp.bfloat16)
    up_bias_grad = jnp.sum(upward_grad.astype(jnp.float32), axis=(0, 1))
    up_weight_grad = jnp.einsum(
        "bcd,bcf->df", normed_two, upward_grad, preferred_element_type=jnp.float32
    )
    normed_two_grad = jnp.einsum(
        "bcf,df->bcd", upward_grad, up_weight, preferred_element_type=jnp.float32
    )
    primal_two, norm_back = jax.vjp(
        normalize, hidden, mlp_gain.astype(jnp.float32), mlp_shift.astype(jnp.float32)
    )
    hidden_grad, mlp_gain_grad, mlp_shift_grad = norm_back(normed_two_grad)
    attn_grad = (change_grad + hidden_grad).astype(jnp.bfloat16)
    out_weight_grad = jnp.einsum(
        "bce,bcd->ed", attended, attn_grad, preferred_element_type=jnp.float32
    )
    attended_grad = jnp.einsum(
        "bcd,ed->bce", attn_grad, out_weight, preferred_element_type=jnp.float32
    ).astype(jnp.bfloat16)
    attended_grad = attended_grad.reshape(group_size, capacity, HEADS, HEAD_DIM)
    queries = projected[:, :, 0]
    key_rows = projected[:, :, 1]
    value_rows = projected[:, :, 2]
    score_scale = HEAD_DIM ** (-0.5)
    key_live = live_mask[:, None, None, :] > 0
    scores = (
        jnp.einsum("bqhe,bkhe->bhqk", queries, key_rows, preferred_element_type=jnp.float32)
        * score_scale
    )
    scores = jnp.where(key_live, scores, -1000000000.0)
    prob_wide = jnp.exp(scores - log_total)
    prob_low = prob_wide.astype(jnp.bfloat16)
    value_grad = jnp.einsum(
        "bhqk,bqhe->bkhe", prob_low, attended_grad, preferred_element_type=jnp.float32
    )
    prob_grad = jnp.einsum(
        "bqhe,bkhe->bhqk", attended_grad, value_rows, preferred_element_type=jnp.float32
    )
    score_grad = prob_wide * (prob_grad - jnp.sum(prob_wide * prob_grad, axis=-1, keepdims=True))
    score_grad = jnp.where(key_live, score_grad.astype(jnp.bfloat16), 0.0) * score_scale
    query_grad = jnp.einsum(
        "bhqk,bkhe->bqhe", score_grad, key_rows, preferred_element_type=jnp.float32
    )
    key_grad = jnp.einsum(
        "bhqk,bqhe->bkhe", score_grad, queries, preferred_element_type=jnp.float32
    )
    projected_grad = jnp.stack([query_grad, key_grad, value_grad], axis=2).astype(jnp.bfloat16)
    projected_grad = projected_grad.reshape(group_size, capacity, 3 * HEADS * HEAD_DIM)
    qkv_weight_grad = jnp.einsum(
        "bcd,bce->de", normed, projected_grad, preferred_element_type=jnp.float32
    )
    normed_grad = jnp.einsum(
        "bce,de->bcd", projected_grad, qkv_weight, preferred_element_type=jnp.float32
    )
    primal_one, first_back = jax.vjp(
        normalize, chosen_wide, attn_gain.astype(jnp.float32), attn_shift.astype(jnp.float32)
    )
    chosen_grad, attn_gain_grad, attn_shift_grad = first_back(normed_grad)
    chosen_grad = (
        chosen_grad + hidden_grad + logit_grad[:, :, None] * router_weight.astype(jnp.float32)
    )
    router_weight_grad = jnp.einsum(
        "bc,bcd->d", logit_grad, chosen_wide, precision=lax.Precision.HIGHEST
    )
    image_rows = jnp.arange(group_size)[:, None]
    token_grad = out_grad.at[image_rows, selected].add(chosen_grad).astype(jnp.bfloat16)
    grad_terms = (
        attn_gain_grad,
        attn_shift_grad,
        mlp_gain_grad,
        mlp_shift_grad,
        router_weight_grad,
        qkv_weight_grad,
        out_weight_grad,
        up_weight_grad,
        up_bias_grad,
        down_weight_grad,
        down_bias_grad,
    )
    return (token_grad, grad_terms)


def on_device(
    tokens,
    lengths,
    selected,
    cotangent,
    attn_gain,
    attn_shift,
    mlp_gain,
    mlp_shift,
    router_weight,
    qkv_weight,
    out_weight,
    up_weight,
    up_bias,
    down_weight,
    down_bias,
):
    outputs = []
    token_grads = []
    totals = None
    for micro_step in range(MICRO):
        forward_weights = (
            lax.all_gather(attn_gain, ("dp", "shard"), axis=0, tiled=True),
            lax.all_gather(attn_shift, ("dp", "shard"), axis=0, tiled=True),
            lax.all_gather(mlp_gain, ("dp", "shard"), axis=0, tiled=True),
            lax.all_gather(mlp_shift, ("dp", "shard"), axis=0, tiled=True),
            lax.all_gather(router_weight, ("dp", "shard"), axis=0, tiled=True),
            lax.all_gather(qkv_weight, ("dp", "shard"), axis=0, tiled=True),
            lax.all_gather(out_weight, ("dp", "shard"), axis=0, tiled=True),
            lax.all_gather(up_weight, ("dp", "shard"), axis=0, tiled=True),
            lax.all_gather(up_bias, ("dp", "shard"), axis=0, tiled=True),
            lax.all_gather(down_weight, ("dp", "shard"), axis=0, tiled=True),
            lax.all_gather(down_bias, ("dp", "shard"), axis=0, tiled=True),
        )
        output, kept_values = forward_pass(
            tokens[micro_step], lengths[micro_step], selected[micro_step], forward_weights
        )
        backward_weights = (
            lax.all_gather(attn_gain, ("dp", "shard"), axis=0, tiled=True),
            lax.all_gather(attn_shift, ("dp", "shard"), axis=0, tiled=True),
            lax.all_gather(mlp_gain, ("dp", "shard"), axis=0, tiled=True),
            lax.all_gather(mlp_shift, ("dp", "shard"), axis=0, tiled=True),
            lax.all_gather(router_weight, ("dp", "shard"), axis=0, tiled=True),
            lax.all_gather(qkv_weight, ("dp", "shard"), axis=0, tiled=True),
            lax.all_gather(out_weight, ("dp", "shard"), axis=0, tiled=True),
            lax.all_gather(up_weight, ("dp", "shard"), axis=0, tiled=True),
            lax.all_gather(up_bias, ("dp", "shard"), axis=0, tiled=True),
            lax.all_gather(down_weight, ("dp", "shard"), axis=0, tiled=True),
            lax.all_gather(down_bias, ("dp", "shard"), axis=0, tiled=True),
        )
        token_grad, grad_terms = backward_pass(
            cotangent[micro_step], selected[micro_step], backward_weights, kept_values
        )
        grad_terms = (
            lax.psum_scatter(grad_terms[0], ("dp", "shard"), scatter_dimension=0, tiled=True),
            lax.psum_scatter(grad_terms[1], ("dp", "shard"), scatter_dimension=0, tiled=True),
            lax.psum_scatter(grad_terms[2], ("dp", "shard"), scatter_dimension=0, tiled=True),
            lax.psum_scatter(grad_terms[3], ("dp", "shard"), scatter_dimension=0, tiled=True),
            lax.psum_scatter(grad_terms[4], ("dp", "shard"), scatter_dimension=0, tiled=True),
            lax.psum_scatter(grad_terms[5], ("dp", "shard"), scatter_dimension=0, tiled=True),
            lax.psum_scatter(grad_terms[6], ("dp", "shard"), scatter_dimension=0, tiled=True),
            lax.psum_scatter(grad_terms[7], ("dp", "shard"), scatter_dimension=0, tiled=True),
            lax.psum_scatter(grad_terms[8], ("dp", "shard"), scatter_dimension=0, tiled=True),
            lax.psum_scatter(grad_terms[9], ("dp", "shard"), scatter_dimension=0, tiled=True),
            lax.psum_scatter(grad_terms[10], ("dp", "shard"), scatter_dimension=0, tiled=True),
        )
        totals = grad_terms if totals is None else jax.tree.map(jnp.add, totals, grad_terms)
        outputs.append(output)
        token_grads.append(token_grad)
    return (
        jnp.stack(outputs),
        jnp.stack(token_grads),
        totals[0],
        totals[1],
        totals[2],
        totals[3],
        totals[4],
        totals[5],
        totals[6],
        totals[7],
        totals[8],
        totals[9],
        totals[10],
    )


def solution(mesh):
    fits = dict(mesh.shape) == {"dp": 16, "shard": 2}
    return jax.shard_map(
        on_device_fast if fits else on_device,
        mesh=mesh,
        in_specs=(
            P(None, ("dp", "shard"), None, None),
            P(None, ("dp", "shard")),
            P(None, ("dp", "shard"), None),
            P(None, ("dp", "shard"), None, None),
            P(("dp", "shard")),
            P(("dp", "shard")),
            P(("dp", "shard")),
            P(("dp", "shard")),
            P(("dp", "shard")),
            P(("dp", "shard"), None),
            P(("dp", "shard"), None),
            P(("dp", "shard"), None),
            P(("dp", "shard")),
            P(("dp", "shard"), None),
            P(("dp", "shard")),
        ),
        out_specs=(
            P(None, ("dp", "shard"), None, None),
            P(None, ("dp", "shard"), None, None),
            P(("dp", "shard")),
            P(("dp", "shard")),
            P(("dp", "shard")),
            P(("dp", "shard")),
            P(("dp", "shard")),
            P(("dp", "shard"), None),
            P(("dp", "shard"), None),
            P(("dp", "shard"), None),
            P(("dp", "shard")),
            P(("dp", "shard"), None),
            P(("dp", "shard")),
        ),
        check_vma=False,
    )
```

```python
import functools
import itertools
import math
import types

import jax
import jax.numpy as jnp
from jax import lax
from jax.experimental import pallas as pl
from jax.experimental.pallas import tpu as pltpu
from jax.sharding import PartitionSpec as P

F32, BF16 = jnp.float32, jnp.bfloat16
D, ROWS, CAP, LONG = 768, 576, 288, 577
SH, CH = 32, 96
NN = (((1,), (0,)), ((), ()))
NT = (((1,), (1,)), ((), ()))
TN = (((0,), (0,)), ((), ()))
def dot(a, b, dims=NN):
    return lax.dot_general(a, b, dims, preferred_element_type=F32)
def ln(rows):
    centered = rows - jnp.mean(rows, axis=-1, keepdims=True)
    rstd = lax.rsqrt(jnp.mean(centered * centered, axis=-1, keepdims=True) + 1e-6)
    return centered * rstd, rstd
def spread(R, i):
    place = lax.broadcasted_iota(jnp.int32, (2 * LONG, CAP), 0)
    return jnp.where(place == 2 * R.sel[i] + i, 1.0, 0.0).astype(BF16)
def choose(R, i):
    place = lax.broadcasted_iota(jnp.int32, (CAP, 2 * LONG), 1)
    column = jnp.transpose(jnp.broadcast_to((2 * R.sel[i] + i).astype(F32), (8, CAP)))[:, 0:1].astype(jnp.int32)
    return jnp.where(place == column, 1.0, 0.0).astype(BF16)
def both(ref, cs=slice(None)):
    return ref[:, :, cs].reshape(2 * LONG, -1)
def live_rows(lens, i):
    slot = lax.broadcasted_iota(jnp.int32, (CAP, 1), 0)
    return (slot < lax.shift_right_logical(lens[:, i : i + 1], 1)).astype(F32)
def live_cols(lens, i):
    slot = lax.broadcasted_iota(jnp.int32, (1, CAP), 1)
    return slot < lax.shift_right_logical(lens[:, i : i + 1], 1)
def relayout(G, W, p, lo, hi, cs=slice(None)):
    for k in range(lo, hi):
        two = [G[(p * SH + 2 * k + u) * CH : (p * SH + 2 * k + u + 1) * CH, cs].astype(F32) for u in range(2)]
        for j in range(4):
            W[D * j + 48 * k : D * j + 48 * k + 48, cs] = jnp.concatenate([t[24 * j : 24 * j + 24, :] for t in two], axis=0).astype(BF16)
def fwd_tiles(R):
    T = []
    def add(name, cost, dep):
        def deco(f): T.append((name, cost, dep, f)); return f
        return deco
    for i in range(2):
        sl = slice(CAP * i, CAP * i + CAP)
        @add(f"pick{i}", 1.0, "tok")
        def _(i=i, sl=sl):
            oh = choose(R, i)
            R.chosen[sl, :] = dot(oh, both(R.tok)).astype(BF16)
            R.live[sl, :] = live_rows(R.lens, i)
            R.picked[sl, :] = (dot(oh, both(R.ct)) * R.live[sl, :]).astype(BF16)
    B = 96
    for b in range(ROWS // B):
        sl = slice(B * b, B * b + B)
        @add(f"norm{b}", 0.4, "vec")
        def _(sl=sl):
            ch = R.chosen[sl, :].astype(F32)
            xh, _ = ln(ch)
            R.normed[sl, :] = (xh * R.vec("attn_gain") + R.vec("attn_shift")).astype(BF16)
            logit = jnp.sum(ch * R.vec("router_weight"), axis=-1, keepdims=True)
            gate = 1.0 / (1.0 + jnp.exp(-logit))
            R.gate[sl, :] = gate
            feed = (gate * R.picked[sl, :].astype(F32)).astype(BF16)
            R.feed[sl, :] = feed
    for g in range(3):
        @add(f"relay0_{g}", 0.4, 0)
        def _(g=g): relayout(R.G, R.w0, 0, 0, 16, slice(256 * g, 256 * g + 256))
    for j in range(3):
        for n in range(3):
            @add(f"qkv{j}{n}", 0.45, 0)
            def _(j=j, n=n):
                cs = slice(256 * n, 256 * n + 256)
                R.proj(j)[:, cs] = dot(R.normed[...], R.W0(j)[:, cs]).astype(BF16)
    for i in range(2):
        sl = slice(CAP * i, CAP * i + CAP)
        for h in range(6):
            @add(f"attn{i}{h}", 1.0, 0)
            def _(i=i, h=h, sl=sl):
                cs = slice(128 * h, 128 * h + 128)
                q, k, v = R.proj(0)[sl, cs], R.proj(1)[sl, cs], R.proj(2)[sl, cs]
                low = lax.broadcasted_iota(jnp.int32, (CAP, 128), 1) < 64
                lane = lax.broadcasted_iota(jnp.int32, (CAP, 128), 1)
                live = live_cols(R.lens, i)
                zero, ones = jnp.zeros_like(q), jnp.ones_like(q)
                q = q * 0.125
                outs = []
                lse = R.lse[i] if h else jnp.zeros((CAP, 128), F32)
                for u in range(2):
                    qm, vm = (jnp.where(low, q, zero), jnp.where(low, v, ones)) if u == 0 else (jnp.where(low, zero, q), jnp.where(low, ones, v))
                    s = jnp.where(live, dot(qm, k, NT), -1e9)
                    m = jnp.max(s, axis=-1, keepdims=True)
                    o = dot(jnp.exp(s - m).astype(BF16), vm)
                    tot = o[:, 64:65] if u == 0 else o[:, 0:1]
                    outs.append(o * (1.0 / tot))
                    lse = jnp.where(lane == 2 * h + u, m + jnp.log(tot), lse)
                R.lse[i] = lse
                R.attended[sl, cs] = jnp.where(low, outs[0], outs[1]).astype(BF16)
                if h == 5:
                    R.lse_row[i] = jnp.transpose(lse)[:16, :]
    for n in range(3):
        @add(f"out{n}", 0.45, 0)
        def _(n=n):
            cs = slice(256 * n, 256 * n + 256)
            R.hidden[:, cs] = R.chosen[:, cs].astype(F32) + dot(R.attended[...], R.W0(3)[:, cs])
    for b in range(ROWS // B):
        sl = slice(B * b, B * b + B)
        @add(f"norm2{b}", 0.3, 0)
        def _(sl=sl):
            xh, _ = ln(R.hidden[sl, :])
            R.normed_two[sl, :] = (xh * R.vec("mlp_gain") + R.vec("mlp_shift")).astype(BF16)
    for g in range(4):
        @add(f"relay1_{g}", 0.4, 1)
        def _(g=g): relayout(R.G, R.w1, 1, 4 * g, 4 * g + 4)
    c0 = math.sqrt(2.0 / math.pi)
    for j in range(4):
        for n in range(3):
            @add(f"up{j}{n}", 1.2, 1)
            def _(j=j, n=n):
                cs = slice(256 * n, 256 * n + 256)
                u = dot(R.normed_two[...], R.W1(j)[:, cs]) + R.vec("up_bias", D * j + 256 * n, 256)
                uu = u * u
                half = 0.5 * jnp.tanh(u * (c0 + (c0 * 0.044715) * uu)) + 0.5
                a = u * half
                R.act(j)[:, cs] = a.astype(BF16)
                R.gp(j)[:, cs] = (half + a * (1.0 - half) * (2 * c0 + (6 * c0 * 0.044715) * uu)).astype(BF16)
    for n in range(3):
        @add(f"down{n}", 1.6, 2)
        def _(n=n):
            cs = slice(256 * n, 256 * n + 256)
            acc = R.vec("down_bias", 256 * n, 256) + dot(R.act(0)[...], R.W2(0)[:, cs])
            for j in range(1, 4): acc = acc + dot(R.act(j)[...], R.W2(j)[:, cs])
            R.delta[:, cs] = (acc + (R.hidden[:, cs] - R.chosen[:, cs].astype(F32))).astype(BF16)
    for b in range(ROWS // B):
        sl = slice(B * b, B * b + B)
        @add(f"gate{b}", 0.3, 2)
        def _(sl=sl):
            d = R.delta[sl, :].astype(F32)
            gate = R.gate[sl, :]
            R.logit[sl, :] = jnp.sum(R.picked[sl, :].astype(F32) * d, axis=-1, keepdims=True) * gate * (1.0 - gate)
            R.change[sl, :] = (d * (gate * R.live[sl, :])).astype(BF16)
    for n in range(2):
        @add(f"output{n}", 1.0, 2)
        def _(n=n):
            cs = slice(384 * n, 384 * n + 384)
            total = both(R.tok, cs).astype(F32)
            for i in range(2): total = total + dot(spread(R, i), R.change[CAP * i : CAP * i + CAP, cs])
            R.output(n, cs, total.astype(BF16).reshape(LONG, 2, 384))
    return T


def bwd_tiles(R):
    T = []
    def add(name, cost, dep=None):
        def deco(f): T.append((name, cost, dep, f)); return f
        return deco
    def grow(name, v, first, off=0):
        r, w = R.VEC[name]
        n = v.shape[1]
        if first: R.vterm[r : r + 1, off : off + n] = v
        else: R.vterm[r : r + 1, off : off + n] = R.vterm[r : r + 1, off : off + n] + v
    def colsum(v): return jnp.sum(v, axis=0, keepdims=True)
    def put_pair(p, half, cs, one, two):
        for s in range(SH):
            R.part(p)[s * CH + 48 * half : s * CH + 48 * half + 48, cs] = jnp.concatenate(
                [one[24 * s : 24 * s + 24, :], two[24 * s : 24 * s + 24, :]], axis=0).astype(BF16)
    B = 96
    for j in range(4):
        for n in range(3):
            @add(f"gdown{j}{n}", 0.55)
            def _(j=j, n=n):
                cs = slice(256 * n, 256 * n + 256)
                R.part(2)[D * j + 256 * n : D * j + 256 * n + 256, :] = dot(R.act(j)[:, cs], R.feed[...], TN).astype(BF16)
    @add("bdown", 0.2)
    def _():
        grow("down_bias", colsum(R.feed[...].astype(F32)), True)
    for j in range(4):
        for n in range(3):
            @add(f"gact{j}{n}", 0.6)
            def _(j=j, n=n):
                cs = slice(256 * n, 256 * n + 256)
                g = (dot(R.feed[...], R.W2(j)[cs, :], NT) * R.gp(j)[:, cs].astype(F32)).astype(BF16)
                R.gp(j)[:, cs] = g
                grow("up_bias", colsum(g.astype(F32)), True, D * j + 256 * n)
    @add("tn2", 0.6)
    def _(): R.trans[...] = jnp.transpose(R.normed_two[...])
    for h in range(2):
        for n in range(3):
            @add(f"gup{h}{n}", 1.2)
            def _(h=h, n=n):
                cs = slice(256 * n, 256 * n + 256)
                put_pair(1, h, cs, dot(R.trans[...], R.gp(2 * h)[:, cs]), dot(R.trans[...], R.gp(2 * h + 1)[:, cs]))
    for n in range(3):
        @add(f"gn2{n}", 1.6)
        def _(n=n):
            cs = slice(256 * n, 256 * n + 256)
            acc = dot(R.gp(0)[...], R.W1(0)[cs, :], NT)
            for j in range(1, 4): acc = acc + dot(R.gp(j)[...], R.W1(j)[cs, :], NT)
            R.tmp[:, cs] = acc
    for b in range(ROWS // B):
        sl = slice(B * b, B * b + B)
        @add(f"ln2b{b}", 0.5)
        def _(sl=sl, b=b):
            g = R.tmp[sl, :]
            xh, r = ln(R.hidden[sl, :])
            grow("mlp_gain", colsum(g * xh), b == 0)
            grow("mlp_shift", colsum(g), b == 0)
            e = g * R.vec("mlp_gain")
            hg = r * (e - jnp.mean(e, axis=-1, keepdims=True) - xh * jnp.mean(e * xh, axis=-1, keepdims=True))
            R.hidden[sl, :] = hg
            R.attn_grad[sl, :] = (R.gate[sl, :] * R.picked[sl, :].astype(F32) + hg).astype(BF16)
    for n in range(3):
        @add(f"gatt{n}", 0.45)
        def _(n=n):
            cs = slice(256 * n, 256 * n + 256)
            R.datt[:, cs] = dot(R.attn_grad[...], R.W0(3)[cs, :], NT).astype(BF16)
    for i in range(2):
        sl = slice(CAP * i, CAP * i + CAP)
        for h in range(6):
            @add(f"attb{i}{h}", 1.6)
            def _(i=i, h=h, sl=sl):
                cs = slice(128 * h, 128 * h + 128)
                q, k, v, do = R.proj(0)[sl, cs], R.proj(1)[sl, cs], R.proj(2)[sl, cs], R.datt[sl, cs]
                low = lax.broadcasted_iota(jnp.int32, (CAP, 128), 1) < 64
                live = live_rows(R.lens, i) > 0
                zero = jnp.zeros_like(q)
                q = q * 0.125
                def own(a, u): return jnp.where(low, a, zero) if u == 0 else jnp.where(low, zero, a)
                dq = dk = dv = None
                for u in range(2):
                    qm, km, dm = own(q, u), own(k, u), own(do, u)
                    s = dot(k, qm, NT) - R.lse_row[i, 2 * h + u : 2 * h + u + 1, :]
                    pt = jnp.where(live, jnp.exp(s), 0.0)
                    dp = dot(v, dm, NT)
                    ds = (pt * (dp - colsum(pt * dp))).astype(BF16)
                    a, b, c = dot(pt.astype(BF16), dm), dot(ds, qm), dot(ds, km, TN)
                    dv, dk, dq = (a, b, c) if u == 0 else (dv + a, dk + b, dq + c)
                R.dproj(0)[sl, cs] = (dq * 0.125).astype(BF16)
                R.dproj(1)[sl, cs] = dk.astype(BF16)
                R.dproj(2)[sl, cs] = dv.astype(BF16)
    @add("tn1", 0.6)
    def _(): R.trans[...] = jnp.transpose(R.normed[...])
    for n in range(3):
        @add(f"gqk{n}", 1.2)
        def _(n=n):
            cs = slice(256 * n, 256 * n + 256)
            put_pair(0, 0, cs, dot(R.trans[...], R.dproj(0)[:, cs]), dot(R.trans[...], R.dproj(1)[:, cs]))
    for n in range(3):
        @add(f"gvo{n}", 1.5)
        def _(n=n):
            cs = slice(256 * n, 256 * n + 256)
            put_pair(0, 1, cs, dot(R.trans[...], R.dproj(2)[:, cs]), dot(R.attended[...], R.attn_grad[:, cs], TN))
    for n in range(3):
        @add(f"gn1{n}", 1.3)
        def _(n=n):
            cs = slice(256 * n, 256 * n + 256)
            acc = dot(R.dproj(0)[...], R.W0(0)[cs, :], NT)
            for j in range(1, 3): acc = acc + dot(R.dproj(j)[...], R.W0(j)[cs, :], NT)
            R.tmp[:, cs] = acc
    for b in range(ROWS // B):
        sl = slice(B * b, B * b + B)
        @add(f"ln1b{b}", 0.5)
        def _(sl=sl, b=b):
            g = R.tmp[sl, :]
            ch = R.chosen[sl, :].astype(F32)
            xh, r = ln(ch)
            grow("attn_gain", colsum(g * xh), b == 0)
            grow("attn_shift", colsum(g), b == 0)
            grow("router_weight", colsum(R.logit[sl, :] * ch), b == 0)
            e = g * R.vec("attn_gain")
            cg = r * (e - jnp.mean(e, axis=-1, keepdims=True) - xh * jnp.mean(e * xh, axis=-1, keepdims=True))
            R.attn_grad[sl, :] = (cg + R.hidden[sl, :] + R.logit[sl, :] * R.vec("router_weight")).astype(BF16)
    for n in range(2):
        @add(f"ingrad{n}", 1.0)
        def _(n=n):
            cs = slice(384 * n, 384 * n + 384)
            total = both(R.ct, cs).astype(F32)
            for i in range(2): total = total + dot(spread(R, i), R.attn_grad[CAP * i : CAP * i + CAP, cs])
            R.input_grad(n, cs, total.astype(BF16).reshape(LONG, 2, 384))
    return T


PHASES = 3
TYPES = (("ZXY", 0, 16), ("XZY", 16, 32), ("ZYX", 48, 16), ("YZX", 64, 32))
MESH = pl.DeviceIdType.MESH
LINK = {"C": 0, "X": 1, "Y": 2, "P": 3, "Q": 4}
NAMES = ("attn_gain", "attn_shift", "mlp_gain", "mlp_shift", "router_weight", "down_bias")
ROW = {name: k for k, name in enumerate(NAMES)} | {"up_bias": 6}
FEW = (("ZXY", 0, 48), ("ZYX", 48, 48))
SPLIT = 1536
AGROUPS = ((0, 0, 256, FEW), (0, 256, 256, FEW), (0, 512, 256, FEW), (3072, 0, 768, TYPES), (6144, 0, 768, TYPES))
GROUPS = ((3072, 0, 768, FEW), (0, 0, 768, FEW), (6144, 0, 256, FEW), (6144, 256, 256, FEW), (6144, 512, 256, TYPES))
VSTEPS = "CXYPW"
ZPARTNERS = "PWV"
PLANE = ("C", "X", "Y", "XC", "YC", "XY", "XYC")


def all_events(trees):
    out = []
    size = {"X": 2, "Y": 2, "Z": 4}
    for t, (perm, _, _) in enumerate(trees):
        for a in range(3):
            for o in range(1, size[perm[a]]):
                for combo in itertools.product(*[range(size[q]) for q in perm[:a]]):
                    e = {"X": 0, "Y": 0, "Z": 0}
                    e[perm[a]] = o
                    for q, v in zip(perm[:a], combo):
                        e[q] = v
                    out.append((t, e["X"], e["Y"], e["Z"], a))
    return out


class Place:
    def __init__(self):
        dp = lax.axis_index("dp")
        self.x, self.dp = lax.axis_index("shard"), dp
        self.c, self.y, self.z = dp % 2, (dp // 2) % 2, dp // 4
        z = self.z
        self.mid = ((z + 1) // 2) % 2
        self.zs = [z, z + 1 - 2 * (z % 2), 2 - z // 2, 3 - 3 * (z // 2)]
        self.me = dp * 2 + self.x

    def dev(self, k):
        dp, x = self.dp, self.x
        if k == "C":
            return (dp + 1 - 2 * self.c, x)
        if k == "X":
            return (dp, 1 - x)
        if k == "Y":
            return (dp + 2 - 4 * self.y, x)
        if k in ZPARTNERS or k == "Q":
            z = {"P": self.zs[1], "Q": 3 - self.z, "V": 3 - self.z, "W": (self.z + 2) % 4}[k]
            return (z * 4 + self.y * 2 + self.c, x)
        c = 1 - self.c if "C" in k else self.c
        y = 1 - self.y if "Y" in k else self.y
        return ((self.z * 2 + y) * 2 + c, 1 - x if "X" in k else x)

    def src(self, xo, yo, j):
        sx = self.x if xo == 0 else 1 - self.x
        sy = self.y if yo == 0 else 1 - self.y
        sz = self.zs[j]
        return (sz * 2 + sy) * 2 + sx, ((sz * 2 + sy) * 2 + self.c) * 2 + sx

    def signal(self, sem, kinds):
        for k in kinds:
            if k == "Q":
                @pl.when(self.mid == 1)
                def _():
                    pl.semaphore_signal(sem, inc=1, device_id=self.dev("Q"), device_id_type=MESH)
            else:
                pl.semaphore_signal(sem, inc=1, device_id=self.dev(k), device_id_type=MESH)


class Traffic:
    def __init__(self, pc, ref, send, spare, width=D):
        self.pc, self.ref, self.send, self.spare, self.width = pc, ref, send, spare, width
        self.rows = {}

    def note(self, k, n, where="all"):
        self.rows[(k, where)] = self.rows.get((k, where), 0) + n

    def wait(self):
        def one(k, where):
            rows = self.rows.get((k, where), 0)
            if rows:
                b = self.ref.at[pl.ds(0, rows), pl.ds(0, self.width)]
                pltpu.make_async_remote_copy(b, b, self.send.at[LINK[k]], self.spare, device_id=self.pc.dev("C"), device_id_type=MESH).wait_send()

        for k in "CXY":
            one(k, "all")
        for m, where in ((1, "mid"), (0, "end")):
            @pl.when(self.pc.mid == m)
            def _():
                for k in "PQ":
                    one(k, where)


class Gather:
    def __init__(self, pc, group, buf, recv, crecv, send):
        self.pc, self.buf, self.recv, self.crecv, self.send = pc, buf, recv, crecv, send
        self.base, self.col, self.width, self.trees = AGROUPS[group]
        self.traffic = Traffic(pc, buf, send, crecv, self.width)

    def block(self, t, shard):
        _, r0, n = self.trees[t]
        return self.buf.at[pl.ds(pl.multiple_of(self.base + shard * CH + r0, 16), n), pl.ds(self.col, self.width)]

    def copy(self, t, chip, shard, k):
        b = self.block(t, shard)
        rs = self.crecv if k == "C" else self.recv.at[t, chip]
        return pltpu.make_async_remote_copy(b, b, self.send.at[LINK[k]], rs, device_id=self.pc.dev(k), device_id_type=MESH)

    def forward(self, t, xo, yo, j, last):
        pc, tr = self.pc, self.traffic
        perm, _, n = self.trees[t]
        chip, shard = pc.src(xo, yo, j)
        if perm.index("Z") >= last:
            if j == 0:
                self.copy(t, chip, shard, "P").start()
                tr.note("P", n, "end")
                tr.note("P", n, "mid")
            k = "Q" if j in (0, 1) else "P"
            tr.note(k, n, "mid")

            @pl.when(pc.mid == 1)
            def _():
                self.copy(t, chip, shard, k).start()
        for k in "XY":
            if k in perm[last + 1 :]:
                self.copy(t, chip, shard, k).start()
                tr.note(k, n)
        self.copy(t, chip, shard, "C").start()
        tr.note("C", n)

    def own(self):
        for t in range(len(self.trees)):
            self.forward(t, 0, 0, 0, -1)

    def step(self, ev):
        t, xo, yo, j, a = ev
        chip, shard = self.pc.src(xo, yo, j)
        b = self.block(t, shard)
        pltpu.make_async_remote_copy(b, b, self.send.at[1], self.recv.at[t, chip], device_id=self.pc.dev("X"), device_id_type=MESH).wait_recv()
        self.forward(t, xo, yo, j, a)

    def all_here(self):
        b = self.buf.at[pl.ds(0, 16 * CH), pl.ds(0, self.width)]
        pltpu.make_async_remote_copy(b, b, self.send.at[0], self.crecv, device_id=self.pc.dev("C"), device_id_type=MESH).wait_recv()


class Landing:
    def __init__(self, trees):
        self.off, self.n, self.sem = {}, 0, {}
        for t, (perm, _, n) in enumerate(trees):
            for k in "XY":
                a = perm.index(k)
                other = "Y" if k == "X" else "X"
                for j in range(4):
                    for o in range(2):
                        if (j and perm.index("Z") > a) or (o and perm.index(other) > a):
                            continue
                        self.add((t, k, j, o), n)
            a = perm.index("Z")
            for xo in range(2):
                for yo in range(2):
                    if (xo and perm.index("X") > a) or (yo and perm.index("Y") > a):
                        continue
                    for s in range(5):
                        self.add((t, "Z", xo, yo, s), n)

    def add(self, key, n):
        if self.n < SPLIT < self.n + n:
            self.n = SPLIT
        self.off[key] = self.n
        self.n += n
        self.sem[key] = len(self.sem)


LANDS = {trees: Landing(trees) for trees in (TYPES, FEW)}
LAND_ROWS = max(v.n for v in LANDS.values())
LAND_SEMS = max(len(v.sem) for v in LANDS.values())


class Reduce:
    def __init__(self, pc, group, buf, land, cland, recv, crecv, send, done):
        self.pc, self.buf, self.land, self.cland, self.recv, self.crecv, self.send, self.done = pc, buf, land, cland, recv, crecv, send, done
        self.base, self.col, self.width, self.trees = GROUPS[group]
        self.places = LANDS[self.trees]
        self.cdone = set()
        self.traffic = Traffic(pc, buf, send, crecv.at[0], self.width)

    def rows(self, off, n):
        return self.buf.at[pl.ds(pl.multiple_of(self.base + off, 16), n), pl.ds(self.col, self.width)]

    def block(self, t, shard):
        _, r0, n = self.trees[t]
        return self.rows(shard * CH + r0, n)

    def cslot(self, xo, yo, j):
        return (j * 2 + yo) * 2 + xo

    def csend(self, offsets):
        pc = self.pc
        for xo, yo, j in offsets:
            _, shard = pc.src(xo, yo, j)
            s = self.cslot(xo, yo, j)
            pltpu.make_async_remote_copy(
                self.rows((shard + 2 - 4 * pc.c) * CH, CH), self.cland(s * CH, CH),
                self.send.at[0], self.crecv.at[s], device_id=pc.dev("C"), device_id_type=MESH).start()
            self.traffic.note("C", CH)

    def arrive(self, key):
        r = self.land(self.places.off[key], self.trees[key[0]][2])
        pltpu.make_async_remote_copy(r, r, self.send.at[1], self.recv.at[self.places.sem[key]], device_id=self.pc.dev("X"), device_id_type=MESH).wait_recv()
        return r[...].astype(F32)

    def total(self, t, xo, yo, j, last):
        pc = self.pc
        perm, r0, n = self.trees[t]
        _, shard = pc.src(xo, yo, j)
        b = self.block(t, shard)
        s = self.cslot(xo, yo, j)
        if s not in self.cdone:
            self.cdone.add(s)
            r = self.cland(s * CH, CH)
            pltpu.make_async_remote_copy(r, r, self.send.at[0], self.crecv.at[s], device_id=pc.dev("C"), device_id_type=MESH).wait_recv()
        acc = b[...].astype(F32) + self.cland(s * CH + r0, n)[...].astype(F32)
        for k in "XY":
            if k in perm[last + 1 :]:
                acc = acc + self.arrive((t, k, j, yo if k == "X" else xo))
        middle = None
        if perm.index("Z") >= last:
            if j == 0:
                acc = acc + self.arrive((t, "Z", xo, yo, 0))
            middle = (t, "Z", xo, yo, 1 if j == 0 else 1 + j)
        return acc, b, middle

    def own(self):
        for t, (_, r0, n) in enumerate(self.trees):
            acc, _, middle = self.total(t, 0, 0, 0, -1)
            dst = self.done.at[pl.ds(r0, n), pl.ds(self.col, self.width)]
            dst[...] = acc

            @pl.when(self.pc.mid == 1)
            def _():
                dst[...] = dst[...] + self.arrive(middle)

    def step(self, ev):
        pc = self.pc
        t, xo, yo, j, a = ev
        perm, _, n = self.trees[t]
        acc, b, middle = self.total(t, xo, yo, j, a)
        b[...] = acc.astype(BF16)
        if middle is not None:
            @pl.when(pc.mid == 1)
            def _():
                b[...] = (b[...].astype(F32) + self.arrive(middle)).astype(BF16)

        def go(key, k):
            pltpu.make_async_remote_copy(b, self.land(self.places.off[key], n), self.send.at[LINK[k]], self.recv.at[self.places.sem[key]],
                                         device_id=pc.dev(k), device_id_type=MESH).start()

        k = perm[a]
        if k in "XY":
            go((t, k, j, yo if k == "X" else xo), k)
            self.traffic.note(k, n)
        elif j == 1:
            go((t, "Z", xo, yo, 0), "P")
            self.traffic.note("P", n, "end")
            self.traffic.note("P", n, "mid")
        else:
            @pl.when(pc.mid == 0)
            def _():
                go((t, "Z", xo, yo, 1 + j), "P")

            @pl.when(pc.mid == 1)
            def _():
                go((t, "Z", xo, yo, j - 1), "Q")

            self.traffic.note("P", n, "end")
            self.traffic.note("Q", n, "mid")


class SmallSum:
    def __init__(self, pc, total, out, arrived, send, recv):
        self.pc, self.total, self.out, self.arrived, self.send, self.recv = pc, total, out, arrived, send, recv

    def copy(self, k):
        return pltpu.make_async_remote_copy(self.out.at[k], self.arrived.at[k], self.send.at[k], self.recv.at[k],
                                            device_id=self.pc.dev(VSTEPS[k]), device_id_type=MESH)

    def step(self, k):
        if k:
            self.copy(k - 1).wait_recv()
            self.total[...] = self.total[...] + self.arrived[k - 1]
        if k < 5:
            self.out[k] = self.total[...]
            self.copy(k).start()

    def finish(self):
        for k in range(5):
            self.copy(k).wait_send()


class PlaneSum:
    def __init__(self, pc, parts, total, one, two, send, recv):
        self.pc, self.parts, self.total, self.one, self.two, self.send, self.recv = pc, parts, total, one, two, send, recv

    def copy(self, k):
        pc = self.pc
        if k < 7:
            kind = PLANE[k]
            y = 1 - pc.y if "Y" in kind else pc.y
            c = 1 - pc.c if "C" in kind else pc.c
            x = 1 - pc.x if "X" in kind else pc.x
            src, dst = self.parts.at[y * 4 + c * 2 + x], self.one.at[k]
        else:
            kind, src, dst = ZPARTNERS[k - 7], self.total.at[0], self.two.at[k - 7]
        return pltpu.make_async_remote_copy(src, dst, self.send.at[k], self.recv.at[k], device_id=pc.dev(kind), device_id_type=MESH)

    def step(self, k):
        pc = self.pc
        if k == 0:
            for i in range(7):
                self.copy(i).start()
        if k == 1:
            acc = self.parts[pc.y * 4 + pc.c * 2 + pc.x]
            for i in range(7):
                self.copy(i).wait_recv()
                acc = acc + self.one[i]
            self.total[0] = acc
            for i in range(7, 10):
                self.copy(i).start()
        if k == 2:
            acc = self.total[0]
            for i in range(3):
                self.copy(7 + i).wait_recv()
                acc = acc + self.two[i]
            self.total[1] = acc

    def finish(self):
        for k in range(10):
            self.copy(k).wait_send()


def lane(rows, columns, axis):
    return lax.broadcasted_iota(jnp.int32, (rows, columns), axis)


def group24(d):
    return lax.shift_right_logical(d * 2731, 16)


def group96(f):
    return lax.shift_right_logical(f * 683, 16)


def unpack_small(total, vecs):
    v = total[...].astype(BF16)
    d = lane(256, D, 1)
    mine = group24(lane(SH, D, 1)) == lane(SH, D, 0)
    for k in range(6):
        pick = jnp.where(lane(256, D, 0) == 24 * k + d - 24 * group24(d), 1.0, 0.0).astype(BF16)
        vecs[k : k + 1, 0:D] = jnp.sum(jnp.where(mine, dot(v, pick), 0.0), axis=0, keepdims=True)
    pick = jnp.where(lane(256, D, 0) == 144 + d - 96 * group96(d), 1.0, 0.0).astype(BF16)
    wide = dot(v, pick)
    for j in range(4):
        mine = group96(lane(SH, D, 1)) + 8 * j == lane(SH, D, 0)
        vecs[6:7, D * j : D * j + D] = jnp.sum(jnp.where(mine, wide, 0.0), axis=0, keepdims=True)


def wide_dot(a, b):
    return lax.dot_general(a, b, NN, precision=lax.Precision.HIGHEST, preferred_element_type=F32)


def pack_small(vterm, parts):
    d = lane(D, 128, 0)
    row = lane(64, D, 0)
    shard = (row & 7) * 8 + lax.shift_right_logical(row, 3)
    owner = group24(lane(64, D, 1))
    place = jnp.where(lane(D, 128, 1) == d - 24 * group24(d), 1.0, 0.0).astype(F32)
    rows = jnp.concatenate([jnp.where(owner == shard, vterm[k : k + 1, 0:D], 0.0) for k in range(6)], axis=0)
    cut = wide_dot(rows, place)
    place = jnp.where(lane(D, 128, 1) == d - 96 * group96(d), 1.0, 0.0).astype(F32)
    owner = group96(lane(64, D, 1))
    rows = jnp.where(owner == shard, vterm[6:7, 0:D], 0.0)
    for j in range(1, 4):
        rows = rows + jnp.where(owner + 8 * j == shard, vterm[6:7, D * j : D * j + D], 0.0)
    last = wide_dot(rows, place)
    out = jnp.zeros((64, 256), F32)
    for k in range(7):
        shift = jnp.where(lane(128, 256, 1) == lane(128, 256, 0) + 24 * k, 1.0, 0.0).astype(F32)
        out = out + wide_dot(cut[64 * k : 64 * k + 64, :] if k < 6 else last, shift)
    for k in range(8):
        parts[k] = out[8 * k : 8 * k + 8, :]


SCRATCH = dict(
    G=((PHASES * SH * CH, D), BF16), w0=((SH * CH, D), BF16), w1=((SH * CH, D), BF16), cl2=((16 * CH, D), BF16),
    land12=((2 * LAND_ROWS, D), BF16), act_=((4 * ROWS, D), BF16), gp_=((4 * ROWS, D), BF16), proj_=((3 * ROWS, D), BF16),
    hidden=((ROWS, D), F32), tmp=((ROWS, D), F32), chosen=((ROWS, D), BF16), picked=((ROWS, D), BF16), normed=((ROWS, D), BF16),
    feed=((ROWS, D), BF16), delta=((ROWS, D), BF16), attended=((ROWS, D), BF16), normed_two=((ROWS, D), BF16), attn_grad=((ROWS, D), BF16),
    trans=((D, ROWS), BF16), lse=((2, CAP, 128), F32), lse_row=((2, 16, CAP), F32), gate=((ROWS, 1), F32), live=((ROWS, 1), F32),
    logit=((ROWS, 1), F32), tok=((LONG, 2, D), BF16), ct=((LONG, 2, D), BF16), vecs=((8, 4 * D), F32), vterm=((8, 4 * D), F32),
    obuf=((PHASES * CH, D), F32), vtotal=((SH, 256), F32), vout=((5, SH, 256), F32), varr=((5, SH, 256), F32),
    pparts=((8, 8, 256), F32), ptotal=((2, 8, 256), F32), pone=((7, 8, 256), F32), ptwo=((3, 8, 256), F32),
)
SEMS = dict(lsem=(2,), osem=(11,), arecv=(len(AGROUPS), len(TYPES), 16), acrecv=(len(AGROUPS),), asend=(len(AGROUPS), 5), rrecv=(len(GROUPS), LAND_SEMS),
            rcrecv=(len(GROUPS), 16), rsend=(len(GROUPS), 5), vsend=(5,), vrecv=(5,), psend=(10,), precv=(10,))
INS = ("sel", "lens", "v0", "v1", "v2", "v3", "v4", "v5", "v6", "qkv_w", "out_w", "up_w", "down_w", "tok_h", "ct_h")
OUTS = ("out_h", "ing_h", "small", "gqkv_h", "gout_h", "gup_h", "gdown_h")


def compute_order():
    out = []

    def tiles(*names):
        out.extend(("tile", name) for name in names)

    def grid(stem, *counts):
        tiles(*[stem + "".join(map(str, at)) for at in itertools.product(*[range(n) for n in counts])])

    grid("pick", 2)
    grid("norm", 6)
    for n in range(3):
        out.append(("pd", n))
        tiles(f"relay0_{n}", *[f"qkv{j}{n}" for j in range(3)])
        tiles(*[f"attn{i}{h}" for h in (2 * n, 2 * n + 1) for i in range(2)])
    grid("out", 3)
    grid("norm2", 6)
    out.append(("pd", 3))
    grid("relay1_", 4)
    grid("up", 4, 3)
    grid("gdown", 4, 3)
    out.append(("csend", 0))
    tiles("bdown")
    out.append(("pd", 4))
    grid("gact", 4, 3)
    grid("down", 3)
    out.extend([("agfin",), ("free",)])
    tiles("tn2")
    grid("gup", 2, 3)
    out.append(("csend", 1))
    grid("gn2", 3)
    grid("ln2b", 6)
    grid("gatt", 3)
    tiles("tn1")
    out.append(("wfree",))
    for n in range(3):
        tiles(*[f"attb{i}{h}" for h in (2 * n, 2 * n + 1) for i in range(2)])
        tiles(f"gqk{n}", f"gvo{n}")
        out.append(("csend", 2 + n))
    grid("gate", 6)
    grid("gn1", 3)
    grid("ln1b", 6)
    tiles("vecpack")
    out.extend(("vstep", 1, k) for k in range(2))
    return out


def catalogue():
    items = [("ag", g, e) for g, group in enumerate(AGROUPS) for e in all_events(group[3])]
    items += [("own", g) for g in range(len(AGROUPS))]
    items += [("rs", g, e) for g, group in enumerate(GROUPS) for e in all_events(group[3])]
    items += [("rsown", g) for g in range(len(GROUPS))]
    items += [("vstep", 0, k) for k in range(5)]
    return items + compute_order() + [("tile", name) for name in ("output0", "output1", "ingrad0", "ingrad1")]


def mega_kernel(names, order, *refs):
    fields = INS + OUTS + tuple(SCRATCH) + tuple(SEMS) + ("free_c", "free_all")
    R = types.SimpleNamespace(**dict(zip(fields, refs)))
    pc = Place()
    loads = [pltpu.make_async_copy(R.tok_h, R.tok, R.lsem.at[0]), pltpu.make_async_copy(R.ct_h, R.ct, R.lsem.at[1])]
    for cp in loads:
        cp.start()
    barrier = pltpu.get_barrier_semaphore()
    pc.signal(barrier, PLANE + ("P", "W", "V", "Q"))
    for p in range(PHASES):
        if p == 0:
            v = jnp.concatenate([R.qkv_w[:, D * j : D * j + D].astype(F32) for j in range(3)] + [R.out_w[...].astype(F32)], axis=0).astype(BF16)
        elif p == 1:
            v = jnp.concatenate([R.up_w[:, D * j : D * j + D].astype(F32) for j in range(4)], axis=0).astype(BF16)
        else:
            v = R.down_w[...]
        R.G[pl.ds(pl.multiple_of((p * SH + pc.me) * CH, 16), CH), :] = v
    vrow = jnp.concatenate([v[...].astype(F32) for v in (R.v0, R.v1, R.v2, R.v3, R.v4, R.v5, R.v6)] + [jnp.zeros((1, 16), F32)], axis=1)
    R.vtotal[...] = jnp.where(lane(SH, 256, 0) == pc.me, vrow, 0.0)
    pl.semaphore_wait(barrier, 10 + pc.mid)

    ag = [Gather(pc, g, R.G, R.arecv.at[g], R.acrecv.at[g], R.asend.at[g]) for g in range(len(AGROUPS))]

    def landing(g):
        def land(off, n):
            if g < 2:
                return R.land12.at[pl.ds(g * LAND_ROWS + off, n), :]
            cs = pl.ds(GROUPS[g][1], GROUPS[g][2])
            if off < SPLIT:
                return R.w1.at[pl.ds(SPLIT + off, n), cs]
            return R.act_.at[pl.ds(off, n), cs]

        def cland(off, n):
            ref = (R.cl2, R.act_, R.w1)[min(g, 2)]
            return ref.at[pl.ds(off, n), pl.ds(GROUPS[g][1], GROUPS[g][2])]

        return land, cland

    owned = [R.obuf.at[pl.ds(CH * (2 - min(g, 2)), CH), :] for g in range(len(GROUPS))]
    rs = [Reduce(pc, g, R.G, *landing(g), R.rrecv.at[g], R.rcrecv.at[g], R.rsend.at[g], owned[g]) for g in range(len(GROUPS))]
    sums = [SmallSum(pc, R.vtotal, R.vout, R.varr, R.vsend, R.vrecv), PlaneSum(pc, R.pparts, R.ptotal, R.pone, R.ptwo, R.psend, R.precv)]

    R.VEC = {name: (k, D) for name, k in ROW.items()}
    R.VEC["up_bias"] = (ROW["up_bias"], 4 * D)

    def vec(name, off=0, n=None):
        r, w = R.VEC[name]
        return R.vecs[r : r + 1, off : off + (n or w)]

    def view(ref, rows):
        return lambda j: ref.at[pl.ds(rows * j, rows), :]

    R.vec = vec
    R.act, R.gp, R.proj, R.dproj = view(R.act_, ROWS), view(R.gp_, ROWS), view(R.proj_, ROWS), view(R.gp_, ROWS)
    R.W0, R.W1 = view(R.w0, D), view(R.w1, D)
    R.W2 = lambda j: R.G.at[pl.ds(2 * SH * CH + D * j, D), :]
    R.part = lambda p: R.G.at[pl.ds(GROUPS[2 - p][0], SH * CH), :]
    R.change = R.datt = R.feed
    stores = []

    def store(src, dst):
        cp = pltpu.make_async_copy(src, dst, R.osem.at[len(stores)])
        cp.start()
        stores.append(cp)

    def output(n, cs, v):
        R.tok[:, :, cs] = v
        if n == 1:
            store(R.tok, R.out_h)

    def input_grad(n, cs, v):
        R.ct[:, :, cs] = v
        if n == 1:
            store(R.ct, R.ing_h)

    R.output, R.input_grad = output, input_grad
    tiles = {name: f for name, _, _, f in fwd_tiles(R) + bwd_tiles(R)}
    program = [names[k] for k in order]
    offsets = {}
    for it in program:
        if it[0] in ("rs", "rsown"):
            o = it[2][1:4] if it[0] == "rs" else (0, 0, 0)
            if o not in offsets.setdefault(it[1], []):
                offsets[it[1]].append(o)
    finished = set()
    for it in program:
        kind = it[0]
        if kind == "ag":
            ag[it[1]].step(it[2])
        elif kind == "own":
            ag[it[1]].own()
        elif kind == "pd":
            ag[it[1]].all_here()
        elif kind == "rs":
            rs[it[1]].step(it[2])
        elif kind == "rsown":
            g = it[1]
            rs[g].own()
            finished.add(g)
            if g == 0:
                store(owned[g], R.gdown_h)
            elif g == 1:
                for j in range(4):
                    store(owned[g].at[pl.ds(24 * j, 24), :], R.gup_h.at[:, pl.ds(D * j, D)])
            elif finished >= {2, 3, 4}:
                for j in range(3):
                    store(owned[g].at[pl.ds(24 * j, 24), :], R.gqkv_h.at[:, pl.ds(D * j, D)])
                store(owned[g].at[pl.ds(72, 24), :], R.gout_h)
        elif kind == "free":
            pc.signal(R.free_c, "C")
        elif kind == "vstep":
            sums[it[1]].step(it[2])
        elif kind == "csend":
            g = it[1]
            if g == 1:
                pl.semaphore_wait(R.free_c, 1)
            if g == 2:
                pl.semaphore_wait(R.free_all, 4 + pc.mid)
            rs[g].csend(offsets[g])
        elif kind == "tile":
            name = it[1]
            if name == "pick0":
                for cp in loads:
                    cp.wait()
            if name == "norm0":
                sums[0].step(5)
                unpack_small(R.vtotal, R.vecs)
            if name == "vecpack":
                pack_small(R.vterm, R.pparts)
            else:
                if name == "gdown00":
                    ag[3].traffic.wait()
                if name == "gup00":
                    for g in range(3):
                        ag[g].traffic.wait()
                if name == "gqk0":
                    ag[4].traffic.wait()
                tiles[name]()
            if name == "gn22":
                pc.signal(R.free_all, "CXYPQ")
    sums[1].step(2)
    R.small[...] = R.ptotal[1, pl.ds(pc.z, 1), :]
    for r in rs:
        r.traffic.wait()
    for s in sums:
        s.finish()
    for cp in stores:
        cp.wait()


def mega(names, order, *args):
    S = jax.ShapeDtypeStruct
    V, H = pl.BlockSpec(memory_space=pltpu.VMEM), pl.BlockSpec(memory_space=pl.ANY)
    outs = [S((LONG, 2, D), BF16), S((LONG, 2, D), BF16), S((1, 256), F32), S((24, 3 * D), F32), S((24, D), F32), S((24, 4 * D), F32), S((96, D), F32)]
    return pl.pallas_call(
        functools.partial(mega_kernel, names, order), out_shape=outs, in_specs=[V] * 13 + [H, H],
        out_specs=[H, H, V, H, H, H, H],
        scratch_shapes=[pltpu.VMEM(*s) for s in SCRATCH.values()] + [pltpu.SemaphoreType.DMA(s) for s in SEMS.values()] + [pltpu.SemaphoreType.REGULAR] * 2,
        compiler_params=pltpu.CompilerParams(collective_id=0, has_side_effects=True, vmem_limit_bytes=VMEM_LIMIT),
        cost_estimate=pl.CostEstimate(flops=26_000_000_000, bytes_accessed=12_000_000, transcendentals=6_000_000),
    )(*args)


def hand_on_kernel(*refs):
    small, srcs, outs, bufs, sems = refs[0], refs[1:7], refs[7:20], refs[20:26], refs[26]
    steps = []
    for k, (src, dst, buf) in enumerate(zip(srcs, outs, bufs)):
        for part in range(4 if k < 2 else 1):
            cut = (lambda r: r.at[pl.ds(145 * part, 145 if part < 3 else LONG - 435)]) if k < 2 else (lambda r: r)
            n = len(steps)
            there = pltpu.make_async_copy(cut(src), cut(buf), sems.at[0, n])
            there.start()
            steps.append((there, pltpu.make_async_copy(cut(buf), cut(dst), sems.at[1, n])))
    for k in range(7):
        outs[6 + k][...] = small[:, 24 * k : 24 * k + (24 if k < 6 else 96)]
    for there, back in steps:
        there.wait()
        back.start()
    for _, back in steps:
        back.wait()


def hand_on(small, *arrays):
    V, H = pl.BlockSpec(memory_space=pltpu.VMEM), pl.BlockSpec(memory_space=pl.ANY)
    outs = [jax.ShapeDtypeStruct(a.shape, a.dtype) for a in arrays]
    outs += [jax.ShapeDtypeStruct((1, 24 if k < 6 else 96), F32) for k in range(7)]
    return pl.pallas_call(hand_on_kernel, out_shape=outs, in_specs=[V] + [H] * 6, out_specs=[H] * 6 + [V] * 7,
                          scratch_shapes=[pltpu.VMEM(a.shape, a.dtype) for a in arrays] + [pltpu.SemaphoreType.DMA((2, 12))],
                          compiler_params=pltpu.CompilerParams(vmem_limit_bytes=VMEM_LIMIT))(small, *arrays)


ORDER = (
    210, 211, 212, 400, 0, 15, 1, 16, 401, 30, 45, 60, 46, 75, 31, 17, 76, 4, 402, 32, 82, 18, 405, 2,
    19, 213, 403, 48, 406, 47, 20, 61, 84, 62, 21, 77, 79, 404, 407, 408, 6, 3, 97, 39, 41, 5, 36, 91,
    49, 90, 9, 56, 34, 105, 409, 410, 50, 7, 411, 33, 121, 22, 10, 51, 13, 138, 142, 69, 28, 412, 120, 25,
    35, 135, 54, 136, 78, 63, 92, 26, 23, 71, 53, 106, 479, 52, 81, 73, 11, 8, 109, 127, 14, 65, 27, 24,
    66, 29, 64, 12, 67, 122, 80, 214, 413, 86, 43, 414, 415, 416, 85, 417, 418, 419, 55, 139, 40, 107, 93, 420,
    421, 110, 59, 129, 58, 88, 37, 57, 44, 123, 42, 38, 137, 68, 94, 140, 108, 125, 124, 146, 422, 423, 424, 425,
    426, 427, 428, 429, 113, 101, 141, 74, 95, 96, 70, 83, 111, 126, 89, 87, 72, 153, 150, 181, 103, 430, 431, 168,
    165, 166, 432, 433, 434, 435, 436, 437, 180, 117, 152, 148, 198, 195, 143, 172, 438, 439, 440, 441, 442, 443, 444, 445,
    151, 157, 196, 116, 115, 182, 187, 128, 131, 130, 100, 112, 169, 133, 102, 202, 145, 183, 114, 147, 99, 98, 104, 167,
    118, 132, 144, 199, 149, 119, 134, 446, 447, 448, 158, 154, 170, 159, 449, 450, 451, 452, 453, 200, 197, 454, 455, 456,
    457, 458, 459, 460, 461, 462, 463, 171, 156, 155, 203, 174, 176, 191, 189, 186, 173, 161, 206, 163, 184, 185, 188, 204,
    201, 464, 465, 466, 467, 468, 469, 470, 471, 472, 473, 474, 475, 190, 160, 207, 205, 179, 192, 162, 177, 193, 175, 178,
    194, 209, 164, 208, 476, 477, 478, 480, 481, 482, 483, 484, 485, 486, 487, 488, 489, 490, 491, 492, 493, 494, 495, 227,
    229, 244, 238, 225, 240, 228, 496, 226, 243, 241, 497, 223, 242, 506, 498, 499, 500, 507, 508, 501, 502, 503, 504, 236,
    224, 505, 221, 219, 509, 510, 511, 512, 513, 514, 515, 516, 517, 518, 259, 274, 256, 270, 273, 234, 519, 239, 520, 521,
    522, 523, 524, 525, 258, 232, 272, 255, 526, 269, 268, 257, 222, 235, 267, 220, 527, 528, 529, 530, 531, 532, 289, 285,
    266, 217, 265, 251, 533, 300, 303, 299, 288, 230, 534, 535, 536, 537, 541, 538, 539, 330, 231, 283, 302, 329, 318, 334,
    332, 319, 286, 540, 264, 304, 271, 262, 547, 542, 548, 543, 544, 545, 377, 345, 247, 333, 326, 392, 287, 284, 390, 364,
    343, 349, 379, 315, 360, 325, 378, 279, 394, 347, 393, 216, 358, 260, 296, 281, 294, 375, 215, 295, 389, 311, 314, 328,
    348, 301, 249, 549, 546, 550, 551, 552, 553, 554, 386, 324, 277, 313, 388, 298, 371, 356, 309, 363, 341, 331, 391, 362,
    292, 307, 322, 385, 317, 373, 339, 346, 250, 280, 233, 370, 253, 382, 291, 275, 344, 555, 556, 320, 282, 340, 237, 352,
    376, 305, 361, 290, 557, 337, 367, 316, 359, 355, 310, 321, 369, 374, 312, 254, 308, 218, 278, 293, 384, 261, 559, 561,
    351, 335, 323, 327, 365, 381, 306, 342, 357, 263, 354, 297, 380, 276, 353, 248, 336, 558, 366, 383, 246, 245, 387, 368,
    252, 372, 395, 338, 350, 398, 397, 560, 562, 399, 396,
)

VMEM_LIMIT = 63 << 20


def on_device_fast(tokens, lengths, selected, cotangent, attn_gain, attn_shift, mlp_gain, mlp_shift, router_weight,
                   qkv_weight, out_weight, up_weight, up_bias, down_weight, down_bias):
    vectors = [v[None] for v in (attn_gain, attn_shift, mlp_gain, mlp_shift, router_weight, down_bias, up_bias)]
    results = mega(catalogue(), ORDER, selected, lengths.T, *vectors, qkv_weight, out_weight, up_weight, down_weight,
                   tokens[:, 0].transpose(1, 0, 2), cotangent[:, 0].transpose(1, 0, 2))
    output, token_grad, owned, gqkv, gout, gup, gdown = results
    output, token_grad, gqkv, gout, gup, gdown, *t = hand_on(owned, output, token_grad, gqkv, gout, gup, gdown)
    t = [v[0] for v in t]
    whole = lambda v: v.transpose(1, 0, 2)[:, None]
    return (whole(output), whole(token_grad), t[0], t[1], t[2], t[3], t[4], gqkv, gout, gup, t[6], gdown, t[5])


HEADS = 12
HEAD_DIM = 64
MICRO = 2


epsilon = 1e-06


def normalize(inputs, norm_gain, norm_shift):
    centered = inputs - jnp.mean(inputs, axis=-1, keepdims=True)
    variance = jnp.mean(centered * centered, axis=-1, keepdims=True)
    return centered * lax.rsqrt(variance + epsilon) * norm_gain + norm_shift


def forward_pass(tokens, lengths, selected, weights):
    (
        attn_gain,
        attn_shift,
        mlp_gain,
        mlp_shift,
        router_weight,
        qkv_weight,
        out_weight,
        up_weight,
        up_bias,
        down_weight,
        down_bias,
    ) = weights
    group_size, capacity = selected.shape
    counts = lengths // 2
    live_mask = (jnp.arange(capacity)[None, :] < counts[:, None]).astype(jnp.float32)
    chosen = jnp.take_along_axis(tokens, selected[:, :, None], axis=1)
    chosen_wide = chosen.astype(jnp.float32)
    logits = jnp.einsum("bcd,d->bc", chosen, router_weight, preferred_element_type=jnp.float32)
    router_gate = jax.nn.sigmoid(logits)
    normed = normalize(
        chosen_wide, attn_gain.astype(jnp.float32), attn_shift.astype(jnp.float32)
    ).astype(jnp.bfloat16)
    projected = jnp.einsum(
        "bcd,de->bce", normed, qkv_weight, preferred_element_type=jnp.float32
    ).astype(jnp.bfloat16)
    projected = projected.reshape(group_size, capacity, 3, HEADS, HEAD_DIM)
    queries = projected[:, :, 0]
    key_rows = projected[:, :, 1]
    value_rows = projected[:, :, 2]
    score_scale = HEAD_DIM ** (-0.5)
    scores = (
        jnp.einsum("bqhe,bkhe->bhqk", queries, key_rows, preferred_element_type=jnp.float32)
        * score_scale
    )
    scores = jnp.where(live_mask[:, None, None, :] > 0, scores, -1000000000.0)
    row_max = jnp.max(scores, axis=-1, keepdims=True)
    exponent = jnp.exp(scores - row_max)
    row_total = jnp.sum(exponent, axis=-1, keepdims=True)
    attention = (exponent / row_total).astype(jnp.bfloat16)
    log_total = row_max + jnp.log(row_total)
    attended = jnp.einsum(
        "bhqk,bkhe->bqhe", attention, value_rows, preferred_element_type=jnp.float32
    ).astype(jnp.bfloat16)
    attended = attended.reshape(group_size, capacity, HEADS * HEAD_DIM)
    attn_out = jnp.einsum("bce,ed->bcd", attended, out_weight, preferred_element_type=jnp.float32)
    hidden = chosen_wide + attn_out
    normed_two = normalize(
        hidden, mlp_gain.astype(jnp.float32), mlp_shift.astype(jnp.float32)
    ).astype(jnp.bfloat16)
    upward = jnp.einsum(
        "bcd,df->bcf", normed_two, up_weight, preferred_element_type=jnp.float32
    ) + up_bias.astype(jnp.float32)
    active = jax.nn.gelu(upward).astype(jnp.bfloat16)
    feed_out = jnp.einsum(
        "bcf,fd->bcd", active, down_weight, preferred_element_type=jnp.float32
    ) + down_bias.astype(jnp.float32)
    change = (attn_out + feed_out) * (router_gate * live_mask)[:, :, None]
    image_rows = jnp.arange(group_size)[:, None]
    output = tokens.astype(jnp.float32).at[image_rows, selected].add(change).astype(jnp.bfloat16)
    kept_values = (
        chosen_wide,
        live_mask,
        router_gate,
        normed,
        projected,
        log_total,
        attended,
        attn_out,
        hidden,
        normed_two,
        upward,
        active,
        feed_out,
    )
    return (output, kept_values)


def backward_pass(cotangent, selected, weights, kept_values):
    (
        attn_gain,
        attn_shift,
        mlp_gain,
        mlp_shift,
        router_weight,
        qkv_weight,
        out_weight,
        up_weight,
        up_bias,
        down_weight,
        down_bias,
    ) = weights
    (
        chosen_wide,
        live_mask,
        router_gate,
        normed,
        projected,
        log_total,
        attended,
        attn_out,
        hidden,
        normed_two,
        upward,
        active,
        feed_out,
    ) = kept_values
    group_size, capacity = selected.shape
    out_grad = cotangent.astype(jnp.float32)
    picked = jnp.take_along_axis(out_grad, selected[:, :, None], axis=1) * live_mask[:, :, None]
    gate_grad = jnp.sum(picked * (attn_out + feed_out), axis=-1)
    logit_grad = gate_grad * router_gate * (1.0 - router_gate)
    change_grad = picked * router_gate[:, :, None]
    feed_grad = change_grad.astype(jnp.bfloat16)
    down_bias_grad = jnp.sum(feed_grad.astype(jnp.float32), axis=(0, 1))
    down_weight_grad = jnp.einsum(
        "bcf,bcd->fd", active, feed_grad, preferred_element_type=jnp.float32
    )
    active_grad = jnp.einsum(
        "bcd,fd->bcf", feed_grad, down_weight, preferred_element_type=jnp.float32
    )
    primal_out, gelu_back = jax.vjp(jax.nn.gelu, upward)
    upward_grad = gelu_back(active_grad)[0].astype(jnp.bfloat16)
    up_bias_grad = jnp.sum(upward_grad.astype(jnp.float32), axis=(0, 1))
    up_weight_grad = jnp.einsum(
        "bcd,bcf->df", normed_two, upward_grad, preferred_element_type=jnp.float32
    )
    normed_two_grad = jnp.einsum(
        "bcf,df->bcd", upward_grad, up_weight, preferred_element_type=jnp.float32
    )
    primal_two, norm_back = jax.vjp(
        normalize, hidden, mlp_gain.astype(jnp.float32), mlp_shift.astype(jnp.float32)
    )
    hidden_grad, mlp_gain_grad, mlp_shift_grad = norm_back(normed_two_grad)
    attn_grad = (change_grad + hidden_grad).astype(jnp.bfloat16)
    out_weight_grad = jnp.einsum(
        "bce,bcd->ed", attended, attn_grad, preferred_element_type=jnp.float32
    )
    attended_grad = jnp.einsum(
        "bcd,ed->bce", attn_grad, out_weight, preferred_element_type=jnp.float32
    ).astype(jnp.bfloat16)
    attended_grad = attended_grad.reshape(group_size, capacity, HEADS, HEAD_DIM)
    queries = projected[:, :, 0]
    key_rows = projected[:, :, 1]
    value_rows = projected[:, :, 2]
    score_scale = HEAD_DIM ** (-0.5)
    key_live = live_mask[:, None, None, :] > 0
    scores = (
        jnp.einsum("bqhe,bkhe->bhqk", queries, key_rows, preferred_element_type=jnp.float32)
        * score_scale
    )
    scores = jnp.where(key_live, scores, -1000000000.0)
    prob_wide = jnp.exp(scores - log_total)
    prob_low = prob_wide.astype(jnp.bfloat16)
    value_grad = jnp.einsum(
        "bhqk,bqhe->bkhe", prob_low, attended_grad, preferred_element_type=jnp.float32
    )
    prob_grad = jnp.einsum(
        "bqhe,bkhe->bhqk", attended_grad, value_rows, preferred_element_type=jnp.float32
    )
    score_grad = prob_wide * (prob_grad - jnp.sum(prob_wide * prob_grad, axis=-1, keepdims=True))
    score_grad = jnp.where(key_live, score_grad.astype(jnp.bfloat16), 0.0) * score_scale
    query_grad = jnp.einsum(
        "bhqk,bkhe->bqhe", score_grad, key_rows, preferred_element_type=jnp.float32
    )
    key_grad = jnp.einsum(
        "bhqk,bqhe->bkhe", score_grad, queries, preferred_element_type=jnp.float32
    )
    projected_grad = jnp.stack([query_grad, key_grad, value_grad], axis=2).astype(jnp.bfloat16)
    projected_grad = projected_grad.reshape(group_size, capacity, 3 * HEADS * HEAD_DIM)
    qkv_weight_grad = jnp.einsum(
        "bcd,bce->de", normed, projected_grad, preferred_element_type=jnp.float32
    )
    normed_grad = jnp.einsum(
        "bce,de->bcd", projected_grad, qkv_weight, preferred_element_type=jnp.float32
    )
    primal_one, first_back = jax.vjp(
        normalize, chosen_wide, attn_gain.astype(jnp.float32), attn_shift.astype(jnp.float32)
    )
    chosen_grad, attn_gain_grad, attn_shift_grad = first_back(normed_grad)
    chosen_grad = (
        chosen_grad + hidden_grad + logit_grad[:, :, None] * router_weight.astype(jnp.float32)
    )
    router_weight_grad = jnp.einsum(
        "bc,bcd->d", logit_grad, chosen_wide, precision=lax.Precision.HIGHEST
    )
    image_rows = jnp.arange(group_size)[:, None]
    token_grad = out_grad.at[image_rows, selected].add(chosen_grad).astype(jnp.bfloat16)
    grad_terms = (
        attn_gain_grad,
        attn_shift_grad,
        mlp_gain_grad,
        mlp_shift_grad,
        router_weight_grad,
        qkv_weight_grad,
        out_weight_grad,
        up_weight_grad,
        up_bias_grad,
        down_weight_grad,
        down_bias_grad,
    )
    return (token_grad, grad_terms)


def on_device(
    tokens,
    lengths,
    selected,
    cotangent,
    attn_gain,
    attn_shift,
    mlp_gain,
    mlp_shift,
    router_weight,
    qkv_weight,
    out_weight,
    up_weight,
    up_bias,
    down_weight,
    down_bias,
):
    outputs = []
    token_grads = []
    totals = None
    for micro_step in range(MICRO):
        forward_weights = (
            lax.all_gather(attn_gain, ("dp", "shard"), axis=0, tiled=True),
            lax.all_gather(attn_shift, ("dp", "shard"), axis=0, tiled=True),
            lax.all_gather(mlp_gain, ("dp", "shard"), axis=0, tiled=True),
            lax.all_gather(mlp_shift, ("dp", "shard"), axis=0, tiled=True),
            lax.all_gather(router_weight, ("dp", "shard"), axis=0, tiled=True),
            lax.all_gather(qkv_weight, ("dp", "shard"), axis=0, tiled=True),
            lax.all_gather(out_weight, ("dp", "shard"), axis=0, tiled=True),
            lax.all_gather(up_weight, ("dp", "shard"), axis=0, tiled=True),
            lax.all_gather(up_bias, ("dp", "shard"), axis=0, tiled=True),
            lax.all_gather(down_weight, ("dp", "shard"), axis=0, tiled=True),
            lax.all_gather(down_bias, ("dp", "shard"), axis=0, tiled=True),
        )
        output, kept_values = forward_pass(
            tokens[micro_step], lengths[micro_step], selected[micro_step], forward_weights
        )
        backward_weights = (
            lax.all_gather(attn_gain, ("dp", "shard"), axis=0, tiled=True),
            lax.all_gather(attn_shift, ("dp", "shard"), axis=0, tiled=True),
            lax.all_gather(mlp_gain, ("dp", "shard"), axis=0, tiled=True),
            lax.all_gather(mlp_shift, ("dp", "shard"), axis=0, tiled=True),
            lax.all_gather(router_weight, ("dp", "shard"), axis=0, tiled=True),
            lax.all_gather(qkv_weight, ("dp", "shard"), axis=0, tiled=True),
            lax.all_gather(out_weight, ("dp", "shard"), axis=0, tiled=True),
            lax.all_gather(up_weight, ("dp", "shard"), axis=0, tiled=True),
            lax.all_gather(up_bias, ("dp", "shard"), axis=0, tiled=True),
            lax.all_gather(down_weight, ("dp", "shard"), axis=0, tiled=True),
            lax.all_gather(down_bias, ("dp", "shard"), axis=0, tiled=True),
        )
        token_grad, grad_terms = backward_pass(
            cotangent[micro_step], selected[micro_step], backward_weights, kept_values
        )
        grad_terms = (
            lax.psum_scatter(grad_terms[0], ("dp", "shard"), scatter_dimension=0, tiled=True),
            lax.psum_scatter(grad_terms[1], ("dp", "shard"), scatter_dimension=0, tiled=True),
            lax.psum_scatter(grad_terms[2], ("dp", "shard"), scatter_dimension=0, tiled=True),
            lax.psum_scatter(grad_terms[3], ("dp", "shard"), scatter_dimension=0, tiled=True),
            lax.psum_scatter(grad_terms[4], ("dp", "shard"), scatter_dimension=0, tiled=True),
            lax.psum_scatter(grad_terms[5], ("dp", "shard"), scatter_dimension=0, tiled=True),
            lax.psum_scatter(grad_terms[6], ("dp", "shard"), scatter_dimension=0, tiled=True),
            lax.psum_scatter(grad_terms[7], ("dp", "shard"), scatter_dimension=0, tiled=True),
            lax.psum_scatter(grad_terms[8], ("dp", "shard"), scatter_dimension=0, tiled=True),
            lax.psum_scatter(grad_terms[9], ("dp", "shard"), scatter_dimension=0, tiled=True),
            lax.psum_scatter(grad_terms[10], ("dp", "shard"), scatter_dimension=0, tiled=True),
        )
        totals = grad_terms if totals is None else jax.tree.map(jnp.add, totals, grad_terms)
        outputs.append(output)
        token_grads.append(token_grad)
    return (
        jnp.stack(outputs),
        jnp.stack(token_grads),
        totals[0],
        totals[1],
        totals[2],
        totals[3],
        totals[4],
        totals[5],
        totals[6],
        totals[7],
        totals[8],
        totals[9],
        totals[10],
    )


def solution(mesh):
    fits = dict(mesh.shape) == {"dp": 16, "shard": 2}
    return jax.shard_map(
        on_device_fast if fits else on_device,
        mesh=mesh,
        in_specs=(
            P(None, ("dp", "shard"), None, None),
            P(None, ("dp", "shard")),
            P(None, ("dp", "shard"), None),
            P(None, ("dp", "shard"), None, None),
            P(("dp", "shard")),
            P(("dp", "shard")),
            P(("dp", "shard")),
            P(("dp", "shard")),
            P(("dp", "shard")),
            P(("dp", "shard"), None),
            P(("dp", "shard"), None),
            P(("dp", "shard"), None),
            P(("dp", "shard")),
            P(("dp", "shard"), None),
            P(("dp", "shard")),
        ),
        out_specs=(
            P(None, ("dp", "shard"), None, None),
            P(None, ("dp", "shard"), None, None),
            P(("dp", "shard")),
            P(("dp", "shard")),
            P(("dp", "shard")),
            P(("dp", "shard")),
            P(("dp", "shard")),
            P(("dp", "shard"), None),
            P(("dp", "shard"), None),
            P(("dp", "shard"), None),
            P(("dp", "shard")),
            P(("dp", "shard"), None),
            P(("dp", "shard")),
        ),
        check_vma=False,
    )
```

```python
import functools
import itertools
import math
import types

import jax
import jax.numpy as jnp
from jax import lax
from jax.experimental import pallas as pl
from jax.experimental.pallas import tpu as pltpu
from jax.sharding import PartitionSpec as P

F32, BF16 = jnp.float32, jnp.bfloat16
D, ROWS, CAP, LONG = 768, 576, 288, 577
SH, CH = 32, 96
NN = (((1,), (0,)), ((), ()))
NT = (((1,), (1,)), ((), ()))
TN = (((0,), (0,)), ((), ()))
def dot(a, b, dims=NN):
    return lax.dot_general(a, b, dims, preferred_element_type=F32)
def ln(rows):
    centered = rows - jnp.mean(rows, axis=-1, keepdims=True)
    rstd = lax.rsqrt(jnp.mean(centered * centered, axis=-1, keepdims=True) + 1e-6)
    return centered * rstd, rstd
def spread(R):
    place = lax.broadcasted_iota(jnp.int32, (2 * LONG, ROWS), 0)
    return jnp.where(place == jnp.concatenate([2 * R.sel[0], 2 * R.sel[1] + 1], axis=1), 1.0, 0.0).astype(BF16)
def choose(R, i):
    place = lax.broadcasted_iota(jnp.int32, (CAP, 2 * LONG), 1)
    column = jnp.transpose(jnp.broadcast_to((2 * R.sel[i] + i).astype(F32), (8, CAP)))[:, 0:1].astype(jnp.int32)
    return jnp.where(place == column, 1.0, 0.0).astype(BF16)
def both(ref, cs=slice(None)):
    return ref[:, :, cs].reshape(2 * LONG, -1)
def live_rows(lens, i):
    slot = lax.broadcasted_iota(jnp.int32, (CAP, 1), 0)
    return (slot < lax.shift_right_logical(lens[:, i : i + 1], 1)).astype(F32)
def live_cols(lens, i):
    slot = lax.broadcasted_iota(jnp.int32, (1, CAP), 1)
    return slot < lax.shift_right_logical(lens[:, i : i + 1], 1)
def relayout(G, W, p, lo, hi, cs=slice(None)):
    for k in range(lo, hi):
        two = [G[(p * SH + 2 * k + u) * CH : (p * SH + 2 * k + u + 1) * CH, cs].astype(F32) for u in range(2)]
        for j in range(4):
            W[D * j + 48 * k : D * j + 48 * k + 48, cs] = jnp.concatenate([t[24 * j : 24 * j + 24, :] for t in two], axis=0).astype(BF16)
def fwd_tiles(R):
    T = []
    def add(name, cost, dep):
        def deco(f): T.append((name, cost, dep, f)); return f
        return deco
    for i in range(2):
        sl = slice(CAP * i, CAP * i + CAP)
        @add(f"pick{i}", 1.0, "tok")
        def _(i=i, sl=sl):
            oh = choose(R, i)
            R.chosen[sl, :] = dot(oh, both(R.tok)).astype(BF16)
            R.stats[sl, 1:2] = live_rows(R.lens, i)
            R.picked[sl, :] = (dot(oh, both(R.ct)) * R.stats[sl, 1:2]).astype(BF16)
    B = 96
    for b in range(ROWS // B):
        sl = slice(B * b, B * b + B)
        @add(f"norm{b}", 0.4, "vec")
        def _(sl=sl):
            ch = R.chosen[sl, :].astype(F32)
            xh, _ = ln(ch)
            R.normed[sl, :] = (xh * R.vec("attn_gain") + R.vec("attn_shift")).astype(BF16)
            logit = jnp.sum(ch * R.vec("router_weight"), axis=-1, keepdims=True)
            gate = 1.0 / (1.0 + jnp.exp(-logit))
            R.stats[sl, 0:1] = gate
            feed = (gate * R.picked[sl, :].astype(F32)).astype(BF16)
            R.feed[sl, :] = feed
    for g in range(3):
        @add(f"relay0_{g}", 0.4, 0)
        def _(g=g): relayout(R.G, R.w0, 0, 0, 16, slice(256 * g, 256 * g + 256))
    for j in range(3):
        for n in range(3):
            @add(f"qkv{j}{n}", 0.45, 0)
            def _(j=j, n=n):
                cs = slice(256 * n, 256 * n + 256)
                R.proj(j)[:, cs] = dot(R.normed[...], R.W0(j)[:, cs]).astype(BF16)
    for i in range(2):
        sl = slice(CAP * i, CAP * i + CAP)
        for h in range(6):
            @add(f"attn{i}{h}", 1.0, 0)
            def _(i=i, h=h, sl=sl):
                cs = slice(128 * h, 128 * h + 128)
                q, k, v = R.proj(0)[sl, cs], R.proj(1)[sl, cs], R.proj(2)[sl, cs]
                low = lax.broadcasted_iota(jnp.int32, (CAP, 128), 1) < 64
                lane = lax.broadcasted_iota(jnp.int32, (CAP, 128), 1)
                live = live_cols(R.lens, i)
                zero, ones = jnp.zeros_like(q), jnp.ones_like(q)
                q = q * 0.125
                outs = []
                lse = R.lse[i] if h else jnp.zeros((CAP, 128), F32)
                for u in range(2):
                    qm, vm = (jnp.where(low, q, zero), jnp.where(low, v, ones)) if u == 0 else (jnp.where(low, zero, q), jnp.where(low, ones, v))
                    s = jnp.where(live, dot(qm, k, NT), -1e9)
                    m = jnp.max(s, axis=-1, keepdims=True)
                    o = dot(jnp.exp(s - m).astype(BF16), vm)
                    tot = o[:, 64:65] if u == 0 else o[:, 0:1]
                    outs.append(o * (1.0 / tot))
                    lse = jnp.where(lane == 2 * h + u, m + jnp.log(tot), lse)
                R.lse[i] = lse
                R.attended[sl, cs] = jnp.where(low, outs[0], outs[1]).astype(BF16)
                if h == 5:
                    R.lse_row[i] = jnp.transpose(lse)[:16, :]
    for n in range(3):
        @add(f"out{n}", 0.45, 0)
        def _(n=n):
            cs = slice(256 * n, 256 * n + 256)
            R.hidden[:, cs] = R.chosen[:, cs].astype(F32) + dot(R.attended[...], R.W0(3)[:, cs])
    for b in range(ROWS // B):
        sl = slice(B * b, B * b + B)
        @add(f"norm2{b}", 0.3, 0)
        def _(sl=sl):
            xh, _ = ln(R.hidden[sl, :])
            R.normed_two[sl, :] = (xh * R.vec("mlp_gain") + R.vec("mlp_shift")).astype(BF16)
    for g in range(4):
        @add(f"relay1_{g}", 0.4, 1)
        def _(g=g): relayout(R.G, R.w1, 1, 4 * g, 4 * g + 4)
    c0 = math.sqrt(2.0 / math.pi)
    for j in range(4):
        for n in range(3):
            @add(f"up{j}{n}", 1.2, 1)
            def _(j=j, n=n):
                cs = slice(256 * n, 256 * n + 256)
                u = dot(R.normed_two[...], R.W1(j)[:, cs]) + R.vec("up_bias", D * j + 256 * n, 256)
                uu = u * u
                half = 0.5 * jnp.tanh(u * (c0 + (c0 * 0.044715) * uu)) + 0.5
                a = u * half
                R.act(j)[:, cs] = a.astype(BF16)
                R.gp(j)[:, cs] = (half + a * (1.0 - half) * (2 * c0 + (6 * c0 * 0.044715) * uu)).astype(BF16)
    for n in range(3):
        @add(f"down{n}", 1.6, 2)
        def _(n=n):
            cs = slice(256 * n, 256 * n + 256)
            acc = R.vec("down_bias", 256 * n, 256) + dot(R.act(0)[...], R.W2(0)[:, cs])
            for j in range(1, 4): acc = acc + dot(R.act(j)[...], R.W2(j)[:, cs])
            R.delta[:, cs] = (acc + (R.hidden[:, cs] - R.chosen[:, cs].astype(F32))).astype(BF16)
    for b in range(ROWS // B):
        sl = slice(B * b, B * b + B)
        @add(f"gate{b}", 0.3, 2)
        def _(sl=sl, b=b):
            if b == 0: R.proj_[0 : 2 * LONG, 0:ROWS] = spread(R)
            d = R.delta[sl, :].astype(F32)
            gate = R.stats[sl, 0:1]
            R.stats[sl, 2:3] = jnp.sum(R.picked[sl, :].astype(F32) * d, axis=-1, keepdims=True) * gate * (1.0 - gate)
            R.change[sl, :] = (d * (gate * R.stats[sl, 1:2])).astype(BF16)
    for n in range(3):
        @add(f"output{n}", 1.0, 2)
        def _(n=n):
            cs = slice(256 * n, 256 * n + 256)
            total = both(R.tok, cs).astype(F32) + dot(R.proj_[0 : 2 * LONG, 0:ROWS], R.change[:, cs])
            R.output(n, cs, total.astype(BF16).reshape(LONG, 2, 256))
    return T


def bwd_tiles(R):
    T = []
    def add(name, cost, dep=None):
        def deco(f): T.append((name, cost, dep, f)); return f
        return deco
    def grow(name, v, first, off=0):
        r, w = R.VEC[name]
        n = v.shape[1]
        if first: R.vterm[r : r + 1, off : off + n] = v
        else: R.vterm[r : r + 1, off : off + n] = R.vterm[r : r + 1, off : off + n] + v
    def colsum(v): return jnp.sum(v, axis=0, keepdims=True)
    def put_pair(p, half, cs, one, two):
        for s in range(SH):
            R.part(p)[s * CH + 48 * half : s * CH + 48 * half + 48, cs] = jnp.concatenate(
                [one[24 * s : 24 * s + 24, :], two[24 * s : 24 * s + 24, :]], axis=0).astype(BF16)
    B = 96
    for j in range(4):
        for n in range(3):
            @add(f"gdown{j}{n}", 0.55)
            def _(j=j, n=n):
                cs = slice(256 * n, 256 * n + 256)
                R.part(2)[D * j + 256 * n : D * j + 256 * n + 256, :] = dot(R.act(j)[:, cs], R.feed[...], TN).astype(BF16)
    @add("bdown", 0.2)
    def _():
        grow("down_bias", colsum(R.feed[...].astype(F32)), True)
    for j in range(4):
        for n in range(3):
            @add(f"gact{j}{n}", 0.6)
            def _(j=j, n=n):
                cs = slice(256 * n, 256 * n + 256)
                g = (dot(R.feed[...], R.W2(j)[cs, :], NT) * R.gp(j)[:, cs].astype(F32)).astype(BF16)
                R.gp(j)[:, cs] = g
                grow("up_bias", colsum(g.astype(F32)), True, D * j + 256 * n)
    @add("tn2", 0.6)
    def _(): R.trans[...] = jnp.transpose(R.normed_two[...])
    for h in range(2):
        for n in range(3):
            @add(f"gup{h}{n}", 1.2)
            def _(h=h, n=n):
                cs = slice(256 * n, 256 * n + 256)
                put_pair(1, h, cs, dot(R.trans[...], R.gp(2 * h)[:, cs]), dot(R.trans[...], R.gp(2 * h + 1)[:, cs]))
    for n in range(3):
        @add(f"gn2{n}", 1.6)
        def _(n=n):
            cs = slice(256 * n, 256 * n + 256)
            acc = dot(R.gp(0)[...], R.W1(0)[cs, :], NT)
            for j in range(1, 4): acc = acc + dot(R.gp(j)[...], R.W1(j)[cs, :], NT)
            R.tmp[:, cs] = acc
    for b in range(ROWS // B):
        sl = slice(B * b, B * b + B)
        @add(f"ln2b{b}", 0.5)
        def _(sl=sl, b=b):
            g = R.tmp[sl, :]
            xh, r = ln(R.hidden[sl, :])
            grow("mlp_gain", colsum(g * xh), b == 0)
            grow("mlp_shift", colsum(g), b == 0)
            e = g * R.vec("mlp_gain")
            hg = r * (e - jnp.mean(e, axis=-1, keepdims=True) - xh * jnp.mean(e * xh, axis=-1, keepdims=True))
            R.hidden[sl, :] = hg
            R.attn_grad[sl, :] = (R.stats[sl, 0:1] * R.picked[sl, :].astype(F32) + hg).astype(BF16)
    for n in range(3):
        @add(f"gatt{n}", 0.45)
        def _(n=n):
            cs = slice(256 * n, 256 * n + 256)
            R.datt[:, cs] = dot(R.attn_grad[...], R.W0(3)[cs, :], NT).astype(BF16)
    for i in range(2):
        sl = slice(CAP * i, CAP * i + CAP)
        for h in range(6):
            @add(f"attb{i}{h}", 1.6)
            def _(i=i, h=h, sl=sl):
                cs = slice(128 * h, 128 * h + 128)
                q, k, v, do = R.proj(0)[sl, cs], R.proj(1)[sl, cs], R.proj(2)[sl, cs], R.datt[sl, cs]
                low = lax.broadcasted_iota(jnp.int32, (CAP, 128), 1) < 64
                live = live_rows(R.lens, i) > 0
                zero = jnp.zeros_like(q)
                q = q * 0.125
                def own(a, u): return jnp.where(low, a, zero) if u == 0 else jnp.where(low, zero, a)
                dq = dk = dv = None
                for u in range(2):
                    qm, km, dm = own(q, u), own(k, u), own(do, u)
                    s = dot(k, qm, NT) - R.lse_row[i, 2 * h + u : 2 * h + u + 1, :]
                    pt = jnp.where(live, jnp.exp(s), 0.0)
                    dp = dot(v, dm, NT)
                    ds = (pt * (dp - colsum(pt * dp))).astype(BF16)
                    a, b, c = dot(pt.astype(BF16), dm), dot(ds, qm), dot(ds, km, TN)
                    dv, dk, dq = (a, b, c) if u == 0 else (dv + a, dk + b, dq + c)
                R.dproj(0)[sl, cs] = (dq * 0.125).astype(BF16)
                R.dproj(1)[sl, cs] = dk.astype(BF16)
                R.dproj(2)[sl, cs] = dv.astype(BF16)
    @add("tn1", 0.6)
    def _(): R.trans[...] = jnp.transpose(R.normed[...])
    for n in range(3):
        @add(f"gqk{n}", 1.2)
        def _(n=n):
            cs = slice(256 * n, 256 * n + 256)
            put_pair(0, 0, cs, dot(R.trans[...], R.dproj(0)[:, cs]), dot(R.trans[...], R.dproj(1)[:, cs]))
    for n in range(3):
        @add(f"gvo{n}", 1.5)
        def _(n=n):
            cs = slice(256 * n, 256 * n + 256)
            put_pair(0, 1, cs, dot(R.trans[...], R.dproj(2)[:, cs]), dot(R.attended[...], R.attn_grad[:, cs], TN))
    for n in range(3):
        @add(f"gn1{n}", 1.3)
        def _(n=n):
            cs = slice(256 * n, 256 * n + 256)
            acc = dot(R.dproj(0)[...], R.W0(0)[cs, :], NT)
            for j in range(1, 3): acc = acc + dot(R.dproj(j)[...], R.W0(j)[cs, :], NT)
            R.tmp[:, cs] = acc
    for b in range(ROWS // B):
        sl = slice(B * b, B * b + B)
        @add(f"ln1b{b}", 0.5)
        def _(sl=sl, b=b):
            g = R.tmp[sl, :]
            ch = R.chosen[sl, :].astype(F32)
            xh, r = ln(ch)
            grow("attn_gain", colsum(g * xh), b == 0)
            grow("attn_shift", colsum(g), b == 0)
            grow("router_weight", colsum(R.stats[sl, 2:3] * ch), b == 0)
            e = g * R.vec("attn_gain")
            cg = r * (e - jnp.mean(e, axis=-1, keepdims=True) - xh * jnp.mean(e * xh, axis=-1, keepdims=True))
            R.attn_grad[sl, :] = (cg + R.hidden[sl, :] + R.stats[sl, 2:3] * R.vec("router_weight")).astype(BF16)
    for n in range(3):
        @add(f"ingrad{n}", 1.0)
        def _(n=n):
            cs = slice(256 * n, 256 * n + 256)
            total = both(R.ct, cs).astype(F32) + dot(R.proj_[0 : 2 * LONG, 0:ROWS], R.attn_grad[:, cs])
            R.input_grad(n, cs, total.astype(BF16).reshape(LONG, 2, 256))
    return T


PHASES = 3
MESH = pl.DeviceIdType.MESH
LINK = {"C": 0, "X": 1, "Y": 2, "P": 3, "Q": 4}
NAMES = ("attn_gain", "attn_shift", "mlp_gain", "mlp_shift", "router_weight", "down_bias")
ROW = {name: k for k, name in enumerate(NAMES)} | {"up_bias": 6}
FEW = (("ZXY", 0, 48), ("ZYX", 48, 48))
SPLIT = 1536
ALSO = (("XZY", 0, 48), ("YZX", 48, 48))
AGROUPS = ((0, 0, 768, ALSO), (3072, 0, 768, FEW), (6144, 0, 768, ALSO))
GROUPS = ((3072, 0, 768, FEW), (0, 0, 768, ALSO), (6144, 0, 256, FEW), (6144, 256, 256, FEW), (6144, 512, 256, FEW))
VSTEPS = "CXYPW"
ZPARTNERS = "PWV"
PLANE = ("C", "X", "Y", "XC", "YC", "XY", "XYC")


def all_events(trees):
    out = []
    size = {"X": 2, "Y": 2, "Z": 4}
    for t, (perm, _, _) in enumerate(trees):
        for a in range(3):
            for o in range(1, size[perm[a]]):
                for combo in itertools.product(*[range(size[q]) for q in perm[:a]]):
                    e = {"X": 0, "Y": 0, "Z": 0}
                    e[perm[a]] = o
                    for q, v in zip(perm[:a], combo):
                        e[q] = v
                    out.append((t, e["X"], e["Y"], e["Z"], a))
    return out


class Place:
    def __init__(self):
        dp = lax.axis_index("dp")
        self.x, self.dp = lax.axis_index("shard"), dp
        self.c, self.y, self.z = dp % 2, (dp // 2) % 2, dp // 4
        z = self.z
        self.mid = ((z + 1) // 2) % 2
        self.zs = [z, z + 1 - 2 * (z % 2), 2 - z // 2, 3 - 3 * (z // 2)]
        self.me = dp * 2 + self.x

    def dev(self, k):
        dp, x = self.dp, self.x
        if k == "C":
            return (dp + 1 - 2 * self.c, x)
        if k == "X":
            return (dp, 1 - x)
        if k == "Y":
            return (dp + 2 - 4 * self.y, x)
        if k in ZPARTNERS or k == "Q":
            z = {"P": self.zs[1], "Q": 3 - self.z, "V": 3 - self.z, "W": (self.z + 2) % 4}[k]
            return (z * 4 + self.y * 2 + self.c, x)
        c = 1 - self.c if "C" in k else self.c
        y = 1 - self.y if "Y" in k else self.y
        return ((self.z * 2 + y) * 2 + c, 1 - x if "X" in k else x)

    def src(self, xo, yo, j):
        sx = self.x if xo == 0 else 1 - self.x
        sy = self.y if yo == 0 else 1 - self.y
        sz = self.zs[j]
        return (sz * 2 + sy) * 2 + sx, ((sz * 2 + sy) * 2 + self.c) * 2 + sx

    def signal(self, sem, kinds):
        for k in kinds:
            if k == "Q":
                @pl.when(self.mid == 1)
                def _():
                    pl.semaphore_signal(sem, inc=1, device_id=self.dev("Q"), device_id_type=MESH)
            else:
                pl.semaphore_signal(sem, inc=1, device_id=self.dev(k), device_id_type=MESH)


class Traffic:
    def __init__(self, pc, ref, send, spare, width=D):
        self.pc, self.ref, self.send, self.spare, self.width = pc, ref, send, spare, width
        self.rows = {}

    def note(self, k, n, where="all"):
        self.rows[(k, where)] = self.rows.get((k, where), 0) + n

    def wait(self):
        def one(k, where):
            rows = self.rows.get((k, where), 0)
            if rows:
                b = self.ref.at[pl.ds(0, rows), pl.ds(0, self.width)]
                pltpu.make_async_remote_copy(b, b, self.send.at[LINK[k]], self.spare, device_id=self.pc.dev("C"), device_id_type=MESH).wait_send()

        for k in "CXY":
            one(k, "all")
        for m, where in ((1, "mid"), (0, "end")):
            @pl.when(self.pc.mid == m)
            def _():
                for k in "PQ":
                    one(k, where)


class Gather:
    def __init__(self, pc, group, buf, recv, crecv, send):
        self.pc, self.buf, self.recv, self.crecv, self.send = pc, buf, recv, crecv, send
        self.base, self.col, self.width, self.trees = AGROUPS[group]
        self.traffic = Traffic(pc, buf, send, crecv, self.width)

    def block(self, t, shard):
        _, r0, n = self.trees[t]
        return self.buf.at[pl.ds(pl.multiple_of(self.base + shard * CH + r0, 16), n), pl.ds(self.col, self.width)]

    def copy(self, t, chip, shard, k):
        b = self.block(t, shard)
        rs = self.crecv if k == "C" else self.recv.at[t, chip]
        return pltpu.make_async_remote_copy(b, b, self.send.at[LINK[k]], rs, device_id=self.pc.dev(k), device_id_type=MESH)

    def forward(self, t, xo, yo, j, last):
        pc, tr = self.pc, self.traffic
        perm, _, n = self.trees[t]
        chip, shard = pc.src(xo, yo, j)
        if perm.index("Z") >= last:
            if j == 0:
                self.copy(t, chip, shard, "P").start()
                tr.note("P", n, "end")
                tr.note("P", n, "mid")
            k = "Q" if j in (0, 1) else "P"
            tr.note(k, n, "mid")

            @pl.when(pc.mid == 1)
            def _():
                self.copy(t, chip, shard, k).start()
        for k in "XY":
            if k in perm[last + 1 :]:
                self.copy(t, chip, shard, k).start()
                tr.note(k, n)
        self.copy(t, chip, shard, "C").start()
        tr.note("C", n)

    def own(self):
        for t in range(len(self.trees)):
            self.forward(t, 0, 0, 0, -1)

    def step(self, ev):
        t, xo, yo, j, a = ev
        chip, shard = self.pc.src(xo, yo, j)
        b = self.block(t, shard)
        pltpu.make_async_remote_copy(b, b, self.send.at[1], self.recv.at[t, chip], device_id=self.pc.dev("X"), device_id_type=MESH).wait_recv()
        self.forward(t, xo, yo, j, a)

    def all_here(self):
        b = self.buf.at[pl.ds(0, 16 * CH), pl.ds(0, self.width)]
        pltpu.make_async_remote_copy(b, b, self.send.at[0], self.crecv, device_id=self.pc.dev("C"), device_id_type=MESH).wait_recv()


class Landing:
    def __init__(self, trees):
        self.off, self.n, self.sem = {}, 0, {}
        for t, (perm, _, n) in enumerate(trees):
            for k in "XY":
                a = perm.index(k)
                other = "Y" if k == "X" else "X"
                for j in range(4):
                    for o in range(2):
                        if (j and perm.index("Z") > a) or (o and perm.index(other) > a):
                            continue
                        self.add((t, k, j, o), n)
            a = perm.index("Z")
            for xo in range(2):
                for yo in range(2):
                    if (xo and perm.index("X") > a) or (yo and perm.index("Y") > a):
                        continue
                    for s in range(5):
                        self.add((t, "Z", xo, yo, s), n)

    def add(self, key, n):
        if self.n < SPLIT < self.n + n:
            self.n = SPLIT
        self.off[key] = self.n
        self.n += n
        self.sem[key] = len(self.sem)


LANDS = {trees: Landing(trees) for trees in (FEW, ALSO)}
LAND_SEMS = max(len(v.sem) for v in LANDS.values())


class Reduce:
    def __init__(self, pc, group, buf, land, cland, recv, crecv, send, done):
        self.pc, self.buf, self.land, self.cland, self.recv, self.crecv, self.send, self.done = pc, buf, land, cland, recv, crecv, send, done
        self.base, self.col, self.width, self.trees = GROUPS[group]
        self.places = LANDS[self.trees]
        self.cdone = set()
        self.traffic = Traffic(pc, buf, send, crecv.at[0], self.width)

    def rows(self, off, n):
        return self.buf.at[pl.ds(pl.multiple_of(self.base + off, 16), n), pl.ds(self.col, self.width)]

    def block(self, t, shard):
        _, r0, n = self.trees[t]
        return self.rows(shard * CH + r0, n)

    def cslot(self, xo, yo, j):
        return (j * 2 + yo) * 2 + xo

    def csend(self, offsets):
        pc = self.pc
        for xo, yo, j in offsets:
            _, shard = pc.src(xo, yo, j)
            s = self.cslot(xo, yo, j)
            pltpu.make_async_remote_copy(
                self.rows((shard + 2 - 4 * pc.c) * CH, CH), self.cland(s * CH, CH),
                self.send.at[0], self.crecv.at[s], device_id=pc.dev("C"), device_id_type=MESH).start()
            self.traffic.note("C", CH)

    def arrive(self, key):
        r = self.land(self.places.off[key], self.trees[key[0]][2])
        pltpu.make_async_remote_copy(r, r, self.send.at[1], self.recv.at[self.places.sem[key]], device_id=self.pc.dev("X"), device_id_type=MESH).wait_recv()
        return r[...].astype(F32)

    def total(self, t, xo, yo, j, last):
        pc = self.pc
        perm, r0, n = self.trees[t]
        _, shard = pc.src(xo, yo, j)
        b = self.block(t, shard)
        s = self.cslot(xo, yo, j)
        if s not in self.cdone:
            self.cdone.add(s)
            r = self.cland(s * CH, CH)
            pltpu.make_async_remote_copy(r, r, self.send.at[0], self.crecv.at[s], device_id=pc.dev("C"), device_id_type=MESH).wait_recv()
        acc = b[...].astype(F32) + self.cland(s * CH + r0, n)[...].astype(F32)
        for k in "XY":
            if k in perm[last + 1 :]:
                acc = acc + self.arrive((t, k, j, yo if k == "X" else xo))
        middle = None
        if perm.index("Z") >= last:
            if j == 0:
                acc = acc + self.arrive((t, "Z", xo, yo, 0))
            middle = (t, "Z", xo, yo, 1 if j == 0 else 1 + j)
        return acc, b, middle

    def own(self):
        for t, (_, r0, n) in enumerate(self.trees):
            acc, _, middle = self.total(t, 0, 0, 0, -1)
            dst = self.done.at[pl.ds(r0, n), pl.ds(self.col, self.width)]
            dst[...] = acc

            @pl.when(self.pc.mid == 1)
            def _():
                dst[...] = dst[...] + self.arrive(middle)

    def step(self, ev):
        pc = self.pc
        t, xo, yo, j, a = ev
        perm, _, n = self.trees[t]
        acc, b, middle = self.total(t, xo, yo, j, a)
        b[...] = acc.astype(BF16)
        if middle is not None:
            @pl.when(pc.mid == 1)
            def _():
                b[...] = (b[...].astype(F32) + self.arrive(middle)).astype(BF16)

        def go(key, k):
            pltpu.make_async_remote_copy(b, self.land(self.places.off[key], n), self.send.at[LINK[k]], self.recv.at[self.places.sem[key]],
                                         device_id=pc.dev(k), device_id_type=MESH).start()

        k = perm[a]
        if k in "XY":
            go((t, k, j, yo if k == "X" else xo), k)
            self.traffic.note(k, n)
        elif j == 1:
            go((t, "Z", xo, yo, 0), "P")
            self.traffic.note("P", n, "end")
            self.traffic.note("P", n, "mid")
        else:
            @pl.when(pc.mid == 0)
            def _():
                go((t, "Z", xo, yo, 1 + j), "P")

            @pl.when(pc.mid == 1)
            def _():
                go((t, "Z", xo, yo, j - 1), "Q")

            self.traffic.note("P", n, "end")
            self.traffic.note("Q", n, "mid")


class SmallSum:
    def __init__(self, pc, total, out, arrived, send, recv):
        self.pc, self.total, self.out, self.arrived, self.send, self.recv = pc, total, out, arrived, send, recv

    def copy(self, k):
        return pltpu.make_async_remote_copy(self.out.at[k], self.arrived.at[k], self.send.at[k], self.recv.at[k],
                                            device_id=self.pc.dev(VSTEPS[k]), device_id_type=MESH)

    def step(self, k):
        if k:
            self.copy(k - 1).wait_recv()
            self.total[...] = self.total[...] + self.arrived[k - 1]
        if k < 5:
            self.out[k] = self.total[...]
            self.copy(k).start()

    def finish(self):
        for k in range(5):
            self.copy(k).wait_send()


class PlaneSum:
    def __init__(self, pc, parts, total, one, two, send, recv):
        self.pc, self.parts, self.total, self.one, self.two, self.send, self.recv = pc, parts, total, one, two, send, recv

    def copy(self, k):
        pc = self.pc
        if k < 7:
            kind = PLANE[k]
            y = 1 - pc.y if "Y" in kind else pc.y
            c = 1 - pc.c if "C" in kind else pc.c
            x = 1 - pc.x if "X" in kind else pc.x
            src, dst = self.parts.at[y * 4 + c * 2 + x], self.one.at[k]
        else:
            kind, src, dst = ZPARTNERS[k - 7], self.total.at[0], self.two.at[k - 7]
        return pltpu.make_async_remote_copy(src, dst, self.send.at[k], self.recv.at[k], device_id=pc.dev(kind), device_id_type=MESH)

    def step(self, k):
        pc = self.pc
        if k == 0:
            for i in range(7):
                self.copy(i).start()
        if k == 1:
            acc = self.parts[pc.y * 4 + pc.c * 2 + pc.x]
            for i in range(7):
                self.copy(i).wait_recv()
                acc = acc + self.one[i]
            self.total[0] = acc
            for i in range(7, 10):
                self.copy(i).start()
        if k == 2:
            acc = self.total[0]
            for i in range(3):
                self.copy(7 + i).wait_recv()
                acc = acc + self.two[i]
            self.total[1] = acc

    def finish(self):
        for k in range(10):
            self.copy(k).wait_send()


def lane(rows, columns, axis):
    return lax.broadcasted_iota(jnp.int32, (rows, columns), axis)


def group24(d):
    return lax.shift_right_logical(d * 2731, 16)


def group96(f):
    return lax.shift_right_logical(f * 683, 16)


def unpack_small(total, vecs):
    v = total[...].astype(BF16)
    d = lane(256, D, 1)
    mine = group24(lane(SH, D, 1)) == lane(SH, D, 0)
    for k in range(6):
        pick = jnp.where(lane(256, D, 0) == 24 * k + d - 24 * group24(d), 1.0, 0.0).astype(BF16)
        vecs[k : k + 1, 0:D] = jnp.sum(jnp.where(mine, dot(v, pick), 0.0), axis=0, keepdims=True)
    pick = jnp.where(lane(256, D, 0) == 144 + d - 96 * group96(d), 1.0, 0.0).astype(BF16)
    wide = dot(v, pick)
    for j in range(4):
        mine = group96(lane(SH, D, 1)) + 8 * j == lane(SH, D, 0)
        vecs[6:7, D * j : D * j + D] = jnp.sum(jnp.where(mine, wide, 0.0), axis=0, keepdims=True)


def pick_dot(a, ones):
    out = None
    for _ in range(3):
        part = a.astype(BF16)
        a = a - part.astype(F32)
        out = dot(part, ones) if out is None else out + dot(part, ones)
    return out


def pack_small(vterm, parts):
    d = lane(D, 128, 0)
    row = lane(64, D, 0)
    shard = (row & 7) * 8 + lax.shift_right_logical(row, 3)
    owner = group24(lane(64, D, 1))
    place = jnp.where(lane(D, 128, 1) == d - 24 * group24(d), 1.0, 0.0).astype(BF16)
    rows = jnp.concatenate([jnp.where(owner == shard, vterm[k : k + 1, 0:D], 0.0) for k in range(6)], axis=0)
    cut = pick_dot(rows, place)
    place = jnp.where(lane(D, 128, 1) == d - 96 * group96(d), 1.0, 0.0).astype(BF16)
    owner = group96(lane(64, D, 1))
    rows = jnp.where(owner == shard, vterm[6:7, 0:D], 0.0)
    for j in range(1, 4):
        rows = rows + jnp.where(owner + 8 * j == shard, vterm[6:7, D * j : D * j + D], 0.0)
    last = pick_dot(rows, place)
    blank = jnp.zeros((64, 128), F32)
    out = jnp.zeros((64, 256), F32)
    for k in range(7):
        wide = jnp.concatenate([cut[64 * k : 64 * k + 64, :] if k < 6 else last, blank], axis=1)
        out = out + (pltpu.roll(wide, 24 * k, 1) if k else wide)
    for k in range(8):
        parts[k] = out[8 * k : 8 * k + 8, :]


SCRATCH = dict(
    G=((PHASES * SH * CH, D), BF16), w0=((SH * CH, D), BF16), w1=((SH * CH, D), BF16), cl2=((16 * CH, D), BF16),
    land12=((LANDS[GROUPS[0][3]].n + LANDS[GROUPS[1][3]].n, D), BF16), act_=((4 * ROWS, D), BF16), gp_=((4 * ROWS, D), BF16), proj_=((3 * ROWS, D), BF16),
    hidden=((ROWS, D), F32), tmp=((ROWS, D), F32), chosen=((ROWS, D), BF16), picked=((ROWS, D), BF16), normed=((ROWS, D), BF16),
    feed=((ROWS, D), BF16), delta=((ROWS, D), BF16), attended=((ROWS, D), BF16), normed_two=((ROWS, D), BF16), attn_grad=((ROWS, D), BF16),
    trans=((D, ROWS), BF16), lse=((2, CAP, 128), F32), lse_row=((2, 16, CAP), F32), stats=((ROWS, 128), F32), tok=((LONG, 2, D), BF16), ct=((LONG, 2, D), BF16), vecs=((8, 4 * D), F32), vterm=((8, 4 * D), F32),
    obuf=((PHASES * CH, D), F32), vtotal=((SH, 256), F32), vout=((5, SH, 256), F32), varr=((5, SH, 256), F32),
    pparts=((8, 8, 256), F32), ptotal=((2, 8, 256), F32), pone=((7, 8, 256), F32), ptwo=((3, 8, 256), F32),
)
SEMS = dict(lsem=(2,), osem=(11,), arecv=(len(AGROUPS), 2, 16), acrecv=(len(AGROUPS),), asend=(len(AGROUPS), 5), rrecv=(len(GROUPS), LAND_SEMS),
            rcrecv=(len(GROUPS), 16), rsend=(len(GROUPS), 5), vsend=(5,), vrecv=(5,), psend=(10,), precv=(10,))
INS = ("sel", "lens", "v0", "v1", "v2", "v3", "v4", "v5", "v6", "qkv_w", "out_w", "up_w", "down_w", "tok_h", "ct_h")
OUTS = ("out_h", "ing_h", "small", "gqkv_h", "gout_h", "gup_h", "gdown_h")


def compute_order():
    out = []

    def tiles(*names):
        out.extend(("tile", name) for name in names)

    def grid(stem, *counts):
        tiles(*[stem + "".join(map(str, at)) for at in itertools.product(*[range(n) for n in counts])])

    grid("pick", 2)
    grid("norm", 6)
    for n in range(3):
        if n == 0:
            out.append(("pd", 0))
        tiles(f"relay0_{n}", *[f"qkv{j}{n}" for j in range(3)])
        tiles(*[f"attn{i}{h}" for h in (2 * n, 2 * n + 1) for i in range(2)])
    grid("out", 3)
    grid("norm2", 6)
    out.append(("pd", 1))
    grid("relay1_", 4)
    grid("up", 4, 3)
    grid("gdown", 4, 3)
    out.append(("csend", 0))
    tiles("bdown")
    out.append(("pd", 2))
    grid("gact", 4, 3)
    grid("down", 3)
    out.extend([("agfin",), ("free",)])
    tiles("tn2")
    grid("gup", 2, 3)
    out.append(("csend", 1))
    grid("gn2", 3)
    grid("ln2b", 6)
    grid("gatt", 3)
    tiles("tn1")
    out.append(("wfree",))
    for n in range(3):
        tiles(*[f"attb{i}{h}" for h in (2 * n, 2 * n + 1) for i in range(2)])
        tiles(f"gqk{n}", f"gvo{n}")
        out.append(("csend", 2 + n))
    grid("gate", 6)
    grid("gn1", 3)
    grid("ln1b", 6)
    tiles("vecpack")
    out.extend(("vstep", 1, k) for k in range(2))
    return out


def catalogue():
    items = [("ag", g, e) for g, group in enumerate(AGROUPS) for e in all_events(group[3])]
    items += [("own", g) for g in range(len(AGROUPS))]
    items += [("rs", g, e) for g, group in enumerate(GROUPS) for e in all_events(group[3])]
    items += [("rsown", g) for g in range(len(GROUPS))]
    items += [("vstep", 0, k) for k in range(5)]
    return items + compute_order() + [("tile", stem + str(n)) for stem in ("output", "ingrad") for n in range(3)]


def mega_kernel(names, order, *refs):
    fields = INS + OUTS + tuple(SCRATCH) + tuple(SEMS) + ("free_c", "free_all")
    R = types.SimpleNamespace(**dict(zip(fields, refs)))
    pc = Place()
    loads = [pltpu.make_async_copy(R.tok_h, R.tok, R.lsem.at[0]), pltpu.make_async_copy(R.ct_h, R.ct, R.lsem.at[1])]
    for cp in loads:
        cp.start()
    barrier = pltpu.get_barrier_semaphore()
    pc.signal(barrier, PLANE + ("P", "W", "V", "Q"))
    for p in range(PHASES):
        if p == 0:
            v = jnp.concatenate([R.qkv_w[:, D * j : D * j + D].astype(F32) for j in range(3)] + [R.out_w[...].astype(F32)], axis=0).astype(BF16)
        elif p == 1:
            v = jnp.concatenate([R.up_w[:, D * j : D * j + D].astype(F32) for j in range(4)], axis=0).astype(BF16)
        else:
            v = R.down_w[...]
        R.G[pl.ds(pl.multiple_of((p * SH + pc.me) * CH, 16), CH), :] = v
    vrow = jnp.concatenate([v[...].astype(F32) for v in (R.v0, R.v1, R.v2, R.v3, R.v4, R.v5, R.v6)] + [jnp.zeros((1, 16), F32)], axis=1)
    R.vtotal[...] = jnp.where(lane(SH, 256, 0) == pc.me, vrow, 0.0)
    pl.semaphore_wait(barrier, 10 + pc.mid)

    ag = [Gather(pc, g, R.G, R.arecv.at[g], R.acrecv.at[g], R.asend.at[g]) for g in range(len(AGROUPS))]

    def landing(g):
        def land(off, n):
            if g < 2:
                return R.land12.at[pl.ds(g * LANDS[GROUPS[0][3]].n + off, n), :]
            cs = pl.ds(GROUPS[g][1], GROUPS[g][2])
            if off < SPLIT:
                return R.w1.at[pl.ds(SPLIT + off, n), cs]
            return R.act_.at[pl.ds(off, n), cs]

        def cland(off, n):
            ref = (R.cl2, R.act_, R.w1)[min(g, 2)]
            return ref.at[pl.ds(off, n), pl.ds(GROUPS[g][1], GROUPS[g][2])]

        return land, cland

    owned = [R.obuf.at[pl.ds(CH * (2 - min(g, 2)), CH), :] for g in range(len(GROUPS))]
    rs = [Reduce(pc, g, R.G, *landing(g), R.rrecv.at[g], R.rcrecv.at[g], R.rsend.at[g], owned[g]) for g in range(len(GROUPS))]
    sums = [SmallSum(pc, R.vtotal, R.vout, R.varr, R.vsend, R.vrecv), PlaneSum(pc, R.pparts, R.ptotal, R.pone, R.ptwo, R.psend, R.precv)]

    R.VEC = {name: (k, D) for name, k in ROW.items()}
    R.VEC["up_bias"] = (ROW["up_bias"], 4 * D)

    def vec(name, off=0, n=None):
        r, w = R.VEC[name]
        return R.vecs[r : r + 1, off : off + (n or w)]

    def view(ref, rows):
        return lambda j: ref.at[pl.ds(rows * j, rows), :]

    R.vec = vec
    R.act, R.gp, R.proj, R.dproj = view(R.act_, ROWS), view(R.gp_, ROWS), view(R.proj_, ROWS), view(R.gp_, ROWS)
    R.W0, R.W1 = view(R.w0, D), view(R.w1, D)
    R.W2 = lambda j: R.G.at[pl.ds(2 * SH * CH + D * j, D), :]
    R.part = lambda p: R.G.at[pl.ds(GROUPS[2 - p][0], SH * CH), :]
    R.change = R.datt = R.feed
    stores = []

    def store(src, dst):
        cp = pltpu.make_async_copy(src, dst, R.osem.at[len(stores)])
        cp.start()
        stores.append(cp)

    def output(n, cs, v):
        R.tok[:, :, cs] = v
        if n == 2:
            store(R.tok, R.out_h)

    def input_grad(n, cs, v):
        R.ct[:, :, cs] = v
        if n == 2:
            store(R.ct, R.ing_h)

    R.output, R.input_grad = output, input_grad
    tiles = {name: f for name, _, _, f in fwd_tiles(R) + bwd_tiles(R)}
    program = [names[k] for k in order]
    offsets = {}
    for it in program:
        if it[0] in ("rs", "rsown"):
            o = it[2][1:4] if it[0] == "rs" else (0, 0, 0)
            if o not in offsets.setdefault(it[1], []):
                offsets[it[1]].append(o)
    finished = set()
    for it in program:
        kind = it[0]
        if kind == "ag":
            ag[it[1]].step(it[2])
        elif kind == "own":
            ag[it[1]].own()
        elif kind == "pd":
            ag[it[1]].all_here()
        elif kind == "rs":
            rs[it[1]].step(it[2])
        elif kind == "rsown":
            g = it[1]
            rs[g].own()
            finished.add(g)
            if g == 0:
                store(owned[g], R.gdown_h)
            elif g == 1:
                for j in range(4):
                    store(owned[g].at[pl.ds(24 * j, 24), :], R.gup_h.at[:, pl.ds(D * j, D)])
            elif finished >= {2, 3, 4}:
                for j in range(3):
                    store(owned[g].at[pl.ds(24 * j, 24), :], R.gqkv_h.at[:, pl.ds(D * j, D)])
                store(owned[g].at[pl.ds(72, 24), :], R.gout_h)
        elif kind == "free":
            pc.signal(R.free_c, "C")
        elif kind == "vstep":
            sums[it[1]].step(it[2])
        elif kind == "csend":
            g = it[1]
            if g == 1:
                pl.semaphore_wait(R.free_c, 1)
            if g == 2:
                pl.semaphore_wait(R.free_all, 4 + pc.mid)
            rs[g].csend(offsets[g])
        elif kind == "tile":
            name = it[1]
            if name == "pick0":
                for cp in loads:
                    cp.wait()
            if name == "norm0":
                sums[0].step(5)
                unpack_small(R.vtotal, R.vecs)
            if name == "vecpack":
                pack_small(R.vterm, R.pparts)
            else:
                if name == "gdown00":
                    ag[1].traffic.wait()
                if name == "gup00":
                    ag[0].traffic.wait()
                if name == "gqk0":
                    ag[2].traffic.wait()
                tiles[name]()
            if name == "gn22":
                pc.signal(R.free_all, "CXYPQ")
    sums[1].step(2)
    R.small[...] = R.ptotal[1, pl.ds(pc.z, 1), :]
    for r in rs:
        r.traffic.wait()
    for s in sums:
        s.finish()
    for cp in stores:
        cp.wait()


def mega(names, order, *args):
    S = jax.ShapeDtypeStruct
    V, H = pl.BlockSpec(memory_space=pltpu.VMEM), pl.BlockSpec(memory_space=pl.ANY)
    outs = [S((LONG, 2, D), BF16), S((LONG, 2, D), BF16), S((1, 256), F32), S((24, 3 * D), F32), S((24, D), F32), S((24, 4 * D), F32), S((96, D), F32)]
    return pl.pallas_call(
        functools.partial(mega_kernel, names, order), out_shape=outs, in_specs=[V] * 13 + [H, H],
        out_specs=[H, H, V, H, H, H, H],
        scratch_shapes=[pltpu.VMEM(*s) for s in SCRATCH.values()] + [pltpu.SemaphoreType.DMA(s) for s in SEMS.values()] + [pltpu.SemaphoreType.REGULAR] * 2,
        compiler_params=pltpu.CompilerParams(collective_id=0, has_side_effects=True, vmem_limit_bytes=VMEM_LIMIT),
        cost_estimate=pl.CostEstimate(flops=26_000_000_000, bytes_accessed=12_000_000, transcendentals=6_000_000),
    )(*args)


def hand_on_kernel(*refs):
    small, srcs, outs, bufs, sems = refs[0], refs[1:7], refs[7:20], refs[20:26], refs[26]
    steps = []
    for k, (src, dst, buf) in enumerate(zip(srcs, outs, bufs)):
        for part in range(4 if k < 2 else 1):
            cut = (lambda r: r.at[pl.ds(145 * part, 145 if part < 3 else LONG - 435)]) if k < 2 else (lambda r: r)
            n = len(steps)
            there = pltpu.make_async_copy(cut(src), cut(buf), sems.at[0, n])
            there.start()
            steps.append((there, pltpu.make_async_copy(cut(buf), cut(dst), sems.at[1, n])))
    for k in range(7):
        outs[6 + k][...] = small[:, 24 * k : 24 * k + (24 if k < 6 else 96)]
    for there, back in steps:
        there.wait()
        back.start()
    for _, back in steps:
        back.wait()


def hand_on(small, *arrays):
    V, H = pl.BlockSpec(memory_space=pltpu.VMEM), pl.BlockSpec(memory_space=pl.ANY)
    outs = [jax.ShapeDtypeStruct(a.shape, a.dtype) for a in arrays]
    outs += [jax.ShapeDtypeStruct((1, 24 if k < 6 else 96), F32) for k in range(7)]
    return pl.pallas_call(hand_on_kernel, out_shape=outs, in_specs=[V] + [H] * 6, out_specs=[H] * 6 + [V] * 7,
                          scratch_shapes=[pltpu.VMEM(a.shape, a.dtype) for a in arrays] + [pltpu.SemaphoreType.DMA((2, 12))],
                          compiler_params=pltpu.CompilerParams(vmem_limit_bytes=VMEM_LIMIT))(small, *arrays)


ORDER = (
    90, 91, 253, 0, 1, 15, 16, 248, 3, 48, 18, 249, 17, 2, 5, 4, 30, 45, 250, 26, 254, 19, 20, 251,
    13, 23, 6, 52, 252, 33, 21, 24, 7, 22, 255, 10, 46, 37, 27, 256, 28, 11, 8, 25, 257, 9, 32, 53,
    14, 258, 259, 260, 12, 29, 325, 31, 92, 49, 54, 261, 262, 263, 264, 265, 266, 267, 268, 269, 270, 271, 272, 47,
    35, 43, 36, 34, 50, 41, 39, 60, 273, 274, 275, 276, 63, 277, 278, 51, 64, 75, 61, 279, 280, 281, 282, 283,
    284, 44, 67, 58, 57, 78, 56, 285, 62, 76, 55, 42, 59, 40, 79, 38, 286, 287, 288, 289, 290, 291, 292, 293,
    294, 82, 71, 86, 295, 65, 296, 297, 298, 299, 300, 66, 77, 301, 302, 303, 304, 305, 306, 307, 80, 308, 309, 310,
    311, 312, 313, 88, 68, 84, 87, 81, 83, 314, 315, 316, 317, 318, 319, 320, 321, 322, 89, 73, 74, 69, 72, 85,
    70, 323, 324, 326, 327, 328, 329, 330, 331, 332, 333, 334, 335, 336, 337, 338, 339, 340, 341, 106, 107, 122, 118, 342,
    103, 119, 120, 117, 343, 104, 101, 344, 345, 346, 352, 347, 348, 353, 349, 350, 99, 121, 116, 351, 97, 105, 115, 102,
    354, 355, 356, 357, 358, 359, 360, 361, 362, 363, 364, 113, 95, 133, 365, 149, 114, 136, 366, 367, 368, 369, 370, 371,
    109, 147, 98, 137, 146, 150, 372, 131, 152, 112, 132, 128, 373, 374, 110, 93, 375, 376, 377, 378, 111, 129, 379, 100,
    96, 380, 94, 108, 180, 124, 148, 208, 206, 196, 135, 165, 212, 134, 182, 381, 382, 383, 384, 385, 144, 197, 193, 195,
    190, 211, 151, 210, 167, 173, 386, 126, 393, 394, 238, 141, 243, 236, 227, 223, 225, 189, 242, 161, 164, 241, 143, 178,
    163, 179, 204, 125, 240, 177, 162, 202, 140, 203, 239, 207, 181, 222, 387, 388, 395, 389, 390, 391, 392, 396, 397, 398,
    399, 400, 401, 402, 187, 221, 185, 224, 218, 142, 174, 192, 234, 191, 159, 226, 219, 166, 209, 403, 237, 200, 232, 176,
    233, 127, 139, 217, 194, 145, 408, 409, 405, 198, 183, 130, 186, 188, 215, 158, 230, 157, 172, 123, 220, 155, 170, 138,
    404, 235, 214, 406, 213, 199, 231, 205, 156, 184, 169, 201, 229, 154, 228, 171, 153, 216, 160, 168, 175, 407, 410, 244,
    246, 247, 245,
)

VMEM_LIMIT = 63 << 20


def on_device_fast(tokens, lengths, selected, cotangent, attn_gain, attn_shift, mlp_gain, mlp_shift, router_weight,
                   qkv_weight, out_weight, up_weight, up_bias, down_weight, down_bias):
    vectors = [v[None] for v in (attn_gain, attn_shift, mlp_gain, mlp_shift, router_weight, down_bias, up_bias)]
    results = mega(catalogue(), ORDER, selected, lengths.T, *vectors, qkv_weight, out_weight, up_weight, down_weight,
                   tokens[:, 0].transpose(1, 0, 2), cotangent[:, 0].transpose(1, 0, 2))
    output, token_grad, owned, gqkv, gout, gup, gdown = results
    output, token_grad, gqkv, gout, gup, gdown, *t = hand_on(owned, output, token_grad, gqkv, gout, gup, gdown)
    t = [v[0] for v in t]
    whole = lambda v: v.transpose(1, 0, 2)[:, None]
    return (whole(output), whole(token_grad), t[0], t[1], t[2], t[3], t[4], gqkv, gout, gup, t[6], gdown, t[5])


HEADS = 12
HEAD_DIM = 64
MICRO = 2


epsilon = 1e-06


def normalize(inputs, norm_gain, norm_shift):
    centered = inputs - jnp.mean(inputs, axis=-1, keepdims=True)
    variance = jnp.mean(centered * centered, axis=-1, keepdims=True)
    return centered * lax.rsqrt(variance + epsilon) * norm_gain + norm_shift


def forward_pass(tokens, lengths, selected, weights):
    (
        attn_gain,
        attn_shift,
        mlp_gain,
        mlp_shift,
        router_weight,
        qkv_weight,
        out_weight,
        up_weight,
        up_bias,
        down_weight,
        down_bias,
    ) = weights
    group_size, capacity = selected.shape
    counts = lengths // 2
    live_mask = (jnp.arange(capacity)[None, :] < counts[:, None]).astype(jnp.float32)
    chosen = jnp.take_along_axis(tokens, selected[:, :, None], axis=1)
    chosen_wide = chosen.astype(jnp.float32)
    logits = jnp.einsum("bcd,d->bc", chosen, router_weight, preferred_element_type=jnp.float32)
    router_gate = jax.nn.sigmoid(logits)
    normed = normalize(
        chosen_wide, attn_gain.astype(jnp.float32), attn_shift.astype(jnp.float32)
    ).astype(jnp.bfloat16)
    projected = jnp.einsum(
        "bcd,de->bce", normed, qkv_weight, preferred_element_type=jnp.float32
    ).astype(jnp.bfloat16)
    projected = projected.reshape(group_size, capacity, 3, HEADS, HEAD_DIM)
    queries = projected[:, :, 0]
    key_rows = projected[:, :, 1]
    value_rows = projected[:, :, 2]
    score_scale = HEAD_DIM ** (-0.5)
    scores = (
        jnp.einsum("bqhe,bkhe->bhqk", queries, key_rows, preferred_element_type=jnp.float32)
        * score_scale
    )
    scores = jnp.where(live_mask[:, None, None, :] > 0, scores, -1000000000.0)
    row_max = jnp.max(scores, axis=-1, keepdims=True)
    exponent = jnp.exp(scores - row_max)
    row_total = jnp.sum(exponent, axis=-1, keepdims=True)
    attention = (exponent / row_total).astype(jnp.bfloat16)
    log_total = row_max + jnp.log(row_total)
    attended = jnp.einsum(
        "bhqk,bkhe->bqhe", attention, value_rows, preferred_element_type=jnp.float32
    ).astype(jnp.bfloat16)
    attended = attended.reshape(group_size, capacity, HEADS * HEAD_DIM)
    attn_out = jnp.einsum("bce,ed->bcd", attended, out_weight, preferred_element_type=jnp.float32)
    hidden = chosen_wide + attn_out
    normed_two = normalize(
        hidden, mlp_gain.astype(jnp.float32), mlp_shift.astype(jnp.float32)
    ).astype(jnp.bfloat16)
    upward = jnp.einsum(
        "bcd,df->bcf", normed_two, up_weight, preferred_element_type=jnp.float32
    ) + up_bias.astype(jnp.float32)
    active = jax.nn.gelu(upward).astype(jnp.bfloat16)
    feed_out = jnp.einsum(
        "bcf,fd->bcd", active, down_weight, preferred_element_type=jnp.float32
    ) + down_bias.astype(jnp.float32)
    change = (attn_out + feed_out) * (router_gate * live_mask)[:, :, None]
    image_rows = jnp.arange(group_size)[:, None]
    output = tokens.astype(jnp.float32).at[image_rows, selected].add(change).astype(jnp.bfloat16)
    kept_values = (
        chosen_wide,
        live_mask,
        router_gate,
        normed,
        projected,
        log_total,
        attended,
        attn_out,
        hidden,
        normed_two,
        upward,
        active,
        feed_out,
    )
    return (output, kept_values)


def backward_pass(cotangent, selected, weights, kept_values):
    (
        attn_gain,
        attn_shift,
        mlp_gain,
        mlp_shift,
        router_weight,
        qkv_weight,
        out_weight,
        up_weight,
        up_bias,
        down_weight,
        down_bias,
    ) = weights
    (
        chosen_wide,
        live_mask,
        router_gate,
        normed,
        projected,
        log_total,
        attended,
        attn_out,
        hidden,
        normed_two,
        upward,
        active,
        feed_out,
    ) = kept_values
    group_size, capacity = selected.shape
    out_grad = cotangent.astype(jnp.float32)
    picked = jnp.take_along_axis(out_grad, selected[:, :, None], axis=1) * live_mask[:, :, None]
    gate_grad = jnp.sum(picked * (attn_out + feed_out), axis=-1)
    logit_grad = gate_grad * router_gate * (1.0 - router_gate)
    change_grad = picked * router_gate[:, :, None]
    feed_grad = change_grad.astype(jnp.bfloat16)
    down_bias_grad = jnp.sum(feed_grad.astype(jnp.float32), axis=(0, 1))
    down_weight_grad = jnp.einsum(
        "bcf,bcd->fd", active, feed_grad, preferred_element_type=jnp.float32
    )
    active_grad = jnp.einsum(
        "bcd,fd->bcf", feed_grad, down_weight, preferred_element_type=jnp.float32
    )
    primal_out, gelu_back = jax.vjp(jax.nn.gelu, upward)
    upward_grad = gelu_back(active_grad)[0].astype(jnp.bfloat16)
    up_bias_grad = jnp.sum(upward_grad.astype(jnp.float32), axis=(0, 1))
    up_weight_grad = jnp.einsum(
        "bcd,bcf->df", normed_two, upward_grad, preferred_element_type=jnp.float32
    )
    normed_two_grad = jnp.einsum(
        "bcf,df->bcd", upward_grad, up_weight, preferred_element_type=jnp.float32
    )
    primal_two, norm_back = jax.vjp(
        normalize, hidden, mlp_gain.astype(jnp.float32), mlp_shift.astype(jnp.float32)
    )
    hidden_grad, mlp_gain_grad, mlp_shift_grad = norm_back(normed_two_grad)
    attn_grad = (change_grad + hidden_grad).astype(jnp.bfloat16)
    out_weight_grad = jnp.einsum(
        "bce,bcd->ed", attended, attn_grad, preferred_element_type=jnp.float32
    )
    attended_grad = jnp.einsum(
        "bcd,ed->bce", attn_grad, out_weight, preferred_element_type=jnp.float32
    ).astype(jnp.bfloat16)
    attended_grad = attended_grad.reshape(group_size, capacity, HEADS, HEAD_DIM)
    queries = projected[:, :, 0]
    key_rows = projected[:, :, 1]
    value_rows = projected[:, :, 2]
    score_scale = HEAD_DIM ** (-0.5)
    key_live = live_mask[:, None, None, :] > 0
    scores = (
        jnp.einsum("bqhe,bkhe->bhqk", queries, key_rows, preferred_element_type=jnp.float32)
        * score_scale
    )
    scores = jnp.where(key_live, scores, -1000000000.0)
    prob_wide = jnp.exp(scores - log_total)
    prob_low = prob_wide.astype(jnp.bfloat16)
    value_grad = jnp.einsum(
        "bhqk,bqhe->bkhe", prob_low, attended_grad, preferred_element_type=jnp.float32
    )
    prob_grad = jnp.einsum(
        "bqhe,bkhe->bhqk", attended_grad, value_rows, preferred_element_type=jnp.float32
    )
    score_grad = prob_wide * (prob_grad - jnp.sum(prob_wide * prob_grad, axis=-1, keepdims=True))
    score_grad = jnp.where(key_live, score_grad.astype(jnp.bfloat16), 0.0) * score_scale
    query_grad = jnp.einsum(
        "bhqk,bkhe->bqhe", score_grad, key_rows, preferred_element_type=jnp.float32
    )
    key_grad = jnp.einsum(
        "bhqk,bqhe->bkhe", score_grad, queries, preferred_element_type=jnp.float32
    )
    projected_grad = jnp.stack([query_grad, key_grad, value_grad], axis=2).astype(jnp.bfloat16)
    projected_grad = projected_grad.reshape(group_size, capacity, 3 * HEADS * HEAD_DIM)
    qkv_weight_grad = jnp.einsum(
        "bcd,bce->de", normed, projected_grad, preferred_element_type=jnp.float32
    )
    normed_grad = jnp.einsum(
        "bce,de->bcd", projected_grad, qkv_weight, preferred_element_type=jnp.float32
    )
    primal_one, first_back = jax.vjp(
        normalize, chosen_wide, attn_gain.astype(jnp.float32), attn_shift.astype(jnp.float32)
    )
    chosen_grad, attn_gain_grad, attn_shift_grad = first_back(normed_grad)
    chosen_grad = (
        chosen_grad + hidden_grad + logit_grad[:, :, None] * router_weight.astype(jnp.float32)
    )
    router_weight_grad = jnp.einsum(
        "bc,bcd->d", logit_grad, chosen_wide, precision=lax.Precision.HIGHEST
    )
    image_rows = jnp.arange(group_size)[:, None]
    token_grad = out_grad.at[image_rows, selected].add(chosen_grad).astype(jnp.bfloat16)
    grad_terms = (
        attn_gain_grad,
        attn_shift_grad,
        mlp_gain_grad,
        mlp_shift_grad,
        router_weight_grad,
        qkv_weight_grad,
        out_weight_grad,
        up_weight_grad,
        up_bias_grad,
        down_weight_grad,
        down_bias_grad,
    )
    return (token_grad, grad_terms)


def on_device(
    tokens,
    lengths,
    selected,
    cotangent,
    attn_gain,
    attn_shift,
    mlp_gain,
    mlp_shift,
    router_weight,
    qkv_weight,
    out_weight,
    up_weight,
    up_bias,
    down_weight,
    down_bias,
):
    outputs = []
    token_grads = []
    totals = None
    for micro_step in range(MICRO):
        forward_weights = (
            lax.all_gather(attn_gain, ("dp", "shard"), axis=0, tiled=True),
            lax.all_gather(attn_shift, ("dp", "shard"), axis=0, tiled=True),
            lax.all_gather(mlp_gain, ("dp", "shard"), axis=0, tiled=True),
            lax.all_gather(mlp_shift, ("dp", "shard"), axis=0, tiled=True),
            lax.all_gather(router_weight, ("dp", "shard"), axis=0, tiled=True),
            lax.all_gather(qkv_weight, ("dp", "shard"), axis=0, tiled=True),
            lax.all_gather(out_weight, ("dp", "shard"), axis=0, tiled=True),
            lax.all_gather(up_weight, ("dp", "shard"), axis=0, tiled=True),
            lax.all_gather(up_bias, ("dp", "shard"), axis=0, tiled=True),
            lax.all_gather(down_weight, ("dp", "shard"), axis=0, tiled=True),
            lax.all_gather(down_bias, ("dp", "shard"), axis=0, tiled=True),
        )
        output, kept_values = forward_pass(
            tokens[micro_step], lengths[micro_step], selected[micro_step], forward_weights
        )
        backward_weights = (
            lax.all_gather(attn_gain, ("dp", "shard"), axis=0, tiled=True),
            lax.all_gather(attn_shift, ("dp", "shard"), axis=0, tiled=True),
            lax.all_gather(mlp_gain, ("dp", "shard"), axis=0, tiled=True),
            lax.all_gather(mlp_shift, ("dp", "shard"), axis=0, tiled=True),
            lax.all_gather(router_weight, ("dp", "shard"), axis=0, tiled=True),
            lax.all_gather(qkv_weight, ("dp", "shard"), axis=0, tiled=True),
            lax.all_gather(out_weight, ("dp", "shard"), axis=0, tiled=True),
            lax.all_gather(up_weight, ("dp", "shard"), axis=0, tiled=True),
            lax.all_gather(up_bias, ("dp", "shard"), axis=0, tiled=True),
            lax.all_gather(down_weight, ("dp", "shard"), axis=0, tiled=True),
            lax.all_gather(down_bias, ("dp", "shard"), axis=0, tiled=True),
        )
        token_grad, grad_terms = backward_pass(
            cotangent[micro_step], selected[micro_step], backward_weights, kept_values
        )
        grad_terms = (
            lax.psum_scatter(grad_terms[0], ("dp", "shard"), scatter_dimension=0, tiled=True),
            lax.psum_scatter(grad_terms[1], ("dp", "shard"), scatter_dimension=0, tiled=True),
            lax.psum_scatter(grad_terms[2], ("dp", "shard"), scatter_dimension=0, tiled=True),
            lax.psum_scatter(grad_terms[3], ("dp", "shard"), scatter_dimension=0, tiled=True),
            lax.psum_scatter(grad_terms[4], ("dp", "shard"), scatter_dimension=0, tiled=True),
            lax.psum_scatter(grad_terms[5], ("dp", "shard"), scatter_dimension=0, tiled=True),
            lax.psum_scatter(grad_terms[6], ("dp", "shard"), scatter_dimension=0, tiled=True),
            lax.psum_scatter(grad_terms[7], ("dp", "shard"), scatter_dimension=0, tiled=True),
            lax.psum_scatter(grad_terms[8], ("dp", "shard"), scatter_dimension=0, tiled=True),
            lax.psum_scatter(grad_terms[9], ("dp", "shard"), scatter_dimension=0, tiled=True),
            lax.psum_scatter(grad_terms[10], ("dp", "shard"), scatter_dimension=0, tiled=True),
        )
        totals = grad_terms if totals is None else jax.tree.map(jnp.add, totals, grad_terms)
        outputs.append(output)
        token_grads.append(token_grad)
    return (
        jnp.stack(outputs),
        jnp.stack(token_grads),
        totals[0],
        totals[1],
        totals[2],
        totals[3],
        totals[4],
        totals[5],
        totals[6],
        totals[7],
        totals[8],
        totals[9],
        totals[10],
    )


def solution(mesh):
    fits = dict(mesh.shape) == {"dp": 16, "shard": 2}
    return jax.shard_map(
        on_device_fast if fits else on_device,
        mesh=mesh,
        in_specs=(
            P(None, ("dp", "shard"), None, None),
            P(None, ("dp", "shard")),
            P(None, ("dp", "shard"), None),
            P(None, ("dp", "shard"), None, None),
            P(("dp", "shard")),
            P(("dp", "shard")),
            P(("dp", "shard")),
            P(("dp", "shard")),
            P(("dp", "shard")),
            P(("dp", "shard"), None),
            P(("dp", "shard"), None),
            P(("dp", "shard"), None),
            P(("dp", "shard")),
            P(("dp", "shard"), None),
            P(("dp", "shard")),
        ),
        out_specs=(
            P(None, ("dp", "shard"), None, None),
            P(None, ("dp", "shard"), None, None),
            P(("dp", "shard")),
            P(("dp", "shard")),
            P(("dp", "shard")),
            P(("dp", "shard")),
            P(("dp", "shard")),
            P(("dp", "shard"), None),
            P(("dp", "shard"), None),
            P(("dp", "shard"), None),
            P(("dp", "shard")),
            P(("dp", "shard"), None),
            P(("dp", "shard")),
        ),
        check_vma=False,
    )
```

```python
import functools
import itertools
import math
import types

import jax
import jax.numpy as jnp
from jax import lax
from jax.experimental import pallas as pl
from jax.experimental.pallas import tpu as pltpu
from jax.sharding import PartitionSpec as P

F32, BF16 = jnp.float32, jnp.bfloat16
D, ROWS, CAP, LONG = 768, 576, 288, 577
SH, CH = 32, 96
NN = (((1,), (0,)), ((), ()))
NT = (((1,), (1,)), ((), ()))
TN = (((0,), (0,)), ((), ()))
def dot(a, b, dims=NN):
    return lax.dot_general(a, b, dims, preferred_element_type=F32)
def ln(rows):
    centered = rows - jnp.mean(rows, axis=-1, keepdims=True)
    rstd = lax.rsqrt(jnp.mean(centered * centered, axis=-1, keepdims=True) + 1e-6)
    return centered * rstd, rstd
def spread(R):
    place = lax.broadcasted_iota(jnp.int32, (2 * LONG, ROWS), 0)
    return jnp.where(place == jnp.concatenate([2 * R.sel[0], 2 * R.sel[1] + 1], axis=1), 1.0, 0.0).astype(BF16)
def choose(R, i):
    place = lax.broadcasted_iota(jnp.int32, (CAP, 2 * LONG), 1)
    column = jnp.transpose(jnp.broadcast_to((2 * R.sel[i] + i).astype(F32), (8, CAP)))[:, 0:1].astype(jnp.int32)
    return jnp.where(place == column, 1.0, 0.0).astype(BF16)
def both(ref, cs=slice(None)):
    return ref[:, :, cs].reshape(2 * LONG, -1)
def live_rows(lens, i):
    slot = lax.broadcasted_iota(jnp.int32, (CAP, 1), 0)
    return (slot < lax.shift_right_logical(lens[:, i : i + 1], 1)).astype(F32)
def live_cols(lens, i):
    slot = lax.broadcasted_iota(jnp.int32, (1, CAP), 1)
    return slot < lax.shift_right_logical(lens[:, i : i + 1], 1)
def relayout(G, W, p, lo, hi, cs=slice(None)):
    for k in range(lo, hi):
        two = [G[(p * SH + 2 * k + u) * CH : (p * SH + 2 * k + u + 1) * CH, cs].astype(F32) for u in range(2)]
        for j in range(4):
            W[D * j + 48 * k : D * j + 48 * k + 48, cs] = jnp.concatenate([t[24 * j : 24 * j + 24, :] for t in two], axis=0).astype(BF16)
def fwd_tiles(R):
    T = []
    def add(name, cost, dep):
        def deco(f): T.append((name, cost, dep, f)); return f
        return deco
    for i in range(2):
        sl = slice(CAP * i, CAP * i + CAP)
        @add(f"pick{i}", 1.0, "tok")
        def _(i=i, sl=sl):
            oh = choose(R, i)
            R.chosen[sl, :] = dot(oh, both(R.tok)).astype(BF16)
            R.stats[sl, 1:2] = live_rows(R.lens, i)
            R.picked[sl, :] = (dot(oh, both(R.ct)) * R.stats[sl, 1:2]).astype(BF16)
    B = 96
    for b in range(ROWS // B):
        sl = slice(B * b, B * b + B)
        @add(f"norm{b}", 0.4, "vec")
        def _(sl=sl):
            ch = R.chosen[sl, :].astype(F32)
            xh, _ = ln(ch)
            R.normed[sl, :] = (xh * R.vec("attn_gain") + R.vec("attn_shift")).astype(BF16)
            logit = jnp.sum(ch * R.vec("router_weight"), axis=-1, keepdims=True)
            gate = 1.0 / (1.0 + jnp.exp(-logit))
            R.stats[sl, 0:1] = gate
            feed = (gate * R.picked[sl, :].astype(F32)).astype(BF16)
            R.feed[sl, :] = feed
    for g in range(3):
        @add(f"relay0_{g}", 0.4, 0)
        def _(g=g): relayout(R.G, R.w0, 0, 0, 16, slice(256 * g, 256 * g + 256))
    for j in range(3):
        for n in range(3):
            @add(f"qkv{j}{n}", 0.45, 0)
            def _(j=j, n=n):
                cs = slice(256 * n, 256 * n + 256)
                R.proj(j)[:, cs] = dot(R.normed[...], R.W0(j)[:, cs]).astype(BF16)
    for i in range(2):
        sl = slice(CAP * i, CAP * i + CAP)
        for h in range(6):
            @add(f"attn{i}{h}", 1.0, 0)
            def _(i=i, h=h, sl=sl):
                cs = slice(128 * h, 128 * h + 128)
                q, k, v = R.proj(0)[sl, cs], R.proj(1)[sl, cs], R.proj(2)[sl, cs]
                low = lax.broadcasted_iota(jnp.int32, (CAP, 128), 1) < 64
                lane = lax.broadcasted_iota(jnp.int32, (CAP, 128), 1)
                live = live_cols(R.lens, i)
                zero, ones = jnp.zeros_like(q), jnp.ones_like(q)
                q = q * 0.125
                outs = []
                lse = R.lse[i] if h else jnp.zeros((CAP, 128), F32)
                for u in range(2):
                    qm, vm = (jnp.where(low, q, zero), jnp.where(low, v, ones)) if u == 0 else (jnp.where(low, zero, q), jnp.where(low, ones, v))
                    s = jnp.where(live, dot(qm, k, NT), -1e9)
                    m = jnp.max(s, axis=-1, keepdims=True)
                    o = dot(jnp.exp(s - m).astype(BF16), vm)
                    tot = o[:, 64:65] if u == 0 else o[:, 0:1]
                    outs.append(o * (1.0 / tot))
                    lse = jnp.where(lane == 2 * h + u, m + jnp.log(tot), lse)
                R.lse[i] = lse
                R.attended[sl, cs] = jnp.where(low, outs[0], outs[1]).astype(BF16)
                if h == 5:
                    R.lse_row[i] = jnp.transpose(lse)[:16, :]
    for n in range(3):
        @add(f"out{n}", 0.45, 0)
        def _(n=n):
            cs = slice(256 * n, 256 * n + 256)
            R.hidden[:, cs] = R.chosen[:, cs].astype(F32) + dot(R.attended[...], R.W0(3)[:, cs])
    for b in range(ROWS // B):
        sl = slice(B * b, B * b + B)
        @add(f"norm2{b}", 0.3, 0)
        def _(sl=sl):
            xh, _ = ln(R.hidden[sl, :])
            R.normed_two[sl, :] = (xh * R.vec("mlp_gain") + R.vec("mlp_shift")).astype(BF16)
    for g in range(4):
        @add(f"relay1_{g}", 0.4, 1)
        def _(g=g): relayout(R.G, R.w1, 1, 4 * g, 4 * g + 4)
    c0 = math.sqrt(2.0 / math.pi)
    for j in range(4):
        for n in range(3):
            @add(f"up{j}{n}", 1.2, 1)
            def _(j=j, n=n):
                cs = slice(256 * n, 256 * n + 256)
                u = dot(R.normed_two[...], R.W1(j)[:, cs]) + R.vec("up_bias", D * j + 256 * n, 256)
                uu = u * u
                half = 0.5 * jnp.tanh(u * (c0 + (c0 * 0.044715) * uu)) + 0.5
                a = u * half
                R.act(j)[:, cs] = a.astype(BF16)
                R.gp(j)[:, cs] = (half + a * (1.0 - half) * (2 * c0 + (6 * c0 * 0.044715) * uu)).astype(BF16)
    for n in range(3):
        @add(f"down{n}", 1.6, 2)
        def _(n=n):
            cs = slice(256 * n, 256 * n + 256)
            acc = R.vec("down_bias", 256 * n, 256) + dot(R.act(0)[...], R.W2(0)[:, cs])
            for j in range(1, 4): acc = acc + dot(R.act(j)[...], R.W2(j)[:, cs])
            R.delta[:, cs] = (acc + (R.hidden[:, cs] - R.chosen[:, cs].astype(F32))).astype(BF16)
    for b in range(ROWS // B):
        sl = slice(B * b, B * b + B)
        @add(f"gate{b}", 0.3, 2)
        def _(sl=sl, b=b):
            if b == 0: R.proj_[0 : 2 * LONG, 0:ROWS] = spread(R)
            d = R.delta[sl, :].astype(F32)
            gate = R.stats[sl, 0:1]
            R.stats[sl, 2:3] = jnp.sum(R.picked[sl, :].astype(F32) * d, axis=-1, keepdims=True) * gate * (1.0 - gate)
            R.change[sl, :] = (d * (gate * R.stats[sl, 1:2])).astype(BF16)
    for n in range(3):
        @add(f"output{n}", 1.0, 2)
        def _(n=n):
            cs = slice(256 * n, 256 * n + 256)
            total = both(R.tok, cs).astype(F32) + dot(R.proj_[0 : 2 * LONG, 0:ROWS], R.change[:, cs])
            R.output(n, cs, total.astype(BF16).reshape(LONG, 2, 256))
    return T


def bwd_tiles(R):
    T = []
    def add(name, cost, dep=None):
        def deco(f): T.append((name, cost, dep, f)); return f
        return deco
    def grow(name, v, first, off=0):
        r, w = R.VEC[name]
        n = v.shape[1]
        if first: R.vterm[r : r + 1, off : off + n] = v
        else: R.vterm[r : r + 1, off : off + n] = R.vterm[r : r + 1, off : off + n] + v
    def colsum(v): return jnp.sum(v, axis=0, keepdims=True)
    def put_pair(p, half, cs, one, two):
        for s in range(SH):
            R.part(p)[s * CH + 48 * half : s * CH + 48 * half + 48, cs] = jnp.concatenate(
                [one[24 * s : 24 * s + 24, :], two[24 * s : 24 * s + 24, :]], axis=0).astype(BF16)
    B = 96
    for j in range(4):
        for n in range(3):
            @add(f"gdown{j}{n}", 0.55)
            def _(j=j, n=n):
                cs = slice(256 * n, 256 * n + 256)
                R.part(2)[D * j + 256 * n : D * j + 256 * n + 256, :] = dot(R.act(j)[:, cs], R.feed[...], TN).astype(BF16)
    @add("bdown", 0.2)
    def _():
        grow("down_bias", colsum(R.feed[...].astype(F32)), True)
    for j in range(4):
        for n in range(3):
            @add(f"gact{j}{n}", 0.6)
            def _(j=j, n=n):
                cs = slice(256 * n, 256 * n + 256)
                g = (dot(R.feed[...], R.W2(j)[cs, :], NT) * R.gp(j)[:, cs].astype(F32)).astype(BF16)
                R.gp(j)[:, cs] = g
                grow("up_bias", colsum(g.astype(F32)), True, D * j + 256 * n)
    @add("tn2", 0.6)
    def _(): R.trans[...] = jnp.transpose(R.normed_two[...])
    for h in range(2):
        for n in range(3):
            @add(f"gup{h}{n}", 1.2)
            def _(h=h, n=n):
                cs = slice(256 * n, 256 * n + 256)
                put_pair(1, h, cs, dot(R.trans[...], R.gp(2 * h)[:, cs]), dot(R.trans[...], R.gp(2 * h + 1)[:, cs]))
    for n in range(3):
        @add(f"gn2{n}", 1.6)
        def _(n=n):
            cs = slice(256 * n, 256 * n + 256)
            acc = dot(R.gp(0)[...], R.W1(0)[cs, :], NT)
            for j in range(1, 4): acc = acc + dot(R.gp(j)[...], R.W1(j)[cs, :], NT)
            R.tmp[:, cs] = acc
    for b in range(ROWS // B):
        sl = slice(B * b, B * b + B)
        @add(f"ln2b{b}", 0.5)
        def _(sl=sl, b=b):
            g = R.tmp[sl, :]
            xh, r = ln(R.hidden[sl, :])
            grow("mlp_gain", colsum(g * xh), b == 0)
            grow("mlp_shift", colsum(g), b == 0)
            e = g * R.vec("mlp_gain")
            hg = r * (e - jnp.mean(e, axis=-1, keepdims=True) - xh * jnp.mean(e * xh, axis=-1, keepdims=True))
            R.hidden[sl, :] = hg
            R.attn_grad[sl, :] = (R.stats[sl, 0:1] * R.picked[sl, :].astype(F32) + hg).astype(BF16)
    for n in range(3):
        @add(f"gatt{n}", 0.45)
        def _(n=n):
            cs = slice(256 * n, 256 * n + 256)
            R.datt[:, cs] = dot(R.attn_grad[...], R.W0(3)[cs, :], NT).astype(BF16)
    for i in range(2):
        sl = slice(CAP * i, CAP * i + CAP)
        for h in range(6):
            @add(f"attb{i}{h}", 1.6)
            def _(i=i, h=h, sl=sl):
                cs = slice(128 * h, 128 * h + 128)
                q, k, v, do = R.proj(0)[sl, cs], R.proj(1)[sl, cs], R.proj(2)[sl, cs], R.datt[sl, cs]
                low = lax.broadcasted_iota(jnp.int32, (CAP, 128), 1) < 64
                live = live_rows(R.lens, i) > 0
                zero = jnp.zeros_like(q)
                q = q * 0.125
                def own(a, u): return jnp.where(low, a, zero) if u == 0 else jnp.where(low, zero, a)
                dq = dk = dv = None
                for u in range(2):
                    qm, km, dm = own(q, u), own(k, u), own(do, u)
                    s = dot(k, qm, NT) - R.lse_row[i, 2 * h + u : 2 * h + u + 1, :]
                    pt = jnp.where(live, jnp.exp(s), 0.0)
                    dp = dot(v, dm, NT)
                    ds = (pt * (dp - colsum(pt * dp))).astype(BF16)
                    a, b, c = dot(pt.astype(BF16), dm), dot(ds, qm), dot(ds, km, TN)
                    dv, dk, dq = (a, b, c) if u == 0 else (dv + a, dk + b, dq + c)
                R.dproj(0)[sl, cs] = (dq * 0.125).astype(BF16)
                R.dproj(1)[sl, cs] = dk.astype(BF16)
                R.dproj(2)[sl, cs] = dv.astype(BF16)
    @add("tn1", 0.6)
    def _(): R.trans[...] = jnp.transpose(R.normed[...])
    for n in range(3):
        @add(f"gqk{n}", 1.2)
        def _(n=n):
            cs = slice(256 * n, 256 * n + 256)
            put_pair(0, 0, cs, dot(R.trans[...], R.dproj(0)[:, cs]), dot(R.trans[...], R.dproj(1)[:, cs]))
    for n in range(3):
        @add(f"gvo{n}", 1.5)
        def _(n=n):
            cs = slice(256 * n, 256 * n + 256)
            put_pair(0, 1, cs, dot(R.trans[...], R.dproj(2)[:, cs]), dot(R.attended[...], R.attn_grad[:, cs], TN))
    for n in range(3):
        @add(f"gn1{n}", 1.3)
        def _(n=n):
            cs = slice(256 * n, 256 * n + 256)
            acc = dot(R.dproj(0)[...], R.W0(0)[cs, :], NT)
            for j in range(1, 3): acc = acc + dot(R.dproj(j)[...], R.W0(j)[cs, :], NT)
            R.tmp[:, cs] = acc
    for b in range(ROWS // B):
        sl = slice(B * b, B * b + B)
        @add(f"ln1b{b}", 0.5)
        def _(sl=sl, b=b):
            g = R.tmp[sl, :]
            ch = R.chosen[sl, :].astype(F32)
            xh, r = ln(ch)
            grow("attn_gain", colsum(g * xh), b == 0)
            grow("attn_shift", colsum(g), b == 0)
            grow("router_weight", colsum(R.stats[sl, 2:3] * ch), b == 0)
            e = g * R.vec("attn_gain")
            cg = r * (e - jnp.mean(e, axis=-1, keepdims=True) - xh * jnp.mean(e * xh, axis=-1, keepdims=True))
            R.attn_grad[sl, :] = (cg + R.hidden[sl, :] + R.stats[sl, 2:3] * R.vec("router_weight")).astype(BF16)
    for n in range(3):
        @add(f"ingrad{n}", 1.0)
        def _(n=n):
            cs = slice(256 * n, 256 * n + 256)
            total = both(R.ct, cs).astype(F32) + dot(R.proj_[0 : 2 * LONG, 0:ROWS], R.attn_grad[:, cs])
            R.input_grad(n, cs, total.astype(BF16).reshape(LONG, 2, 256))
    return T


PHASES = 3
MESH = pl.DeviceIdType.MESH
LINK = {"C": 0, "X": 1, "Y": 2, "P": 3, "Q": 4}
NAMES = ("attn_gain", "attn_shift", "mlp_gain", "mlp_shift", "router_weight", "down_bias")
ROW = {name: k for k, name in enumerate(NAMES)} | {"up_bias": 6}
FEW = (("ZXY", 0, 48), ("ZYX", 48, 48))
SPLIT = 1536
ALSO = (("XZY", 0, 48), ("YZX", 48, 48))
AGROUPS = ((0, 0, 768, ALSO), (3072, 0, 768, FEW), (6144, 0, 768, ALSO))
GROUPS = ((3072, 0, 768, FEW), (0, 0, 768, ALSO), (6144, 0, 256, FEW), (6144, 256, 256, FEW), (6144, 512, 256, FEW))
VSTEPS = "CXYPW"
ZPARTNERS = "PWV"
PLANE = ("C", "X", "Y", "XC", "YC", "XY", "XYC")


def all_events(trees):
    out = []
    size = {"X": 2, "Y": 2, "Z": 4}
    for t, (perm, _, _) in enumerate(trees):
        for a in range(3):
            for o in range(1, size[perm[a]]):
                for combo in itertools.product(*[range(size[q]) for q in perm[:a]]):
                    e = {"X": 0, "Y": 0, "Z": 0}
                    e[perm[a]] = o
                    for q, v in zip(perm[:a], combo):
                        e[q] = v
                    out.append((t, e["X"], e["Y"], e["Z"], a))
    return out


class Place:
    def __init__(self):
        dp = lax.axis_index("dp")
        self.x, self.dp = lax.axis_index("shard"), dp
        self.c, self.y, self.z = dp % 2, (dp // 2) % 2, dp // 4
        z = self.z
        self.mid = ((z + 1) // 2) % 2
        self.zs = [z, z + 1 - 2 * (z % 2), 2 - z // 2, 3 - 3 * (z // 2)]
        self.me = dp * 2 + self.x

    def dev(self, k):
        dp, x = self.dp, self.x
        if k == "C":
            return (dp + 1 - 2 * self.c, x)
        if k == "X":
            return (dp, 1 - x)
        if k == "Y":
            return (dp + 2 - 4 * self.y, x)
        if k in ZPARTNERS or k == "Q":
            z = {"P": self.zs[1], "Q": 3 - self.z, "V": 3 - self.z, "W": (self.z + 2) % 4}[k]
            return (z * 4 + self.y * 2 + self.c, x)
        c = 1 - self.c if "C" in k else self.c
        y = 1 - self.y if "Y" in k else self.y
        return ((self.z * 2 + y) * 2 + c, 1 - x if "X" in k else x)

    def src(self, xo, yo, j):
        sx = self.x if xo == 0 else 1 - self.x
        sy = self.y if yo == 0 else 1 - self.y
        sz = self.zs[j]
        return (sz * 2 + sy) * 2 + sx, ((sz * 2 + sy) * 2 + self.c) * 2 + sx

    def signal(self, sem, kinds):
        for k in kinds:
            if k == "Q":
                @pl.when(self.mid == 1)
                def _():
                    pl.semaphore_signal(sem, inc=1, device_id=self.dev("Q"), device_id_type=MESH)
            else:
                pl.semaphore_signal(sem, inc=1, device_id=self.dev(k), device_id_type=MESH)


class Traffic:
    def __init__(self, pc, ref, send, spare, width=D):
        self.pc, self.ref, self.send, self.spare, self.width = pc, ref, send, spare, width
        self.rows = {}

    def note(self, k, n, where="all"):
        self.rows[(k, where)] = self.rows.get((k, where), 0) + n

    def wait(self):
        def one(k, where):
            rows = self.rows.get((k, where), 0)
            if rows:
                b = self.ref.at[pl.ds(0, rows), pl.ds(0, self.width)]
                pltpu.make_async_remote_copy(b, b, self.send.at[LINK[k]], self.spare, device_id=self.pc.dev("C"), device_id_type=MESH).wait_send()

        for k in "CXY":
            one(k, "all")
        for m, where in ((1, "mid"), (0, "end")):
            @pl.when(self.pc.mid == m)
            def _():
                for k in "PQ":
                    one(k, where)


class Gather:
    def __init__(self, pc, group, buf, recv, crecv, send):
        self.pc, self.buf, self.recv, self.crecv, self.send = pc, buf, recv, crecv, send
        self.base, self.col, self.width, self.trees = AGROUPS[group]
        self.traffic = Traffic(pc, buf, send, crecv, self.width)

    def block(self, t, shard):
        _, r0, n = self.trees[t]
        return self.buf.at[pl.ds(pl.multiple_of(self.base + shard * CH + r0, 16), n), pl.ds(self.col, self.width)]

    def copy(self, t, chip, shard, k):
        b = self.block(t, shard)
        rs = self.crecv if k == "C" else self.recv.at[t, chip]
        return pltpu.make_async_remote_copy(b, b, self.send.at[LINK[k]], rs, device_id=self.pc.dev(k), device_id_type=MESH)

    def forward(self, t, xo, yo, j, last):
        pc, tr = self.pc, self.traffic
        perm, _, n = self.trees[t]
        chip, shard = pc.src(xo, yo, j)
        if perm.index("Z") >= last:
            if j == 0:
                self.copy(t, chip, shard, "P").start()
                tr.note("P", n, "end")
                tr.note("P", n, "mid")
            k = "Q" if j in (0, 1) else "P"
            tr.note(k, n, "mid")

            @pl.when(pc.mid == 1)
            def _():
                self.copy(t, chip, shard, k).start()
        for k in "XY":
            if k in perm[last + 1 :]:
                self.copy(t, chip, shard, k).start()
                tr.note(k, n)
        self.copy(t, chip, shard, "C").start()
        tr.note("C", n)

    def own(self):
        for t in range(len(self.trees)):
            self.forward(t, 0, 0, 0, -1)

    def step(self, ev):
        t, xo, yo, j, a = ev
        chip, shard = self.pc.src(xo, yo, j)
        b = self.block(t, shard)
        pltpu.make_async_remote_copy(b, b, self.send.at[1], self.recv.at[t, chip], device_id=self.pc.dev("X"), device_id_type=MESH).wait_recv()
        self.forward(t, xo, yo, j, a)

    def all_here(self):
        b = self.buf.at[pl.ds(0, 16 * CH), pl.ds(0, self.width)]
        pltpu.make_async_remote_copy(b, b, self.send.at[0], self.crecv, device_id=self.pc.dev("C"), device_id_type=MESH).wait_recv()


class Landing:
    def __init__(self, trees):
        self.off, self.n, self.sem = {}, 0, {}
        for t, (perm, _, n) in enumerate(trees):
            for k in "XY":
                a = perm.index(k)
                other = "Y" if k == "X" else "X"
                for j in range(4):
                    for o in range(2):
                        if (j and perm.index("Z") > a) or (o and perm.index(other) > a):
                            continue
                        self.add((t, k, j, o), n)
            a = perm.index("Z")
            for xo in range(2):
                for yo in range(2):
                    if (xo and perm.index("X") > a) or (yo and perm.index("Y") > a):
                        continue
                    for s in range(5):
                        self.add((t, "Z", xo, yo, s), n)

    def add(self, key, n):
        if self.n < SPLIT < self.n + n:
            self.n = SPLIT
        self.off[key] = self.n
        self.n += n
        self.sem[key] = len(self.sem)


LANDS = {trees: Landing(trees) for trees in (FEW, ALSO)}
LAND_SEMS = max(len(v.sem) for v in LANDS.values())


class Reduce:
    def __init__(self, pc, group, buf, land, cland, recv, crecv, send, done):
        self.pc, self.buf, self.land, self.cland, self.recv, self.crecv, self.send, self.done = pc, buf, land, cland, recv, crecv, send, done
        self.base, self.col, self.width, self.trees = GROUPS[group]
        self.places = LANDS[self.trees]
        self.cdone = set()
        self.traffic = Traffic(pc, buf, send, crecv.at[0], self.width)

    def rows(self, off, n):
        return self.buf.at[pl.ds(pl.multiple_of(self.base + off, 16), n), pl.ds(self.col, self.width)]

    def block(self, t, shard):
        _, r0, n = self.trees[t]
        return self.rows(shard * CH + r0, n)

    def cslot(self, xo, yo, j):
        return (j * 2 + yo) * 2 + xo

    def csend(self, offsets):
        pc = self.pc
        for xo, yo, j in offsets:
            _, shard = pc.src(xo, yo, j)
            s = self.cslot(xo, yo, j)
            pltpu.make_async_remote_copy(
                self.rows((shard + 2 - 4 * pc.c) * CH, CH), self.cland(s * CH, CH),
                self.send.at[0], self.crecv.at[s], device_id=pc.dev("C"), device_id_type=MESH).start()
            self.traffic.note("C", CH)

    def arrive(self, key):
        r = self.land(self.places.off[key], self.trees[key[0]][2])
        pltpu.make_async_remote_copy(r, r, self.send.at[1], self.recv.at[self.places.sem[key]], device_id=self.pc.dev("X"), device_id_type=MESH).wait_recv()
        return r[...].astype(F32)

    def total(self, t, xo, yo, j, last):
        pc = self.pc
        perm, r0, n = self.trees[t]
        _, shard = pc.src(xo, yo, j)
        b = self.block(t, shard)
        s = self.cslot(xo, yo, j)
        if s not in self.cdone:
            self.cdone.add(s)
            r = self.cland(s * CH, CH)
            pltpu.make_async_remote_copy(r, r, self.send.at[0], self.crecv.at[s], device_id=pc.dev("C"), device_id_type=MESH).wait_recv()
        acc = b[...].astype(F32) + self.cland(s * CH + r0, n)[...].astype(F32)
        for k in "XY":
            if k in perm[last + 1 :]:
                acc = acc + self.arrive((t, k, j, yo if k == "X" else xo))
        middle = None
        if perm.index("Z") >= last:
            if j == 0:
                acc = acc + self.arrive((t, "Z", xo, yo, 0))
            middle = (t, "Z", xo, yo, 1 if j == 0 else 1 + j)
        return acc, b, middle

    def own(self):
        for t, (_, r0, n) in enumerate(self.trees):
            acc, _, middle = self.total(t, 0, 0, 0, -1)
            dst = self.done.at[pl.ds(r0, n), pl.ds(self.col, self.width)]
            dst[...] = acc

            @pl.when(self.pc.mid == 1)
            def _():
                dst[...] = dst[...] + self.arrive(middle)

    def step(self, ev):
        pc = self.pc
        t, xo, yo, j, a = ev
        perm, _, n = self.trees[t]
        acc, b, middle = self.total(t, xo, yo, j, a)
        b[...] = acc.astype(BF16)
        if middle is not None:
            @pl.when(pc.mid == 1)
            def _():
                b[...] = (b[...].astype(F32) + self.arrive(middle)).astype(BF16)

        def go(key, k):
            pltpu.make_async_remote_copy(b, self.land(self.places.off[key], n), self.send.at[LINK[k]], self.recv.at[self.places.sem[key]],
                                         device_id=pc.dev(k), device_id_type=MESH).start()

        k = perm[a]
        if k in "XY":
            go((t, k, j, yo if k == "X" else xo), k)
            self.traffic.note(k, n)
        elif j == 1:
            go((t, "Z", xo, yo, 0), "P")
            self.traffic.note("P", n, "end")
            self.traffic.note("P", n, "mid")
        else:
            @pl.when(pc.mid == 0)
            def _():
                go((t, "Z", xo, yo, 1 + j), "P")

            @pl.when(pc.mid == 1)
            def _():
                go((t, "Z", xo, yo, j - 1), "Q")

            self.traffic.note("P", n, "end")
            self.traffic.note("Q", n, "mid")


class SmallSum:
    def __init__(self, pc, total, out, arrived, send, recv):
        self.pc, self.total, self.out, self.arrived, self.send, self.recv = pc, total, out, arrived, send, recv

    def copy(self, k):
        return pltpu.make_async_remote_copy(self.out.at[k], self.arrived.at[k], self.send.at[k], self.recv.at[k],
                                            device_id=self.pc.dev(VSTEPS[k]), device_id_type=MESH)

    def step(self, k):
        if k:
            self.copy(k - 1).wait_recv()
            self.total[...] = self.total[...] + self.arrived[k - 1]
        if k < 5:
            self.out[k] = self.total[...]
            self.copy(k).start()

    def finish(self):
        for k in range(5):
            self.copy(k).wait_send()


class PlaneSum:
    def __init__(self, pc, parts, total, one, two, send, recv):
        self.pc, self.parts, self.total, self.one, self.two, self.send, self.recv = pc, parts, total, one, two, send, recv

    def copy(self, k):
        pc = self.pc
        if k < 7:
            kind = PLANE[k]
            y = 1 - pc.y if "Y" in kind else pc.y
            c = 1 - pc.c if "C" in kind else pc.c
            x = 1 - pc.x if "X" in kind else pc.x
            src, dst = self.parts.at[y * 4 + c * 2 + x], self.one.at[k]
        else:
            kind, src, dst = ZPARTNERS[k - 7], self.total.at[0], self.two.at[k - 7]
        return pltpu.make_async_remote_copy(src, dst, self.send.at[k], self.recv.at[k], device_id=pc.dev(kind), device_id_type=MESH)

    def step(self, k):
        pc = self.pc
        if k == 0:
            for i in range(7):
                self.copy(i).start()
        if k == 1:
            acc = self.parts[pc.y * 4 + pc.c * 2 + pc.x]
            for i in range(7):
                self.copy(i).wait_recv()
                acc = acc + self.one[i]
            self.total[0] = acc
            for i in range(7, 10):
                self.copy(i).start()
        if k == 2:
            acc = self.total[0]
            for i in range(3):
                self.copy(7 + i).wait_recv()
                acc = acc + self.two[i]
            self.total[1] = acc

    def finish(self):
        for k in range(10):
            self.copy(k).wait_send()


def lane(rows, columns, axis):
    return lax.broadcasted_iota(jnp.int32, (rows, columns), axis)


def group24(d):
    return lax.shift_right_logical(d * 2731, 16)


def group96(f):
    return lax.shift_right_logical(f * 683, 16)


def unpack_small(total, vecs):
    v = total[...].astype(BF16)
    d = lane(256, D, 1)
    mine = group24(lane(SH, D, 1)) == lane(SH, D, 0)
    for k in range(6):
        pick = jnp.where(lane(256, D, 0) == 24 * k + d - 24 * group24(d), 1.0, 0.0).astype(BF16)
        vecs[k : k + 1, 0:D] = jnp.sum(jnp.where(mine, dot(v, pick), 0.0), axis=0, keepdims=True)
    pick = jnp.where(lane(256, D, 0) == 144 + d - 96 * group96(d), 1.0, 0.0).astype(BF16)
    wide = dot(v, pick)
    for j in range(4):
        mine = group96(lane(SH, D, 1)) + 8 * j == lane(SH, D, 0)
        vecs[6:7, D * j : D * j + D] = jnp.sum(jnp.where(mine, wide, 0.0), axis=0, keepdims=True)


def pick_dot(a, ones):
    out = None
    for _ in range(3):
        part = a.astype(BF16)
        a = a - part.astype(F32)
        out = dot(part, ones) if out is None else out + dot(part, ones)
    return out


def pack_small(vterm, parts):
    d = lane(D, 128, 0)
    row = lane(64, D, 0)
    shard = (row & 7) * 8 + lax.shift_right_logical(row, 3)
    owner = group24(lane(64, D, 1))
    place = jnp.where(lane(D, 128, 1) == d - 24 * group24(d), 1.0, 0.0).astype(BF16)
    rows = jnp.concatenate([jnp.where(owner == shard, vterm[k : k + 1, 0:D], 0.0) for k in range(6)], axis=0)
    cut = pick_dot(rows, place)
    place = jnp.where(lane(D, 128, 1) == d - 96 * group96(d), 1.0, 0.0).astype(BF16)
    owner = group96(lane(64, D, 1))
    rows = jnp.where(owner == shard, vterm[6:7, 0:D], 0.0)
    for j in range(1, 4):
        rows = rows + jnp.where(owner + 8 * j == shard, vterm[6:7, D * j : D * j + D], 0.0)
    last = pick_dot(rows, place)
    blank = jnp.zeros((64, 128), F32)
    out = jnp.zeros((64, 256), F32)
    for k in range(7):
        wide = jnp.concatenate([cut[64 * k : 64 * k + 64, :] if k < 6 else last, blank], axis=1)
        out = out + (pltpu.roll(wide, 24 * k, 1) if k else wide)
    for k in range(8):
        parts[k] = out[8 * k : 8 * k + 8, :]


SCRATCH = dict(
    G=((PHASES * SH * CH, D), BF16), w0=((SH * CH, D), BF16), w1=((SH * CH, D), BF16), cl2=((16 * CH, D), BF16),
    land12=((LANDS[GROUPS[0][3]].n + LANDS[GROUPS[1][3]].n, D), BF16), act_=((4 * ROWS, D), BF16), gp_=((4 * ROWS, D), BF16), proj_=((3 * ROWS, D), BF16),
    hidden=((ROWS, D), F32), tmp=((ROWS, D), F32), chosen=((ROWS, D), BF16), picked=((ROWS, D), BF16), normed=((ROWS, D), BF16),
    feed=((ROWS, D), BF16), delta=((ROWS, D), BF16), attended=((ROWS, D), BF16), normed_two=((ROWS, D), BF16), attn_grad=((ROWS, D), BF16),
    trans=((D, ROWS), BF16), lse=((2, CAP, 128), F32), lse_row=((2, 16, CAP), F32), stats=((ROWS, 128), F32), tok=((LONG, 2, D), BF16), ct=((LONG, 2, D), BF16), vecs=((8, 4 * D), F32), vterm=((8, 4 * D), F32),
    obuf=((PHASES * CH, D), F32), vtotal=((SH, 256), F32), vout=((5, SH, 256), F32), varr=((5, SH, 256), F32),
    pparts=((8, 8, 256), F32), ptotal=((2, 8, 256), F32), pone=((7, 8, 256), F32), ptwo=((3, 8, 256), F32),
)
SEMS = dict(lsem=(2,), osem=(11,), arecv=(len(AGROUPS), 2, 16), acrecv=(len(AGROUPS),), asend=(len(AGROUPS), 5), rrecv=(len(GROUPS), LAND_SEMS),
            rcrecv=(len(GROUPS), 16), rsend=(len(GROUPS), 5), vsend=(5,), vrecv=(5,), psend=(10,), precv=(10,))
INS = ("sel", "lens", "v0", "v1", "v2", "v3", "v4", "v5", "v6", "qkv_w", "out_w", "up_w", "down_w", "tok_h", "ct_h")
OUTS = ("out_h", "ing_h", "small", "gqkv_h", "gout_h", "gup_h", "gdown_h")


def compute_order():
    out = []

    def tiles(*names):
        out.extend(("tile", name) for name in names)

    def grid(stem, *counts):
        tiles(*[stem + "".join(map(str, at)) for at in itertools.product(*[range(n) for n in counts])])

    grid("pick", 2)
    grid("norm", 6)
    for n in range(3):
        if n == 0:
            out.append(("pd", 0))
        tiles(f"relay0_{n}", *[f"qkv{j}{n}" for j in range(3)])
        tiles(*[f"attn{i}{h}" for h in (2 * n, 2 * n + 1) for i in range(2)])
    grid("out", 3)
    grid("norm2", 6)
    out.append(("pd", 1))
    grid("relay1_", 4)
    grid("up", 4, 3)
    grid("gdown", 4, 3)
    out.append(("csend", 0))
    tiles("bdown")
    out.append(("pd", 2))
    grid("gact", 4, 3)
    grid("down", 3)
    out.extend([("agfin",), ("free",)])
    tiles("tn2")
    grid("gup", 2, 3)
    out.append(("csend", 1))
    grid("gn2", 3)
    grid("ln2b", 6)
    grid("gatt", 3)
    tiles("tn1")
    out.append(("wfree",))
    for n in range(3):
        tiles(*[f"attb{i}{h}" for h in (2 * n, 2 * n + 1) for i in range(2)])
        tiles(f"gqk{n}", f"gvo{n}")
        out.append(("csend", 2 + n))
    grid("gate", 6)
    grid("gn1", 3)
    grid("ln1b", 6)
    tiles("vecpack")
    out.extend(("vstep", 1, k) for k in range(2))
    return out


def catalogue():
    items = [("ag", g, e) for g, group in enumerate(AGROUPS) for e in all_events(group[3])]
    items += [("own", g) for g in range(len(AGROUPS))]
    items += [("rs", g, e) for g, group in enumerate(GROUPS) for e in all_events(group[3])]
    items += [("rsown", g) for g in range(len(GROUPS))]
    items += [("vstep", 0, k) for k in range(5)]
    return items + compute_order() + [("tile", stem + str(n)) for stem in ("output", "ingrad") for n in range(3)]


def mega_kernel(names, order, *refs):
    fields = INS + OUTS + tuple(SCRATCH) + tuple(SEMS) + ("free_c", "free_all")
    R = types.SimpleNamespace(**dict(zip(fields, refs)))
    pc = Place()
    loads = [pltpu.make_async_copy(R.tok_h, R.tok, R.lsem.at[0]), pltpu.make_async_copy(R.ct_h, R.ct, R.lsem.at[1])]
    for cp in loads:
        cp.start()
    barrier = pltpu.get_barrier_semaphore()
    pc.signal(barrier, PLANE + ("P", "W", "V", "Q"))
    for p in range(PHASES):
        if p == 0:
            v = jnp.concatenate([R.qkv_w[:, D * j : D * j + D].astype(F32) for j in range(3)] + [R.out_w[...].astype(F32)], axis=0).astype(BF16)
        elif p == 1:
            v = jnp.concatenate([R.up_w[:, D * j : D * j + D].astype(F32) for j in range(4)], axis=0).astype(BF16)
        else:
            v = R.down_w[...]
        R.G[pl.ds(pl.multiple_of((p * SH + pc.me) * CH, 16), CH), :] = v
    vrow = jnp.concatenate([v[...].astype(F32) for v in (R.v0, R.v1, R.v2, R.v3, R.v4, R.v5, R.v6)] + [jnp.zeros((1, 16), F32)], axis=1)
    R.vtotal[...] = jnp.where(lane(SH, 256, 0) == pc.me, vrow, 0.0)
    pl.semaphore_wait(barrier, 10 + pc.mid)

    ag = [Gather(pc, g, R.G, R.arecv.at[g], R.acrecv.at[g], R.asend.at[g]) for g in range(len(AGROUPS))]

    def landing(g):
        def land(off, n):
            if g < 2:
                return R.land12.at[pl.ds(g * LANDS[GROUPS[0][3]].n + off, n), :]
            cs = pl.ds(GROUPS[g][1], GROUPS[g][2])
            if off < SPLIT:
                return R.w1.at[pl.ds(SPLIT + off, n), cs]
            return R.act_.at[pl.ds(off, n), cs]

        def cland(off, n):
            ref = (R.cl2, R.act_, R.w1)[min(g, 2)]
            return ref.at[pl.ds(off, n), pl.ds(GROUPS[g][1], GROUPS[g][2])]

        return land, cland

    owned = [R.obuf.at[pl.ds(CH * (2 - min(g, 2)), CH), :] for g in range(len(GROUPS))]
    rs = [Reduce(pc, g, R.G, *landing(g), R.rrecv.at[g], R.rcrecv.at[g], R.rsend.at[g], owned[g]) for g in range(len(GROUPS))]
    sums = [SmallSum(pc, R.vtotal, R.vout, R.varr, R.vsend, R.vrecv), PlaneSum(pc, R.pparts, R.ptotal, R.pone, R.ptwo, R.psend, R.precv)]

    R.VEC = {name: (k, D) for name, k in ROW.items()}
    R.VEC["up_bias"] = (ROW["up_bias"], 4 * D)

    def vec(name, off=0, n=None):
        r, w = R.VEC[name]
        return R.vecs[r : r + 1, off : off + (n or w)]

    def view(ref, rows):
        return lambda j: ref.at[pl.ds(rows * j, rows), :]

    R.vec = vec
    R.act, R.gp, R.proj, R.dproj = view(R.act_, ROWS), view(R.gp_, ROWS), view(R.proj_, ROWS), view(R.gp_, ROWS)
    R.W0, R.W1 = view(R.w0, D), view(R.w1, D)
    R.W2 = lambda j: R.G.at[pl.ds(2 * SH * CH + D * j, D), :]
    R.part = lambda p: R.G.at[pl.ds(GROUPS[2 - p][0], SH * CH), :]
    R.change = R.datt = R.feed
    stores = []

    def store(src, dst):
        cp = pltpu.make_async_copy(src, dst, R.osem.at[len(stores)])
        cp.start()
        stores.append(cp)

    def output(n, cs, v):
        R.tok[:, :, cs] = v
        if n == 2:
            store(R.tok, R.out_h)

    def input_grad(n, cs, v):
        R.ct[:, :, cs] = v
        if n == 2:
            store(R.ct, R.ing_h)

    R.output, R.input_grad = output, input_grad
    tiles = {name: f for name, _, _, f in fwd_tiles(R) + bwd_tiles(R)}
    program = [names[k] for k in order]
    offsets = {}
    for it in program:
        if it[0] in ("rs", "rsown"):
            o = it[2][1:4] if it[0] == "rs" else (0, 0, 0)
            if o not in offsets.setdefault(it[1], []):
                offsets[it[1]].append(o)
    finished = set()
    for it in program:
        kind = it[0]
        if kind == "ag":
            ag[it[1]].step(it[2])
        elif kind == "own":
            ag[it[1]].own()
        elif kind == "pd":
            ag[it[1]].all_here()
        elif kind == "rs":
            rs[it[1]].step(it[2])
        elif kind == "rsown":
            g = it[1]
            rs[g].own()
            finished.add(g)
            if g == 0:
                store(owned[g], R.gdown_h)
            elif g == 1:
                for j in range(4):
                    store(owned[g].at[pl.ds(24 * j, 24), :], R.gup_h.at[:, pl.ds(D * j, D)])
            elif finished >= {2, 3, 4}:
                for j in range(3):
                    store(owned[g].at[pl.ds(24 * j, 24), :], R.gqkv_h.at[:, pl.ds(D * j, D)])
                store(owned[g].at[pl.ds(72, 24), :], R.gout_h)
        elif kind == "free":
            pc.signal(R.free_c, "C")
        elif kind == "vstep":
            sums[it[1]].step(it[2])
        elif kind == "csend":
            g = it[1]
            if g == 1:
                pl.semaphore_wait(R.free_c, 1)
            if g == 2:
                pl.semaphore_wait(R.free_all, 4 + pc.mid)
            rs[g].csend(offsets[g])
        elif kind == "tile":
            name = it[1]
            if name == "pick0":
                for cp in loads:
                    cp.wait()
            if name == "norm0":
                sums[0].step(5)
                unpack_small(R.vtotal, R.vecs)
            if name == "vecpack":
                pack_small(R.vterm, R.pparts)
            else:
                if name == "gdown00":
                    ag[1].traffic.wait()
                if name == "gup00":
                    ag[0].traffic.wait()
                if name == "gqk0":
                    ag[2].traffic.wait()
                tiles[name]()
            if name == "gn22":
                pc.signal(R.free_all, "CXYPQ")
    sums[1].step(2)
    R.small[...] = R.ptotal[1, pl.ds(pc.z, 1), :]
    for r in rs:
        r.traffic.wait()
    for s in sums:
        s.finish()
    for cp in stores:
        cp.wait()


def mega(names, order, *args):
    S = jax.ShapeDtypeStruct
    V, H = pl.BlockSpec(memory_space=pltpu.VMEM), pl.BlockSpec(memory_space=pl.ANY)
    outs = [S((LONG, 2, D), BF16), S((LONG, 2, D), BF16), S((1, 256), F32), S((24, 3 * D), F32), S((24, D), F32), S((24, 4 * D), F32), S((96, D), F32)]
    return pl.pallas_call(
        functools.partial(mega_kernel, names, order), out_shape=outs, in_specs=[V] * 13 + [H, H],
        out_specs=[H, H, V, H, H, H, H],
        scratch_shapes=[pltpu.VMEM(*s) for s in SCRATCH.values()] + [pltpu.SemaphoreType.DMA(s) for s in SEMS.values()] + [pltpu.SemaphoreType.REGULAR] * 2,
        compiler_params=pltpu.CompilerParams(collective_id=0, has_side_effects=True, vmem_limit_bytes=VMEM_LIMIT),
        cost_estimate=pl.CostEstimate(flops=26_000_000_000, bytes_accessed=12_000_000, transcendentals=6_000_000),
    )(*args)


def hand_on_kernel(*refs):
    small, srcs, outs, bufs, sems = refs[0], refs[1:7], refs[7:20], refs[20:26], refs[26]
    steps = []
    for k, (src, dst, buf) in enumerate(zip(srcs, outs, bufs)):
        for part in range(2 if k < 2 else 1):
            cut = (lambda r: r.at[pl.ds(288 * part, 288 + part)]) if k < 2 else (lambda r: r)
            n = len(steps)
            there = pltpu.make_async_copy(cut(src), cut(buf), sems.at[0, n])
            there.start()
            steps.append((there, pltpu.make_async_copy(cut(buf), cut(dst), sems.at[1, n])))
    for k in range(7):
        outs[6 + k][...] = small[:, 24 * k : 24 * k + (24 if k < 6 else 96)]
    for there, back in steps:
        there.wait()
        back.start()
    for _, back in steps:
        back.wait()


def hand_on(small, *arrays):
    V, H = pl.BlockSpec(memory_space=pltpu.VMEM), pl.BlockSpec(memory_space=pl.ANY)
    outs = [jax.ShapeDtypeStruct(a.shape, a.dtype) for a in arrays]
    outs += [jax.ShapeDtypeStruct((1, 24 if k < 6 else 96), F32) for k in range(7)]
    return pl.pallas_call(hand_on_kernel, out_shape=outs, in_specs=[V] + [H] * 6, out_specs=[H] * 6 + [V] * 7,
                          scratch_shapes=[pltpu.VMEM(a.shape, a.dtype) for a in arrays] + [pltpu.SemaphoreType.DMA((2, 8))],
                          compiler_params=pltpu.CompilerParams(vmem_limit_bytes=VMEM_LIMIT))(small, *arrays)


ORDER = (
    90, 91, 248, 253, 254, 0, 249, 15, 16, 1, 250, 3, 30, 251, 4, 2, 48, 18, 33, 8, 26, 20, 19, 17,
    11, 23, 252, 255, 5, 52, 6, 45, 37, 21, 13, 53, 256, 39, 31, 257, 38, 258, 10, 12, 24, 9, 22, 46,
    259, 7, 14, 260, 325, 28, 27, 25, 29, 32, 92, 49, 34, 261, 262, 263, 264, 265, 266, 267, 268, 269, 270, 47,
    54, 35, 41, 50, 271, 272, 273, 60, 43, 36, 274, 275, 63, 75, 276, 277, 278, 279, 280, 281, 282, 51, 61, 64,
    283, 284, 78, 55, 58, 76, 285, 286, 287, 79, 56, 40, 71, 67, 42, 57, 82, 62, 86, 44, 59, 288, 289, 290,
    291, 292, 293, 294, 77, 65, 295, 296, 297, 298, 299, 300, 301, 80, 302, 303, 304, 305, 306, 307, 308, 309, 66, 310,
    311, 312, 313, 68, 83, 88, 81, 87, 69, 73, 314, 315, 316, 317, 318, 319, 320, 321, 322, 74, 70, 85, 72, 89,
    84, 323, 324, 326, 327, 328, 329, 330, 331, 332, 333, 334, 335, 336, 337, 338, 339, 340, 341, 100, 107, 106, 120, 105,
    103, 342, 343, 115, 122, 117, 352, 353, 344, 354, 355, 345, 356, 346, 357, 358, 347, 99, 119, 101, 102, 118, 113, 359,
    348, 349, 360, 361, 362, 363, 350, 364, 365, 351, 97, 95, 104, 121, 114, 366, 367, 368, 133, 98, 116, 152, 109, 137,
    369, 370, 371, 149, 372, 110, 131, 373, 112, 146, 150, 135, 128, 167, 93, 374, 375, 376, 377, 378, 144, 147, 134, 180,
    379, 132, 148, 136, 96, 111, 151, 129, 124, 108, 380, 381, 382, 383, 384, 385, 126, 182, 195, 165, 386, 196, 181, 210,
    173, 178, 193, 208, 197, 207, 94, 212, 191, 166, 125, 211, 140, 163, 242, 240, 227, 387, 393, 388, 394, 389, 390, 395,
    174, 238, 223, 192, 243, 143, 225, 189, 206, 176, 241, 226, 179, 391, 392, 396, 397, 164, 159, 234, 127, 187, 204, 161,
    221, 222, 219, 172, 237, 158, 160, 233, 209, 162, 202, 203, 224, 185, 217, 236, 157, 142, 177, 139, 405, 398, 399, 400,
    401, 402, 200, 403, 194, 230, 218, 188, 239, 170, 155, 232, 183, 145, 130, 215, 154, 408, 406, 198, 175, 205, 141, 231,
    138, 214, 123, 186, 404, 184, 220, 199, 169, 235, 201, 216, 229, 213, 190, 228, 156, 153, 168, 171, 409, 410, 407, 244,
    246, 247, 245,
)

VMEM_LIMIT = 63 << 20


def on_device_fast(tokens, lengths, selected, cotangent, attn_gain, attn_shift, mlp_gain, mlp_shift, router_weight,
                   qkv_weight, out_weight, up_weight, up_bias, down_weight, down_bias):
    vectors = [v[None] for v in (attn_gain, attn_shift, mlp_gain, mlp_shift, router_weight, down_bias, up_bias)]
    results = mega(catalogue(), ORDER, selected, lengths.T, *vectors, qkv_weight, out_weight, up_weight, down_weight,
                   tokens[:, 0].transpose(1, 0, 2), cotangent[:, 0].transpose(1, 0, 2))
    output, token_grad, owned, gqkv, gout, gup, gdown = results
    output, token_grad, gqkv, gout, gup, gdown, *t = hand_on(owned, output, token_grad, gqkv, gout, gup, gdown)
    t = [v[0] for v in t]
    whole = lambda v: v.transpose(1, 0, 2)[:, None]
    return (whole(output), whole(token_grad), t[0], t[1], t[2], t[3], t[4], gqkv, gout, gup, t[6], gdown, t[5])


HEADS = 12
HEAD_DIM = 64
MICRO = 2


epsilon = 1e-06


def normalize(inputs, norm_gain, norm_shift):
    centered = inputs - jnp.mean(inputs, axis=-1, keepdims=True)
    variance = jnp.mean(centered * centered, axis=-1, keepdims=True)
    return centered * lax.rsqrt(variance + epsilon) * norm_gain + norm_shift


def forward_pass(tokens, lengths, selected, weights):
    (
        attn_gain,
        attn_shift,
        mlp_gain,
        mlp_shift,
        router_weight,
        qkv_weight,
        out_weight,
        up_weight,
        up_bias,
        down_weight,
        down_bias,
    ) = weights
    group_size, capacity = selected.shape
    counts = lengths // 2
    live_mask = (jnp.arange(capacity)[None, :] < counts[:, None]).astype(jnp.float32)
    chosen = jnp.take_along_axis(tokens, selected[:, :, None], axis=1)
    chosen_wide = chosen.astype(jnp.float32)
    logits = jnp.einsum("bcd,d->bc", chosen, router_weight, preferred_element_type=jnp.float32)
    router_gate = jax.nn.sigmoid(logits)
    normed = normalize(
        chosen_wide, attn_gain.astype(jnp.float32), attn_shift.astype(jnp.float32)
    ).astype(jnp.bfloat16)
    projected = jnp.einsum(
        "bcd,de->bce", normed, qkv_weight, preferred_element_type=jnp.float32
    ).astype(jnp.bfloat16)
    projected = projected.reshape(group_size, capacity, 3, HEADS, HEAD_DIM)
    queries = projected[:, :, 0]
    key_rows = projected[:, :, 1]
    value_rows = projected[:, :, 2]
    score_scale = HEAD_DIM ** (-0.5)
    scores = (
        jnp.einsum("bqhe,bkhe->bhqk", queries, key_rows, preferred_element_type=jnp.float32)
        * score_scale
    )
    scores = jnp.where(live_mask[:, None, None, :] > 0, scores, -1000000000.0)
    row_max = jnp.max(scores, axis=-1, keepdims=True)
    exponent = jnp.exp(scores - row_max)
    row_total = jnp.sum(exponent, axis=-1, keepdims=True)
    attention = (exponent / row_total).astype(jnp.bfloat16)
    log_total = row_max + jnp.log(row_total)
    attended = jnp.einsum(
        "bhqk,bkhe->bqhe", attention, value_rows, preferred_element_type=jnp.float32
    ).astype(jnp.bfloat16)
    attended = attended.reshape(group_size, capacity, HEADS * HEAD_DIM)
    attn_out = jnp.einsum("bce,ed->bcd", attended, out_weight, preferred_element_type=jnp.float32)
    hidden = chosen_wide + attn_out
    normed_two = normalize(
        hidden, mlp_gain.astype(jnp.float32), mlp_shift.astype(jnp.float32)
    ).astype(jnp.bfloat16)
    upward = jnp.einsum(
        "bcd,df->bcf", normed_two, up_weight, preferred_element_type=jnp.float32
    ) + up_bias.astype(jnp.float32)
    active = jax.nn.gelu(upward).astype(jnp.bfloat16)
    feed_out = jnp.einsum(
        "bcf,fd->bcd", active, down_weight, preferred_element_type=jnp.float32
    ) + down_bias.astype(jnp.float32)
    change = (attn_out + feed_out) * (router_gate * live_mask)[:, :, None]
    image_rows = jnp.arange(group_size)[:, None]
    output = tokens.astype(jnp.float32).at[image_rows, selected].add(change).astype(jnp.bfloat16)
    kept_values = (
        chosen_wide,
        live_mask,
        router_gate,
        normed,
        projected,
        log_total,
        attended,
        attn_out,
        hidden,
        normed_two,
        upward,
        active,
        feed_out,
    )
    return (output, kept_values)


def backward_pass(cotangent, selected, weights, kept_values):
    (
        attn_gain,
        attn_shift,
        mlp_gain,
        mlp_shift,
        router_weight,
        qkv_weight,
        out_weight,
        up_weight,
        up_bias,
        down_weight,
        down_bias,
    ) = weights
    (
        chosen_wide,
        live_mask,
        router_gate,
        normed,
        projected,
        log_total,
        attended,
        attn_out,
        hidden,
        normed_two,
        upward,
        active,
        feed_out,
    ) = kept_values
    group_size, capacity = selected.shape
    out_grad = cotangent.astype(jnp.float32)
    picked = jnp.take_along_axis(out_grad, selected[:, :, None], axis=1) * live_mask[:, :, None]
    gate_grad = jnp.sum(picked * (attn_out + feed_out), axis=-1)
    logit_grad = gate_grad * router_gate * (1.0 - router_gate)
    change_grad = picked * router_gate[:, :, None]
    feed_grad = change_grad.astype(jnp.bfloat16)
    down_bias_grad = jnp.sum(feed_grad.astype(jnp.float32), axis=(0, 1))
    down_weight_grad = jnp.einsum(
        "bcf,bcd->fd", active, feed_grad, preferred_element_type=jnp.float32
    )
    active_grad = jnp.einsum(
        "bcd,fd->bcf", feed_grad, down_weight, preferred_element_type=jnp.float32
    )
    primal_out, gelu_back = jax.vjp(jax.nn.gelu, upward)
    upward_grad = gelu_back(active_grad)[0].astype(jnp.bfloat16)
    up_bias_grad = jnp.sum(upward_grad.astype(jnp.float32), axis=(0, 1))
    up_weight_grad = jnp.einsum(
        "bcd,bcf->df", normed_two, upward_grad, preferred_element_type=jnp.float32
    )
    normed_two_grad = jnp.einsum(
        "bcf,df->bcd", upward_grad, up_weight, preferred_element_type=jnp.float32
    )
    primal_two, norm_back = jax.vjp(
        normalize, hidden, mlp_gain.astype(jnp.float32), mlp_shift.astype(jnp.float32)
    )
    hidden_grad, mlp_gain_grad, mlp_shift_grad = norm_back(normed_two_grad)
    attn_grad = (change_grad + hidden_grad).astype(jnp.bfloat16)
    out_weight_grad = jnp.einsum(
        "bce,bcd->ed", attended, attn_grad, preferred_element_type=jnp.float32
    )
    attended_grad = jnp.einsum(
        "bcd,ed->bce", attn_grad, out_weight, preferred_element_type=jnp.float32
    ).astype(jnp.bfloat16)
    attended_grad = attended_grad.reshape(group_size, capacity, HEADS, HEAD_DIM)
    queries = projected[:, :, 0]
    key_rows = projected[:, :, 1]
    value_rows = projected[:, :, 2]
    score_scale = HEAD_DIM ** (-0.5)
    key_live = live_mask[:, None, None, :] > 0
    scores = (
        jnp.einsum("bqhe,bkhe->bhqk", queries, key_rows, preferred_element_type=jnp.float32)
        * score_scale
    )
    scores = jnp.where(key_live, scores, -1000000000.0)
    prob_wide = jnp.exp(scores - log_total)
    prob_low = prob_wide.astype(jnp.bfloat16)
    value_grad = jnp.einsum(
        "bhqk,bqhe->bkhe", prob_low, attended_grad, preferred_element_type=jnp.float32
    )
    prob_grad = jnp.einsum(
        "bqhe,bkhe->bhqk", attended_grad, value_rows, preferred_element_type=jnp.float32
    )
    score_grad = prob_wide * (prob_grad - jnp.sum(prob_wide * prob_grad, axis=-1, keepdims=True))
    score_grad = jnp.where(key_live, score_grad.astype(jnp.bfloat16), 0.0) * score_scale
    query_grad = jnp.einsum(
        "bhqk,bkhe->bqhe", score_grad, key_rows, preferred_element_type=jnp.float32
    )
    key_grad = jnp.einsum(
        "bhqk,bqhe->bkhe", score_grad, queries, preferred_element_type=jnp.float32
    )
    projected_grad = jnp.stack([query_grad, key_grad, value_grad], axis=2).astype(jnp.bfloat16)
    projected_grad = projected_grad.reshape(group_size, capacity, 3 * HEADS * HEAD_DIM)
    qkv_weight_grad = jnp.einsum(
        "bcd,bce->de", normed, projected_grad, preferred_element_type=jnp.float32
    )
    normed_grad = jnp.einsum(
        "bce,de->bcd", projected_grad, qkv_weight, preferred_element_type=jnp.float32
    )
    primal_one, first_back = jax.vjp(
        normalize, chosen_wide, attn_gain.astype(jnp.float32), attn_shift.astype(jnp.float32)
    )
    chosen_grad, attn_gain_grad, attn_shift_grad = first_back(normed_grad)
    chosen_grad = (
        chosen_grad + hidden_grad + logit_grad[:, :, None] * router_weight.astype(jnp.float32)
    )
    router_weight_grad = jnp.einsum(
        "bc,bcd->d", logit_grad, chosen_wide, precision=lax.Precision.HIGHEST
    )
    image_rows = jnp.arange(group_size)[:, None]
    token_grad = out_grad.at[image_rows, selected].add(chosen_grad).astype(jnp.bfloat16)
    grad_terms = (
        attn_gain_grad,
        attn_shift_grad,
        mlp_gain_grad,
        mlp_shift_grad,
        router_weight_grad,
        qkv_weight_grad,
        out_weight_grad,
        up_weight_grad,
        up_bias_grad,
        down_weight_grad,
        down_bias_grad,
    )
    return (token_grad, grad_terms)


def on_device(
    tokens,
    lengths,
    selected,
    cotangent,
    attn_gain,
    attn_shift,
    mlp_gain,
    mlp_shift,
    router_weight,
    qkv_weight,
    out_weight,
    up_weight,
    up_bias,
    down_weight,
    down_bias,
):
    outputs = []
    token_grads = []
    totals = None
    for micro_step in range(MICRO):
        forward_weights = (
            lax.all_gather(attn_gain, ("dp", "shard"), axis=0, tiled=True),
            lax.all_gather(attn_shift, ("dp", "shard"), axis=0, tiled=True),
            lax.all_gather(mlp_gain, ("dp", "shard"), axis=0, tiled=True),
            lax.all_gather(mlp_shift, ("dp", "shard"), axis=0, tiled=True),
            lax.all_gather(router_weight, ("dp", "shard"), axis=0, tiled=True),
            lax.all_gather(qkv_weight, ("dp", "shard"), axis=0, tiled=True),
            lax.all_gather(out_weight, ("dp", "shard"), axis=0, tiled=True),
            lax.all_gather(up_weight, ("dp", "shard"), axis=0, tiled=True),
            lax.all_gather(up_bias, ("dp", "shard"), axis=0, tiled=True),
            lax.all_gather(down_weight, ("dp", "shard"), axis=0, tiled=True),
            lax.all_gather(down_bias, ("dp", "shard"), axis=0, tiled=True),
        )
        output, kept_values = forward_pass(
            tokens[micro_step], lengths[micro_step], selected[micro_step], forward_weights
        )
        backward_weights = (
            lax.all_gather(attn_gain, ("dp", "shard"), axis=0, tiled=True),
            lax.all_gather(attn_shift, ("dp", "shard"), axis=0, tiled=True),
            lax.all_gather(mlp_gain, ("dp", "shard"), axis=0, tiled=True),
            lax.all_gather(mlp_shift, ("dp", "shard"), axis=0, tiled=True),
            lax.all_gather(router_weight, ("dp", "shard"), axis=0, tiled=True),
            lax.all_gather(qkv_weight, ("dp", "shard"), axis=0, tiled=True),
            lax.all_gather(out_weight, ("dp", "shard"), axis=0, tiled=True),
            lax.all_gather(up_weight, ("dp", "shard"), axis=0, tiled=True),
            lax.all_gather(up_bias, ("dp", "shard"), axis=0, tiled=True),
            lax.all_gather(down_weight, ("dp", "shard"), axis=0, tiled=True),
            lax.all_gather(down_bias, ("dp", "shard"), axis=0, tiled=True),
        )
        token_grad, grad_terms = backward_pass(
            cotangent[micro_step], selected[micro_step], backward_weights, kept_values
        )
        grad_terms = (
            lax.psum_scatter(grad_terms[0], ("dp", "shard"), scatter_dimension=0, tiled=True),
            lax.psum_scatter(grad_terms[1], ("dp", "shard"), scatter_dimension=0, tiled=True),
            lax.psum_scatter(grad_terms[2], ("dp", "shard"), scatter_dimension=0, tiled=True),
            lax.psum_scatter(grad_terms[3], ("dp", "shard"), scatter_dimension=0, tiled=True),
            lax.psum_scatter(grad_terms[4], ("dp", "shard"), scatter_dimension=0, tiled=True),
            lax.psum_scatter(grad_terms[5], ("dp", "shard"), scatter_dimension=0, tiled=True),
            lax.psum_scatter(grad_terms[6], ("dp", "shard"), scatter_dimension=0, tiled=True),
            lax.psum_scatter(grad_terms[7], ("dp", "shard"), scatter_dimension=0, tiled=True),
            lax.psum_scatter(grad_terms[8], ("dp", "shard"), scatter_dimension=0, tiled=True),
            lax.psum_scatter(grad_terms[9], ("dp", "shard"), scatter_dimension=0, tiled=True),
            lax.psum_scatter(grad_terms[10], ("dp", "shard"), scatter_dimension=0, tiled=True),
        )
        totals = grad_terms if totals is None else jax.tree.map(jnp.add, totals, grad_terms)
        outputs.append(output)
        token_grads.append(token_grad)
    return (
        jnp.stack(outputs),
        jnp.stack(token_grads),
        totals[0],
        totals[1],
        totals[2],
        totals[3],
        totals[4],
        totals[5],
        totals[6],
        totals[7],
        totals[8],
        totals[9],
        totals[10],
    )


def solution(mesh):
    fits = dict(mesh.shape) == {"dp": 16, "shard": 2}
    return jax.shard_map(
        on_device_fast if fits else on_device,
        mesh=mesh,
        in_specs=(
            P(None, ("dp", "shard"), None, None),
            P(None, ("dp", "shard")),
            P(None, ("dp", "shard"), None),
            P(None, ("dp", "shard"), None, None),
            P(("dp", "shard")),
            P(("dp", "shard")),
            P(("dp", "shard")),
            P(("dp", "shard")),
            P(("dp", "shard")),
            P(("dp", "shard"), None),
            P(("dp", "shard"), None),
            P(("dp", "shard"), None),
            P(("dp", "shard")),
            P(("dp", "shard"), None),
            P(("dp", "shard")),
        ),
        out_specs=(
            P(None, ("dp", "shard"), None, None),
            P(None, ("dp", "shard"), None, None),
            P(("dp", "shard")),
            P(("dp", "shard")),
            P(("dp", "shard")),
            P(("dp", "shard")),
            P(("dp", "shard")),
            P(("dp", "shard"), None),
            P(("dp", "shard"), None),
            P(("dp", "shard"), None),
            P(("dp", "shard")),
            P(("dp", "shard"), None),
            P(("dp", "shard")),
        ),
        check_vma=False,
    )
```

```python
import functools
import itertools
import math
import types

import jax
import jax.numpy as jnp
from jax import lax
from jax.experimental import pallas as pl
from jax.experimental.pallas import tpu as pltpu
from jax.sharding import PartitionSpec as P

F32, BF16 = jnp.float32, jnp.bfloat16
D, ROWS, CAP, LONG = 768, 576, 288, 577
SH, CH = 32, 96
NN = (((1,), (0,)), ((), ()))
NT = (((1,), (1,)), ((), ()))
TN = (((0,), (0,)), ((), ()))
def dot(a, b, dims=NN):
    return lax.dot_general(a, b, dims, preferred_element_type=F32)
def ln(rows):
    centered = rows - jnp.mean(rows, axis=-1, keepdims=True)
    rstd = lax.rsqrt(jnp.mean(centered * centered, axis=-1, keepdims=True) + 1e-6)
    return centered * rstd, rstd
def spread(R):
    place = lax.broadcasted_iota(jnp.int32, (2 * LONG, ROWS), 0)
    return jnp.where(place == jnp.concatenate([2 * R.sel[0], 2 * R.sel[1] + 1], axis=1), 1.0, 0.0).astype(BF16)
def choose(R, i):
    place = lax.broadcasted_iota(jnp.int32, (CAP, 2 * LONG), 1)
    column = jnp.transpose(jnp.broadcast_to((2 * R.sel[i] + i).astype(F32), (8, CAP)))[:, 0:1].astype(jnp.int32)
    return jnp.where(place == column, 1.0, 0.0).astype(BF16)
def both(ref, cs=slice(None)):
    return ref[:, :, cs].reshape(2 * LONG, -1)
def live_rows(lens, i):
    slot = lax.broadcasted_iota(jnp.int32, (CAP, 1), 0)
    return (slot < lax.shift_right_logical(lens[:, i : i + 1], 1)).astype(F32)
def live_cols(lens, i):
    slot = lax.broadcasted_iota(jnp.int32, (1, CAP), 1)
    return slot < lax.shift_right_logical(lens[:, i : i + 1], 1)
def relayout(G, W, p, lo, hi, cs=slice(None)):
    for k in range(lo, hi):
        two = [G[(p * SH + 2 * k + u) * CH : (p * SH + 2 * k + u + 1) * CH, cs].astype(F32) for u in range(2)]
        for j in range(4):
            W[D * j + 48 * k : D * j + 48 * k + 48, cs] = jnp.concatenate([t[24 * j : 24 * j + 24, :] for t in two], axis=0).astype(BF16)
def fwd_tiles(R):
    T = []
    def add(name, cost, dep):
        def deco(f): T.append((name, cost, dep, f)); return f
        return deco
    for i in range(2):
        sl = slice(CAP * i, CAP * i + CAP)
        @add(f"pick{i}", 1.0, "tok")
        def _(i=i, sl=sl):
            oh = choose(R, i)
            R.chosen[sl, :] = dot(oh, both(R.tok)).astype(BF16)
            R.stats[sl, 1:2] = live_rows(R.lens, i)
            R.picked[sl, :] = (dot(oh, both(R.ct)) * R.stats[sl, 1:2]).astype(BF16)
    B = 96
    for b in range(ROWS // B):
        sl = slice(B * b, B * b + B)
        @add(f"norm{b}", 0.4, "vec")
        def _(sl=sl):
            ch = R.chosen[sl, :].astype(F32)
            xh, _ = ln(ch)
            R.normed[sl, :] = (xh * R.vec("ag") + R.vec("as")).astype(BF16)
            logit = jnp.sum(ch * R.vec("rw"), axis=-1, keepdims=True)
            gate = 1.0 / (1.0 + jnp.exp(-logit))
            R.stats[sl, 0:1] = gate
            feed = (gate * R.picked[sl, :].astype(F32)).astype(BF16)
            R.feed[sl, :] = feed
    for g in range(3):
        @add(f"relay0_{g}", 0.4, 0)
        def _(g=g): relayout(R.G, R.w0, 0, 0, 16, slice(256 * g, 256 * g + 256))
    for j in range(3):
        for n in range(3):
            @add(f"qkv{j}{n}", 0.45, 0)
            def _(j=j, n=n):
                cs = slice(256 * n, 256 * n + 256)
                R.proj(j)[:, cs] = dot(R.normed[...], R.W0(j)[:, cs]).astype(BF16)
    for i in range(2):
        sl = slice(CAP * i, CAP * i + CAP)
        for h in range(6):
            @add(f"attn{i}{h}", 1.0, 0)
            def _(i=i, h=h, sl=sl):
                cs = slice(128 * h, 128 * h + 128)
                q, k, v = R.proj(0)[sl, cs], R.proj(1)[sl, cs], R.proj(2)[sl, cs]
                low = lax.broadcasted_iota(jnp.int32, (CAP, 128), 1) < 64
                lane = lax.broadcasted_iota(jnp.int32, (CAP, 128), 1)
                live = live_cols(R.lens, i)
                zero, ones = jnp.zeros_like(q), jnp.ones_like(q)
                q = q * 0.125
                outs = []
                lse = R.lse[i] if h else jnp.zeros((CAP, 128), F32)
                for u in range(2):
                    qm, vm = (jnp.where(low, q, zero), jnp.where(low, v, ones)) if u == 0 else (jnp.where(low, zero, q), jnp.where(low, ones, v))
                    s = jnp.where(live, dot(qm, k, NT), -1e9)
                    m = jnp.max(s, axis=-1, keepdims=True)
                    o = dot(jnp.exp(s - m).astype(BF16), vm)
                    tot = o[:, 64:65] if u == 0 else o[:, 0:1]
                    outs.append(o * (1.0 / tot))
                    lse = jnp.where(lane == 2 * h + u, m + jnp.log(tot), lse)
                R.lse[i] = lse
                R.attended[sl, cs] = jnp.where(low, outs[0], outs[1]).astype(BF16)
                if h == 5:
                    R.lse_row[i] = jnp.transpose(lse)[:16, :]
    for n in range(3):
        @add(f"out{n}", 0.45, 0)
        def _(n=n):
            cs = slice(256 * n, 256 * n + 256)
            R.hidden[:, cs] = R.chosen[:, cs].astype(F32) + dot(R.attended[...], R.W0(3)[:, cs])
    for b in range(ROWS // B):
        sl = slice(B * b, B * b + B)
        @add(f"norm2{b}", 0.3, 0)
        def _(sl=sl):
            xh, _ = ln(R.hidden[sl, :])
            R.normed_two[sl, :] = (xh * R.vec("mg") + R.vec("ms")).astype(BF16)
    for g in range(4):
        @add(f"relay1_{g}", 0.4, 1)
        def _(g=g): relayout(R.G, R.w1, 1, 4 * g, 4 * g + 4)
    c0 = math.sqrt(2.0 / math.pi)
    for j in range(4):
        for n in range(3):
            @add(f"up{j}{n}", 1.2, 1)
            def _(j=j, n=n):
                cs = slice(256 * n, 256 * n + 256)
                u = dot(R.normed_two[...], R.W1(j)[:, cs]) + R.vec("ub", D * j + 256 * n, 256)
                uu = u * u
                half = 0.5 * jnp.tanh(u * (c0 + (c0 * 0.044715) * uu)) + 0.5
                a = u * half
                R.act(j)[:, cs] = a.astype(BF16)
                R.gp(j)[:, cs] = (half + a * (1.0 - half) * (2 * c0 + (6 * c0 * 0.044715) * uu)).astype(BF16)
    for n in range(3):
        @add(f"down{n}", 1.6, 2)
        def _(n=n):
            cs = slice(256 * n, 256 * n + 256)
            acc = R.vec("db", 256 * n, 256) + dot(R.act(0)[...], R.W2(0)[:, cs])
            for j in range(1, 4): acc = acc + dot(R.act(j)[...], R.W2(j)[:, cs])
            R.delta[:, cs] = (acc + (R.hidden[:, cs] - R.chosen[:, cs].astype(F32))).astype(BF16)
    for b in range(ROWS // B):
        sl = slice(B * b, B * b + B)
        @add(f"gate{b}", 0.3, 2)
        def _(sl=sl, b=b):
            if b == 0: R.proj_[0 : 2 * LONG, 0:ROWS] = spread(R)
            d = R.delta[sl, :].astype(F32)
            gate = R.stats[sl, 0:1]
            R.stats[sl, 2:3] = jnp.sum(R.picked[sl, :].astype(F32) * d, axis=-1, keepdims=True) * gate * (1.0 - gate)
            R.change[sl, :] = (d * (gate * R.stats[sl, 1:2])).astype(BF16)
    for n in range(3):
        @add(f"output{n}", 1.0, 2)
        def _(n=n):
            cs = slice(256 * n, 256 * n + 256)
            total = both(R.tok, cs).astype(F32) + dot(R.proj_[0 : 2 * LONG, 0:ROWS], R.change[:, cs])
            R.output(n, cs, total.astype(BF16).reshape(LONG, 2, 256))
    return T


def bwd_tiles(R):
    T = []
    def add(name, cost, dep=None):
        def deco(f): T.append((name, cost, dep, f)); return f
        return deco
    def grow(name, v, first, off=0):
        r, w = R.VEC[name]
        n = v.shape[1]
        if first: R.vterm[r : r + 1, off : off + n] = v
        else: R.vterm[r : r + 1, off : off + n] = R.vterm[r : r + 1, off : off + n] + v
    def colsum(v): return jnp.sum(v, axis=0, keepdims=True)
    def put_pair(p, half, cs, one, two):
        for s in range(SH):
            R.part(p)[s * CH + 48 * half : s * CH + 48 * half + 48, cs] = jnp.concatenate(
                [one[24 * s : 24 * s + 24, :], two[24 * s : 24 * s + 24, :]], axis=0).astype(BF16)
    B = 96
    for j in range(4):
        for n in range(3):
            @add(f"gdown{j}{n}", 0.55)
            def _(j=j, n=n):
                cs = slice(256 * n, 256 * n + 256)
                R.part(2)[D * j + 256 * n : D * j + 256 * n + 256, :] = dot(R.act(j)[:, cs], R.feed[...], TN).astype(BF16)
    @add("bdown", 0.2)
    def _():
        grow("db", colsum(R.feed[...].astype(F32)), True)
    for j in range(4):
        for n in range(3):
            @add(f"gact{j}{n}", 0.6)
            def _(j=j, n=n):
                cs = slice(256 * n, 256 * n + 256)
                g = (dot(R.feed[...], R.W2(j)[cs, :], NT) * R.gp(j)[:, cs].astype(F32)).astype(BF16)
                R.gp(j)[:, cs] = g
                grow("ub", colsum(g.astype(F32)), True, D * j + 256 * n)
    @add("tn2", 0.6)
    def _(): R.trans[...] = jnp.transpose(R.normed_two[...])
    for h in range(2):
        for n in range(3):
            @add(f"gup{h}{n}", 1.2)
            def _(h=h, n=n):
                cs = slice(256 * n, 256 * n + 256)
                put_pair(1, h, cs, dot(R.trans[...], R.gp(2 * h)[:, cs]), dot(R.trans[...], R.gp(2 * h + 1)[:, cs]))
    for n in range(3):
        @add(f"gn2{n}", 1.6)
        def _(n=n):
            cs = slice(256 * n, 256 * n + 256)
            acc = dot(R.gp(0)[...], R.W1(0)[cs, :], NT)
            for j in range(1, 4): acc = acc + dot(R.gp(j)[...], R.W1(j)[cs, :], NT)
            R.tmp[:, cs] = acc
    for b in range(ROWS // B):
        sl = slice(B * b, B * b + B)
        @add(f"ln2b{b}", 0.5)
        def _(sl=sl, b=b):
            g = R.tmp[sl, :]
            xh, r = ln(R.hidden[sl, :])
            grow("mg", colsum(g * xh), b == 0)
            grow("ms", colsum(g), b == 0)
            e = g * R.vec("mg")
            hg = r * (e - jnp.mean(e, axis=-1, keepdims=True) - xh * jnp.mean(e * xh, axis=-1, keepdims=True))
            R.hidden[sl, :] = hg
            R.attn_grad[sl, :] = (R.stats[sl, 0:1] * R.picked[sl, :].astype(F32) + hg).astype(BF16)
    for n in range(3):
        @add(f"gatt{n}", 0.45)
        def _(n=n):
            cs = slice(256 * n, 256 * n + 256)
            R.datt[:, cs] = dot(R.attn_grad[...], R.W0(3)[cs, :], NT).astype(BF16)
    for i in range(2):
        sl = slice(CAP * i, CAP * i + CAP)
        for h in range(6):
            @add(f"attb{i}{h}", 1.6)
            def _(i=i, h=h, sl=sl):
                cs = slice(128 * h, 128 * h + 128)
                q, k, v, do = R.proj(0)[sl, cs], R.proj(1)[sl, cs], R.proj(2)[sl, cs], R.datt[sl, cs]
                low = lax.broadcasted_iota(jnp.int32, (CAP, 128), 1) < 64
                live = live_rows(R.lens, i) > 0
                zero = jnp.zeros_like(q)
                q = q * 0.125
                def own(a, u): return jnp.where(low, a, zero) if u == 0 else jnp.where(low, zero, a)
                dq = dk = dv = None
                for u in range(2):
                    qm, km, dm = own(q, u), own(k, u), own(do, u)
                    s = dot(k, qm, NT) - R.lse_row[i, 2 * h + u : 2 * h + u + 1, :]
                    pt = jnp.where(live, jnp.exp(s), 0.0)
                    dp = dot(v, dm, NT)
                    ds = (pt * (dp - colsum(pt * dp))).astype(BF16)
                    a, b, c = dot(pt.astype(BF16), dm), dot(ds, qm), dot(ds, km, TN)
                    dv, dk, dq = (a, b, c) if u == 0 else (dv + a, dk + b, dq + c)
                R.dproj(0)[sl, cs] = (dq * 0.125).astype(BF16)
                R.dproj(1)[sl, cs] = dk.astype(BF16)
                R.dproj(2)[sl, cs] = dv.astype(BF16)
    @add("tn1", 0.6)
    def _(): R.trans[...] = jnp.transpose(R.normed[...])
    for n in range(3):
        @add(f"gqk{n}", 1.2)
        def _(n=n):
            cs = slice(256 * n, 256 * n + 256)
            put_pair(0, 0, cs, dot(R.trans[...], R.dproj(0)[:, cs]), dot(R.trans[...], R.dproj(1)[:, cs]))
    for n in range(3):
        @add(f"gvo{n}", 1.5)
        def _(n=n):
            cs = slice(256 * n, 256 * n + 256)
            put_pair(0, 1, cs, dot(R.trans[...], R.dproj(2)[:, cs]), dot(R.attended[...], R.attn_grad[:, cs], TN))
    for n in range(3):
        @add(f"gn1{n}", 1.3)
        def _(n=n):
            cs = slice(256 * n, 256 * n + 256)
            acc = dot(R.dproj(0)[...], R.W0(0)[cs, :], NT)
            for j in range(1, 3): acc = acc + dot(R.dproj(j)[...], R.W0(j)[cs, :], NT)
            R.tmp[:, cs] = acc
    for b in range(ROWS // B):
        sl = slice(B * b, B * b + B)
        @add(f"ln1b{b}", 0.5)
        def _(sl=sl, b=b):
            g = R.tmp[sl, :]
            ch = R.chosen[sl, :].astype(F32)
            xh, r = ln(ch)
            grow("ag", colsum(g * xh), b == 0)
            grow("as", colsum(g), b == 0)
            grow("rw", colsum(R.stats[sl, 2:3] * ch), b == 0)
            e = g * R.vec("ag")
            cg = r * (e - jnp.mean(e, axis=-1, keepdims=True) - xh * jnp.mean(e * xh, axis=-1, keepdims=True))
            R.attn_grad[sl, :] = (cg + R.hidden[sl, :] + R.stats[sl, 2:3] * R.vec("rw")).astype(BF16)
    for n in range(3):
        @add(f"ingrad{n}", 1.0)
        def _(n=n):
            cs = slice(256 * n, 256 * n + 256)
            total = both(R.ct, cs).astype(F32) + dot(R.proj_[0 : 2 * LONG, 0:ROWS], R.attn_grad[:, cs])
            R.input_grad(n, cs, total.astype(BF16).reshape(LONG, 2, 256))
    return T


PHASES = 3
MESH = pl.DeviceIdType.MESH
LINK = {"C": 0, "X": 1, "Y": 2, "P": 3, "Q": 4}
NAMES = ("ag", "as", "mg", "ms", "rw", "db")
ROW = {name: k for k, name in enumerate(NAMES)} | {"ub": 6}
FEW = (("ZXY", 0, 48), ("ZYX", 48, 48))
SPLIT = 1536
ALSO = (("XZY", 0, 48), ("YZX", 48, 48))
AGROUPS = ((0, 0, 768, ALSO), (3072, 0, 768, FEW), (6144, 0, 768, ALSO))
GROUPS = ((3072, 0, 768, FEW), (0, 0, 768, ALSO), (6144, 0, 256, FEW), (6144, 256, 256, FEW), (6144, 512, 256, FEW))
VSTEPS = "CXYPW"
ZPARTNERS = "PWV"
PLANE = ("C", "X", "Y", "XC", "YC", "XY", "XYC")


def all_events(trees):
    out = []
    size = {"X": 2, "Y": 2, "Z": 4}
    for t, (perm, _, _) in enumerate(trees):
        for a in range(3):
            for o in range(1, size[perm[a]]):
                for combo in itertools.product(*[range(size[q]) for q in perm[:a]]):
                    e = {"X": 0, "Y": 0, "Z": 0}
                    e[perm[a]] = o
                    for q, v in zip(perm[:a], combo):
                        e[q] = v
                    out.append((t, e["X"], e["Y"], e["Z"], a))
    return out


class Place:
    def __init__(self):
        dp = lax.axis_index("dp")
        self.x, self.dp = lax.axis_index("shard"), dp
        self.c, self.y, self.z = dp % 2, (dp // 2) % 2, dp // 4
        z = self.z
        self.mid = ((z + 1) // 2) % 2
        self.zs = [z, z + 1 - 2 * (z % 2), 2 - z // 2, 3 - 3 * (z // 2)]
        self.me = dp * 2 + self.x

    def dev(self, k):
        dp, x = self.dp, self.x
        if k == "C":
            return (dp + 1 - 2 * self.c, x)
        if k == "X":
            return (dp, 1 - x)
        if k == "Y":
            return (dp + 2 - 4 * self.y, x)
        if k in ZPARTNERS or k == "Q":
            z = {"P": self.zs[1], "Q": 3 - self.z, "V": 3 - self.z, "W": (self.z + 2) % 4}[k]
            return (z * 4 + self.y * 2 + self.c, x)
        c = 1 - self.c if "C" in k else self.c
        y = 1 - self.y if "Y" in k else self.y
        return ((self.z * 2 + y) * 2 + c, 1 - x if "X" in k else x)

    def src(self, xo, yo, j):
        sx = self.x if xo == 0 else 1 - self.x
        sy = self.y if yo == 0 else 1 - self.y
        sz = self.zs[j]
        return (sz * 2 + sy) * 2 + sx, ((sz * 2 + sy) * 2 + self.c) * 2 + sx

    def signal(self, sem, kinds):
        for k in kinds:
            if k == "Q":
                @pl.when(self.mid == 1)
                def _():
                    pl.semaphore_signal(sem, inc=1, device_id=self.dev("Q"), device_id_type=MESH)
            else:
                pl.semaphore_signal(sem, inc=1, device_id=self.dev(k), device_id_type=MESH)


class Traffic:
    def __init__(self, pc, ref, send, spare, width=D):
        self.pc, self.ref, self.send, self.spare, self.width = pc, ref, send, spare, width
        self.rows = {}

    def note(self, k, n, where="all"):
        self.rows[(k, where)] = self.rows.get((k, where), 0) + n

    def wait(self):
        def one(k, where):
            rows = self.rows.get((k, where), 0)
            if rows:
                b = self.ref.at[pl.ds(0, rows), pl.ds(0, self.width)]
                pltpu.make_async_remote_copy(b, b, self.send.at[LINK[k]], self.spare, device_id=self.pc.dev("C"), device_id_type=MESH).wait_send()

        for k in "CXY":
            one(k, "all")
        for m, where in ((1, "mid"), (0, "end")):
            @pl.when(self.pc.mid == m)
            def _():
                for k in "PQ":
                    one(k, where)


class Gather:
    def __init__(self, pc, group, buf, recv, crecv, send):
        self.pc, self.buf, self.recv, self.crecv, self.send = pc, buf, recv, crecv, send
        self.base, self.col, self.width, self.trees = AGROUPS[group]
        self.traffic = Traffic(pc, buf, send, crecv, self.width)

    def block(self, t, shard):
        _, r0, n = self.trees[t]
        return self.buf.at[pl.ds(pl.multiple_of(self.base + shard * CH + r0, 16), n), pl.ds(self.col, self.width)]

    def copy(self, t, chip, shard, k):
        b = self.block(t, shard)
        rs = self.crecv if k == "C" else self.recv.at[t, chip]
        return pltpu.make_async_remote_copy(b, b, self.send.at[LINK[k]], rs, device_id=self.pc.dev(k), device_id_type=MESH)

    def forward(self, t, xo, yo, j, last):
        pc, tr = self.pc, self.traffic
        perm, _, n = self.trees[t]
        chip, shard = pc.src(xo, yo, j)
        if perm.index("Z") >= last:
            if j == 0:
                self.copy(t, chip, shard, "P").start()
                tr.note("P", n, "end")
                tr.note("P", n, "mid")
            k = "Q" if j in (0, 1) else "P"
            tr.note(k, n, "mid")

            @pl.when(pc.mid == 1)
            def _():
                self.copy(t, chip, shard, k).start()
        for k in "XY":
            if k in perm[last + 1 :]:
                self.copy(t, chip, shard, k).start()
                tr.note(k, n)
        self.copy(t, chip, shard, "C").start()
        tr.note("C", n)

    def own(self):
        for t in range(len(self.trees)):
            self.forward(t, 0, 0, 0, -1)

    def step(self, ev):
        t, xo, yo, j, a = ev
        chip, shard = self.pc.src(xo, yo, j)
        b = self.block(t, shard)
        pltpu.make_async_remote_copy(b, b, self.send.at[1], self.recv.at[t, chip], device_id=self.pc.dev("X"), device_id_type=MESH).wait_recv()
        self.forward(t, xo, yo, j, a)

    def all_here(self):
        b = self.buf.at[pl.ds(0, 16 * CH), pl.ds(0, self.width)]
        pltpu.make_async_remote_copy(b, b, self.send.at[0], self.crecv, device_id=self.pc.dev("C"), device_id_type=MESH).wait_recv()


class Landing:
    def __init__(self, trees):
        self.off, self.n, self.sem = {}, 0, {}
        for t, (perm, _, n) in enumerate(trees):
            for k in "XY":
                a = perm.index(k)
                other = "Y" if k == "X" else "X"
                for j in range(4):
                    for o in range(2):
                        if (j and perm.index("Z") > a) or (o and perm.index(other) > a):
                            continue
                        self.add((t, k, j, o), n)
            a = perm.index("Z")
            for xo in range(2):
                for yo in range(2):
                    if (xo and perm.index("X") > a) or (yo and perm.index("Y") > a):
                        continue
                    for s in range(5):
                        self.add((t, "Z", xo, yo, s), n)

    def add(self, key, n):
        if self.n < SPLIT < self.n + n:
            self.n = SPLIT
        self.off[key] = self.n
        self.n += n
        self.sem[key] = len(self.sem)


LANDS = {trees: Landing(trees) for trees in (FEW, ALSO)}
LAND_SEMS = max(len(v.sem) for v in LANDS.values())


class Reduce:
    def __init__(self, pc, group, buf, land, cland, recv, crecv, send, done):
        self.pc, self.buf, self.land, self.cland, self.recv, self.crecv, self.send, self.done = pc, buf, land, cland, recv, crecv, send, done
        self.base, self.col, self.width, self.trees = GROUPS[group]
        self.places = LANDS[self.trees]
        self.cdone = set()
        self.traffic = Traffic(pc, buf, send, crecv.at[0], self.width)

    def rows(self, off, n):
        return self.buf.at[pl.ds(pl.multiple_of(self.base + off, 16), n), pl.ds(self.col, self.width)]

    def block(self, t, shard):
        _, r0, n = self.trees[t]
        return self.rows(shard * CH + r0, n)

    def cslot(self, xo, yo, j):
        return (j * 2 + yo) * 2 + xo

    def csend(self, offsets):
        pc = self.pc
        for xo, yo, j in offsets:
            _, shard = pc.src(xo, yo, j)
            s = self.cslot(xo, yo, j)
            pltpu.make_async_remote_copy(
                self.rows((shard + 2 - 4 * pc.c) * CH, CH), self.cland(s * CH, CH),
                self.send.at[0], self.crecv.at[s], device_id=pc.dev("C"), device_id_type=MESH).start()
            self.traffic.note("C", CH)

    def arrive(self, key):
        r = self.land(self.places.off[key], self.trees[key[0]][2])
        pltpu.make_async_remote_copy(r, r, self.send.at[1], self.recv.at[self.places.sem[key]], device_id=self.pc.dev("X"), device_id_type=MESH).wait_recv()
        return r[...].astype(F32)

    def total(self, t, xo, yo, j, last):
        pc = self.pc
        perm, r0, n = self.trees[t]
        _, shard = pc.src(xo, yo, j)
        b = self.block(t, shard)
        s = self.cslot(xo, yo, j)
        if s not in self.cdone:
            self.cdone.add(s)
            r = self.cland(s * CH, CH)
            pltpu.make_async_remote_copy(r, r, self.send.at[0], self.crecv.at[s], device_id=pc.dev("C"), device_id_type=MESH).wait_recv()
        acc = b[...].astype(F32) + self.cland(s * CH + r0, n)[...].astype(F32)
        for k in "XY":
            if k in perm[last + 1 :]:
                acc = acc + self.arrive((t, k, j, yo if k == "X" else xo))
        middle = None
        if perm.index("Z") >= last:
            if j == 0:
                acc = acc + self.arrive((t, "Z", xo, yo, 0))
            middle = (t, "Z", xo, yo, 1 if j == 0 else 1 + j)
        return acc, b, middle

    def own(self):
        for t, (_, r0, n) in enumerate(self.trees):
            acc, _, middle = self.total(t, 0, 0, 0, -1)
            dst = self.done.at[pl.ds(r0, n), pl.ds(self.col, self.width)]
            dst[...] = acc

            @pl.when(self.pc.mid == 1)
            def _():
                dst[...] = dst[...] + self.arrive(middle)

    def step(self, ev):
        pc = self.pc
        t, xo, yo, j, a = ev
        perm, _, n = self.trees[t]
        acc, b, middle = self.total(t, xo, yo, j, a)
        b[...] = acc.astype(BF16)
        if middle is not None:
            @pl.when(pc.mid == 1)
            def _():
                b[...] = (b[...].astype(F32) + self.arrive(middle)).astype(BF16)

        def go(key, k):
            pltpu.make_async_remote_copy(b, self.land(self.places.off[key], n), self.send.at[LINK[k]], self.recv.at[self.places.sem[key]],
                                         device_id=pc.dev(k), device_id_type=MESH).start()

        k = perm[a]
        if k in "XY":
            go((t, k, j, yo if k == "X" else xo), k)
            self.traffic.note(k, n)
        elif j == 1:
            go((t, "Z", xo, yo, 0), "P")
            self.traffic.note("P", n, "end")
            self.traffic.note("P", n, "mid")
        else:
            @pl.when(pc.mid == 0)
            def _():
                go((t, "Z", xo, yo, 1 + j), "P")

            @pl.when(pc.mid == 1)
            def _():
                go((t, "Z", xo, yo, j - 1), "Q")

            self.traffic.note("P", n, "end")
            self.traffic.note("Q", n, "mid")


class SmallSum:
    def __init__(self, pc, total, out, arrived, send, recv):
        self.pc, self.total, self.out, self.arrived, self.send, self.recv = pc, total, out, arrived, send, recv

    def copy(self, k):
        return pltpu.make_async_remote_copy(self.out.at[k], self.arrived.at[k], self.send.at[k], self.recv.at[k],
                                            device_id=self.pc.dev(VSTEPS[k]), device_id_type=MESH)

    def step(self, k):
        if k:
            self.copy(k - 1).wait_recv()
            self.total[...] = self.total[...] + self.arrived[k - 1]
        if k < 5:
            self.out[k] = self.total[...]
            self.copy(k).start()

    def finish(self):
        for k in range(5):
            self.copy(k).wait_send()


class PlaneSum:
    def __init__(self, pc, parts, total, one, two, send, recv):
        self.pc, self.parts, self.total, self.one, self.two, self.send, self.recv = pc, parts, total, one, two, send, recv

    def copy(self, k):
        pc = self.pc
        if k < 7:
            kind = PLANE[k]
            y = 1 - pc.y if "Y" in kind else pc.y
            c = 1 - pc.c if "C" in kind else pc.c
            x = 1 - pc.x if "X" in kind else pc.x
            src, dst = self.parts.at[y * 4 + c * 2 + x], self.one.at[k]
        else:
            kind, src, dst = ZPARTNERS[k - 7], self.total.at[0], self.two.at[k - 7]
        return pltpu.make_async_remote_copy(src, dst, self.send.at[k], self.recv.at[k], device_id=pc.dev(kind), device_id_type=MESH)

    def step(self, k):
        pc = self.pc
        if k == 0:
            for i in range(7):
                self.copy(i).start()
        if k == 1:
            acc = self.parts[pc.y * 4 + pc.c * 2 + pc.x]
            for i in range(7):
                self.copy(i).wait_recv()
                acc = acc + self.one[i]
            self.total[0] = acc
            for i in range(7, 10):
                self.copy(i).start()
        if k == 2:
            acc = self.total[0]
            for i in range(3):
                self.copy(7 + i).wait_recv()
                acc = acc + self.two[i]
            self.total[1] = acc

    def finish(self):
        for k in range(10):
            self.copy(k).wait_send()


def lane(rows, columns, axis):
    return lax.broadcasted_iota(jnp.int32, (rows, columns), axis)


def group24(d):
    return lax.shift_right_logical(d * 2731, 16)


def group96(f):
    return lax.shift_right_logical(f * 683, 16)


def unpack_small(total, vecs):
    v = total[...].astype(BF16)
    d = lane(256, D, 1)
    mine = group24(lane(SH, D, 1)) == lane(SH, D, 0)
    for k in range(6):
        pick = jnp.where(lane(256, D, 0) == 24 * k + d - 24 * group24(d), 1.0, 0.0).astype(BF16)
        vecs[k : k + 1, 0:D] = jnp.sum(jnp.where(mine, dot(v, pick), 0.0), axis=0, keepdims=True)
    pick = jnp.where(lane(256, D, 0) == 144 + d - 96 * group96(d), 1.0, 0.0).astype(BF16)
    wide = dot(v, pick)
    for j in range(4):
        mine = group96(lane(SH, D, 1)) + 8 * j == lane(SH, D, 0)
        vecs[6:7, D * j : D * j + D] = jnp.sum(jnp.where(mine, wide, 0.0), axis=0, keepdims=True)


def pick_dot(a, ones):
    out = None
    for _ in range(3):
        part = a.astype(BF16)
        a = a - part.astype(F32)
        out = dot(part, ones) if out is None else out + dot(part, ones)
    return out


def pack_small(vterm, parts):
    d = lane(D, 128, 0)
    row = lane(64, D, 0)
    shard = (row & 7) * 8 + lax.shift_right_logical(row, 3)
    owner = group24(lane(64, D, 1))
    place = jnp.where(lane(D, 128, 1) == d - 24 * group24(d), 1.0, 0.0).astype(BF16)
    rows = jnp.concatenate([jnp.where(owner == shard, vterm[k : k + 1, 0:D], 0.0) for k in range(6)], axis=0)
    cut = pick_dot(rows, place)
    place = jnp.where(lane(D, 128, 1) == d - 96 * group96(d), 1.0, 0.0).astype(BF16)
    owner = group96(lane(64, D, 1))
    rows = jnp.where(owner == shard, vterm[6:7, 0:D], 0.0)
    for j in range(1, 4):
        rows = rows + jnp.where(owner + 8 * j == shard, vterm[6:7, D * j : D * j + D], 0.0)
    last = pick_dot(rows, place)
    blank = jnp.zeros((64, 128), F32)
    out = jnp.zeros((64, 256), F32)
    for k in range(7):
        wide = jnp.concatenate([cut[64 * k : 64 * k + 64, :] if k < 6 else last, blank], axis=1)
        out = out + (pltpu.roll(wide, 24 * k, 1) if k else wide)
    for k in range(8):
        parts[k] = out[8 * k : 8 * k + 8, :]


SCRATCH = dict(
    G=((PHASES * SH * CH, D), BF16), w0=((SH * CH, D), BF16), w1=((SH * CH, D), BF16), cl2=((16 * CH, D), BF16),
    land12=((LANDS[GROUPS[0][3]].n + LANDS[GROUPS[1][3]].n, D), BF16), act_=((4 * ROWS, D), BF16), gp_=((4 * ROWS, D), BF16), proj_=((3 * ROWS, D), BF16),
    hidden=((ROWS, D), F32), tmp=((ROWS, D), F32), chosen=((ROWS, D), BF16), picked=((ROWS, D), BF16), normed=((ROWS, D), BF16),
    feed=((ROWS, D), BF16), delta=((ROWS, D), BF16), attended=((ROWS, D), BF16), normed_two=((ROWS, D), BF16), attn_grad=((ROWS, D), BF16),
    trans=((D, ROWS), BF16), lse=((2, CAP, 128), F32), lse_row=((2, 16, CAP), F32), stats=((ROWS, 128), F32), tok=((LONG, 2, D), BF16), ct=((LONG, 2, D), BF16), vecs=((8, 4 * D), F32), vterm=((8, 4 * D), F32),
    obuf=((PHASES * CH, D), F32), vtotal=((SH, 256), F32), vout=((5, SH, 256), F32), varr=((5, SH, 256), F32),
    pparts=((8, 8, 256), F32), ptotal=((2, 8, 256), F32), pone=((7, 8, 256), F32), ptwo=((3, 8, 256), F32),
)
SEMS = dict(lsem=(2,), osem=(11,), arecv=(len(AGROUPS), 2, 16), acrecv=(len(AGROUPS),), asend=(len(AGROUPS), 5), rrecv=(len(GROUPS), LAND_SEMS),
            rcrecv=(len(GROUPS), 16), rsend=(len(GROUPS), 5), vsend=(5,), vrecv=(5,), psend=(10,), precv=(10,))
INS = ("sel", "lens", "v0", "v1", "v2", "v3", "v4", "v5", "v6", "qkv_w", "out_w", "up_w", "down_w", "tok_h", "ct_h")
OUTS = ("out_h", "ing_h", "small", "gqkv_h", "gout_h", "gup_h", "gdown_h")


def compute_order():
    out = []

    def tiles(*names):
        out.extend(("tile", name) for name in names)

    def grid(stem, *counts):
        tiles(*[stem + "".join(map(str, at)) for at in itertools.product(*[range(n) for n in counts])])

    grid("pick", 2)
    grid("norm", 6)
    for n in range(3):
        if n == 0:
            out.append(("pd", 0))
        tiles(f"relay0_{n}", *[f"qkv{j}{n}" for j in range(3)])
        tiles(*[f"attn{i}{h}" for h in (2 * n, 2 * n + 1) for i in range(2)])
    grid("out", 3)
    grid("norm2", 6)
    out.append(("pd", 1))
    grid("relay1_", 4)
    grid("up", 4, 3)
    grid("gdown", 4, 3)
    out.append(("csend", 0))
    tiles("bdown")
    out.append(("pd", 2))
    grid("gact", 4, 3)
    grid("down", 3)
    out.extend([("agfin",), ("free",)])
    tiles("tn2")
    grid("gup", 2, 3)
    out.append(("csend", 1))
    grid("gn2", 3)
    grid("ln2b", 6)
    grid("gatt", 3)
    tiles("tn1")
    out.append(("wfree",))
    for n in range(3):
        tiles(*[f"attb{i}{h}" for h in (2 * n, 2 * n + 1) for i in range(2)])
        tiles(f"gqk{n}", f"gvo{n}")
        out.append(("csend", 2 + n))
    grid("gate", 6)
    grid("gn1", 3)
    grid("ln1b", 6)
    tiles("vecpack")
    out.extend(("vstep", 1, k) for k in range(2))
    return out


def catalogue():
    items = [("ag", g, e) for g, group in enumerate(AGROUPS) for e in all_events(group[3])]
    items += [("own", g) for g in range(len(AGROUPS))]
    items += [("rs", g, e) for g, group in enumerate(GROUPS) for e in all_events(group[3])]
    items += [("rsown", g) for g in range(len(GROUPS))]
    items += [("vstep", 0, k) for k in range(5)]
    return items + compute_order() + [("tile", stem + str(n)) for stem in ("output", "ingrad") for n in range(3)]


def mega_kernel(names, order, *refs):
    fields = INS + OUTS + tuple(SCRATCH) + tuple(SEMS) + ("free_c", "free_all")
    R = types.SimpleNamespace(**dict(zip(fields, refs)))
    pc = Place()
    loads = [pltpu.make_async_copy(R.tok_h, R.tok, R.lsem.at[0]), pltpu.make_async_copy(R.ct_h, R.ct, R.lsem.at[1])]
    for cp in loads:
        cp.start()
    barrier = pltpu.get_barrier_semaphore()
    pc.signal(barrier, PLANE + ("P", "W", "V", "Q"))
    for p in range(PHASES):
        if p == 0:
            v = jnp.concatenate([R.qkv_w[:, D * j : D * j + D].astype(F32) for j in range(3)] + [R.out_w[...].astype(F32)], axis=0).astype(BF16)
        elif p == 1:
            v = jnp.concatenate([R.up_w[:, D * j : D * j + D].astype(F32) for j in range(4)], axis=0).astype(BF16)
        else:
            v = R.down_w[...]
        R.G[pl.ds(pl.multiple_of((p * SH + pc.me) * CH, 16), CH), :] = v
    vrow = jnp.concatenate([v[...].astype(F32) for v in (R.v0, R.v1, R.v2, R.v3, R.v4, R.v5, R.v6)] + [jnp.zeros((1, 16), F32)], axis=1)
    R.vtotal[...] = jnp.where(lane(SH, 256, 0) == pc.me, vrow, 0.0)
    pl.semaphore_wait(barrier, 10 + pc.mid)

    ag = [Gather(pc, g, R.G, R.arecv.at[g], R.acrecv.at[g], R.asend.at[g]) for g in range(len(AGROUPS))]

    def landing(g):
        def land(off, n):
            if g < 2:
                return R.land12.at[pl.ds(g * LANDS[GROUPS[0][3]].n + off, n), :]
            cs = pl.ds(GROUPS[g][1], GROUPS[g][2])
            if off < SPLIT:
                return R.w1.at[pl.ds(SPLIT + off, n), cs]
            return R.act_.at[pl.ds(off, n), cs]

        def cland(off, n):
            ref = (R.cl2, R.act_, R.w1)[min(g, 2)]
            return ref.at[pl.ds(off, n), pl.ds(GROUPS[g][1], GROUPS[g][2])]

        return land, cland

    owned = [R.obuf.at[pl.ds(CH * (2 - min(g, 2)), CH), :] for g in range(len(GROUPS))]
    rs = [Reduce(pc, g, R.G, *landing(g), R.rrecv.at[g], R.rcrecv.at[g], R.rsend.at[g], owned[g]) for g in range(len(GROUPS))]
    sums = [SmallSum(pc, R.vtotal, R.vout, R.varr, R.vsend, R.vrecv), PlaneSum(pc, R.pparts, R.ptotal, R.pone, R.ptwo, R.psend, R.precv)]

    R.VEC = {name: (k, D) for name, k in ROW.items()}
    R.VEC["ub"] = (ROW["ub"], 4 * D)

    def vec(name, off=0, n=None):
        r, w = R.VEC[name]
        return R.vecs[r : r + 1, off : off + (n or w)]

    def view(ref, rows):
        return lambda j: ref.at[pl.ds(rows * j, rows), :]

    R.vec = vec
    R.act, R.gp, R.proj, R.dproj = view(R.act_, ROWS), view(R.gp_, ROWS), view(R.proj_, ROWS), view(R.gp_, ROWS)
    R.W0, R.W1 = view(R.w0, D), view(R.w1, D)
    R.W2 = lambda j: R.G.at[pl.ds(2 * SH * CH + D * j, D), :]
    R.part = lambda p: R.G.at[pl.ds(GROUPS[2 - p][0], SH * CH), :]
    R.change = R.datt = R.feed
    stores = []

    def store(src, dst):
        cp = pltpu.make_async_copy(src, dst, R.osem.at[len(stores)])
        cp.start()
        stores.append(cp)

    def output(n, cs, v):
        R.tok[:, :, cs] = v
        if n == 2:
            store(R.tok, R.out_h)

    def input_grad(n, cs, v):
        R.ct[:, :, cs] = v
        if n == 2:
            store(R.ct, R.ing_h)

    R.output, R.input_grad = output, input_grad
    tiles = {name: f for name, _, _, f in fwd_tiles(R) + bwd_tiles(R)}
    program = [names[k] for k in order]
    offsets = {}
    for it in program:
        if it[0] in ("rs", "rsown"):
            o = it[2][1:4] if it[0] == "rs" else (0, 0, 0)
            if o not in offsets.setdefault(it[1], []):
                offsets[it[1]].append(o)
    finished = set()
    for it in program:
        kind = it[0]
        if kind == "ag":
            ag[it[1]].step(it[2])
        elif kind == "own":
            ag[it[1]].own()
        elif kind == "pd":
            ag[it[1]].all_here()
        elif kind == "rs":
            rs[it[1]].step(it[2])
        elif kind == "rsown":
            g = it[1]
            rs[g].own()
            finished.add(g)
            if g == 0:
                store(owned[g], R.gdown_h)
            elif g == 1:
                for j in range(4):
                    store(owned[g].at[pl.ds(24 * j, 24), :], R.gup_h.at[:, pl.ds(D * j, D)])
            elif finished >= {2, 3, 4}:
                for j in range(3):
                    store(owned[g].at[pl.ds(24 * j, 24), :], R.gqkv_h.at[:, pl.ds(D * j, D)])
                store(owned[g].at[pl.ds(72, 24), :], R.gout_h)
        elif kind == "free":
            pc.signal(R.free_c, "C")
        elif kind == "vstep":
            sums[it[1]].step(it[2])
        elif kind == "csend":
            g = it[1]
            if g == 1:
                pl.semaphore_wait(R.free_c, 1)
            if g == 2:
                pl.semaphore_wait(R.free_all, 4 + pc.mid)
            rs[g].csend(offsets[g])
        elif kind == "tile":
            name = it[1]
            if name == "pick0":
                for cp in loads:
                    cp.wait()
            if name == "norm0":
                sums[0].step(5)
                unpack_small(R.vtotal, R.vecs)
            if name == "vecpack":
                pack_small(R.vterm, R.pparts)
            else:
                if name == "gdown00":
                    ag[1].traffic.wait()
                if name == "gup00":
                    ag[0].traffic.wait()
                if name == "gqk0":
                    ag[2].traffic.wait()
                tiles[name]()
            if name == "gn22":
                pc.signal(R.free_all, "CXYPQ")
    sums[1].step(2)
    R.small[...] = R.ptotal[1, pl.ds(pc.z, 1), :]
    for r in rs:
        r.traffic.wait()
    for s in sums:
        s.finish()
    for cp in stores:
        cp.wait()


def mega(names, order, *args):
    S = jax.ShapeDtypeStruct
    V, H = pl.BlockSpec(memory_space=pltpu.VMEM), pl.BlockSpec(memory_space=pl.ANY)
    outs = [S((LONG, 2, D), BF16), S((LONG, 2, D), BF16), S((1, 256), F32), S((24, 3 * D), F32), S((24, D), F32), S((24, 4 * D), F32), S((96, D), F32)]
    return pl.pallas_call(
        functools.partial(mega_kernel, names, order), out_shape=outs, in_specs=[V] * 13 + [H, H],
        out_specs=[H, H, V, H, H, H, H],
        scratch_shapes=[pltpu.VMEM(*s) for s in SCRATCH.values()] + [pltpu.SemaphoreType.DMA(s) for s in SEMS.values()] + [pltpu.SemaphoreType.REGULAR] * 2,
        compiler_params=pltpu.CompilerParams(collective_id=0, has_side_effects=True, vmem_limit_bytes=VMEM_LIMIT),
        cost_estimate=pl.CostEstimate(flops=26_000_000_000, bytes_accessed=12_000_000, transcendentals=6_000_000),
    )(*args)


def hand_on_kernel(*refs):
    small, srcs, outs, bufs, sems = refs[0], refs[1:7], refs[7:20], refs[20:26], refs[26]
    steps = []
    for k, (src, dst, buf) in enumerate(zip(srcs, outs, bufs)):
        for part in range(2 if k < 2 else 1):
            cut = (lambda r: r.at[pl.ds(288 * part, 288 + part)]) if k < 2 else (lambda r: r)
            n = len(steps)
            there = pltpu.make_async_copy(cut(src), cut(buf), sems.at[0, n])
            there.start()
            steps.append((there, pltpu.make_async_copy(cut(buf), cut(dst), sems.at[1, n])))
    for k in range(7):
        outs[6 + k][...] = small[:, 24 * k : 24 * k + (24 if k < 6 else 96)]
    for there, back in steps:
        there.wait()
        back.start()
    for _, back in steps:
        back.wait()


def hand_on(small, *arrays):
    V, H = pl.BlockSpec(memory_space=pltpu.VMEM), pl.BlockSpec(memory_space=pl.ANY)
    outs = [jax.ShapeDtypeStruct(a.shape, a.dtype) for a in arrays]
    outs += [jax.ShapeDtypeStruct((1, 24 if k < 6 else 96), F32) for k in range(7)]
    return pl.pallas_call(hand_on_kernel, out_shape=outs, in_specs=[V] + [H] * 6, out_specs=[H] * 6 + [V] * 7,
                          scratch_shapes=[pltpu.VMEM(a.shape, a.dtype) for a in arrays] + [pltpu.SemaphoreType.DMA((2, 8))],
                          compiler_params=pltpu.CompilerParams(vmem_limit_bytes=VMEM_LIMIT))(small, *arrays)


ORDER = (
    90, 91, 248, 253, 254, 0, 249, 15, 16, 1, 250, 3, 30, 251, 4, 2, 48, 18, 33, 8, 26, 20, 19, 17,
    11, 23, 252, 255, 5, 52, 6, 45, 37, 21, 13, 53, 256, 39, 31, 257, 38, 258, 10, 12, 24, 9, 22, 46,
    259, 7, 14, 260, 325, 28, 27, 25, 29, 32, 92, 49, 34, 261, 262, 263, 264, 265, 266, 267, 268, 269, 270, 47,
    54, 35, 41, 50, 271, 272, 273, 60, 43, 36, 274, 275, 63, 75, 276, 277, 278, 279, 280, 281, 282, 51, 61, 64,
    283, 284, 78, 55, 58, 76, 285, 286, 287, 79, 56, 40, 71, 67, 42, 57, 82, 62, 86, 44, 59, 288, 289, 290,
    291, 292, 293, 294, 77, 65, 295, 296, 297, 298, 299, 300, 301, 80, 302, 303, 304, 305, 306, 307, 308, 309, 66, 310,
    311, 312, 313, 68, 83, 88, 81, 87, 69, 73, 314, 315, 316, 317, 318, 319, 320, 321, 322, 74, 70, 85, 72, 89,
    84, 323, 324, 326, 327, 328, 329, 330, 331, 332, 333, 334, 335, 336, 337, 338, 339, 340, 341, 100, 107, 106, 120, 105,
    103, 342, 343, 115, 122, 117, 352, 353, 344, 354, 355, 345, 356, 346, 357, 358, 347, 99, 119, 101, 102, 118, 113, 359,
    348, 349, 360, 361, 362, 363, 350, 364, 365, 351, 97, 95, 104, 121, 114, 366, 367, 368, 133, 98, 116, 152, 109, 137,
    369, 370, 371, 149, 372, 110, 131, 373, 112, 146, 150, 135, 128, 167, 93, 374, 375, 376, 377, 378, 144, 147, 134, 180,
    379, 132, 148, 136, 96, 111, 151, 129, 124, 108, 380, 381, 382, 383, 384, 385, 126, 182, 195, 165, 386, 196, 181, 210,
    173, 178, 193, 208, 197, 207, 94, 212, 191, 166, 125, 211, 140, 163, 242, 240, 227, 387, 393, 388, 394, 389, 390, 395,
    174, 238, 223, 192, 243, 143, 225, 189, 206, 176, 241, 226, 179, 391, 392, 396, 397, 164, 159, 234, 127, 187, 204, 161,
    221, 222, 219, 172, 237, 158, 160, 233, 209, 162, 202, 203, 224, 185, 217, 236, 157, 142, 177, 139, 405, 398, 399, 400,
    401, 402, 200, 403, 194, 230, 218, 188, 239, 170, 155, 232, 183, 145, 130, 215, 154, 408, 406, 198, 175, 205, 141, 231,
    138, 214, 123, 186, 404, 184, 220, 199, 169, 235, 201, 216, 229, 213, 190, 228, 156, 153, 168, 171, 409, 410, 407, 244,
    246, 247, 245,
)

VMEM_LIMIT = 63 << 20


def on_device_fast(tokens, lengths, selected, cotangent, attn_gain, attn_shift, mlp_gain, mlp_shift, router_weight,
                   qkv_weight, out_weight, up_weight, up_bias, down_weight, down_bias):
    vectors = [v[None] for v in (attn_gain, attn_shift, mlp_gain, mlp_shift, router_weight, down_bias, up_bias)]
    results = mega(catalogue(), ORDER, selected, lengths.T, *vectors, qkv_weight, out_weight, up_weight, down_weight,
                   tokens[:, 0].transpose(1, 0, 2), cotangent[:, 0].transpose(1, 0, 2))
    output, token_grad, owned, gqkv, gout, gup, gdown = results
    output, token_grad, gqkv, gout, gup, gdown, *t = hand_on(owned, output, token_grad, gqkv, gout, gup, gdown)
    t = [v[0] for v in t]
    whole = lambda v: v.transpose(1, 0, 2)[:, None]
    return (whole(output), whole(token_grad), t[0], t[1], t[2], t[3], t[4], gqkv, gout, gup, t[6], gdown, t[5])


BOTH = ("dp", "shard")
QUERY = "bhqk,bkhe->bqhe"
KEYS = "bhqk,bqhe->bkhe"
SCORE = "bqhe,bkhe->bhqk"
TERM = "bcd,bce->de"
BACK = "bce,de->bcd"
DENSE = "bcd,de->bce"
HEADS = 12
HEAD_DIM = 64
MICRO = 2


epsilon = 1e-06


def normalize(inputs, norm_gain, norm_shift):
    centered = inputs - jnp.mean(inputs, axis=-1, keepdims=True)
    variance = jnp.mean(centered * centered, axis=-1, keepdims=True)
    return centered * lax.rsqrt(variance + epsilon) * norm_gain + norm_shift


def forward_pass(tokens, lengths, selected, weights):
    (
        attn_gain,
        attn_shift,
        mlp_gain,
        mlp_shift,
        router_weight,
        qkv_weight,
        out_weight,
        up_weight,
        up_bias,
        down_weight,
        down_bias,
    ) = weights
    group_size, capacity = selected.shape
    counts = lengths // 2
    live_mask = (jnp.arange(capacity)[None, :] < counts[:, None]).astype(jnp.float32)
    chosen = jnp.take_along_axis(tokens, selected[:, :, None], axis=1)
    chosen_wide = chosen.astype(jnp.float32)
    logits = jnp.einsum("bcd,d->bc", chosen, router_weight, preferred_element_type=jnp.float32)
    router_gate = jax.nn.sigmoid(logits)
    normed = normalize(
        chosen_wide, attn_gain.astype(jnp.float32), attn_shift.astype(jnp.float32)
    ).astype(jnp.bfloat16)
    projected = jnp.einsum(
        DENSE, normed, qkv_weight, preferred_element_type=jnp.float32
    ).astype(jnp.bfloat16)
    projected = projected.reshape(group_size, capacity, 3, HEADS, HEAD_DIM)
    queries = projected[:, :, 0]
    key_rows = projected[:, :, 1]
    value_rows = projected[:, :, 2]
    score_scale = HEAD_DIM ** (-0.5)
    scores = (
        jnp.einsum(SCORE, queries, key_rows, preferred_element_type=jnp.float32)
        * score_scale
    )
    scores = jnp.where(live_mask[:, None, None, :] > 0, scores, -1000000000.0)
    row_max = jnp.max(scores, axis=-1, keepdims=True)
    exponent = jnp.exp(scores - row_max)
    row_total = jnp.sum(exponent, axis=-1, keepdims=True)
    attention = (exponent / row_total).astype(jnp.bfloat16)
    log_total = row_max + jnp.log(row_total)
    attended = jnp.einsum(
        QUERY, attention, value_rows, preferred_element_type=jnp.float32
    ).astype(jnp.bfloat16)
    attended = attended.reshape(group_size, capacity, HEADS * HEAD_DIM)
    attn_out = jnp.einsum(DENSE, attended, out_weight, preferred_element_type=jnp.float32)
    hidden = chosen_wide + attn_out
    normed_two = normalize(
        hidden, mlp_gain.astype(jnp.float32), mlp_shift.astype(jnp.float32)
    ).astype(jnp.bfloat16)
    upward = jnp.einsum(
        DENSE, normed_two, up_weight, preferred_element_type=jnp.float32
    ) + up_bias.astype(jnp.float32)
    active = jax.nn.gelu(upward).astype(jnp.bfloat16)
    feed_out = jnp.einsum(
        DENSE, active, down_weight, preferred_element_type=jnp.float32
    ) + down_bias.astype(jnp.float32)
    change = (attn_out + feed_out) * (router_gate * live_mask)[:, :, None]
    image_rows = jnp.arange(group_size)[:, None]
    output = tokens.astype(jnp.float32).at[image_rows, selected].add(change).astype(jnp.bfloat16)
    kept_values = (
        chosen_wide,
        live_mask,
        router_gate,
        normed,
        projected,
        log_total,
        attended,
        attn_out,
        hidden,
        normed_two,
        upward,
        active,
        feed_out,
    )
    return (output, kept_values)


def backward_pass(cotangent, selected, weights, kept_values):
    (
        attn_gain,
        attn_shift,
        mlp_gain,
        mlp_shift,
        router_weight,
        qkv_weight,
        out_weight,
        up_weight,
        up_bias,
        down_weight,
        down_bias,
    ) = weights
    (
        chosen_wide,
        live_mask,
        router_gate,
        normed,
        projected,
        log_total,
        attended,
        attn_out,
        hidden,
        normed_two,
        upward,
        active,
        feed_out,
    ) = kept_values
    group_size, capacity = selected.shape
    out_grad = cotangent.astype(jnp.float32)
    picked = jnp.take_along_axis(out_grad, selected[:, :, None], axis=1) * live_mask[:, :, None]
    gate_grad = jnp.sum(picked * (attn_out + feed_out), axis=-1)
    logit_grad = gate_grad * router_gate * (1.0 - router_gate)
    change_grad = picked * router_gate[:, :, None]
    feed_grad = change_grad.astype(jnp.bfloat16)
    down_bias_grad = jnp.sum(feed_grad.astype(jnp.float32), axis=(0, 1))
    down_weight_grad = jnp.einsum(
        TERM, active, feed_grad, preferred_element_type=jnp.float32
    )
    active_grad = jnp.einsum(
        BACK, feed_grad, down_weight, preferred_element_type=jnp.float32
    )
    primal_out, gelu_back = jax.vjp(jax.nn.gelu, upward)
    upward_grad = gelu_back(active_grad)[0].astype(jnp.bfloat16)
    up_bias_grad = jnp.sum(upward_grad.astype(jnp.float32), axis=(0, 1))
    up_weight_grad = jnp.einsum(
        TERM, normed_two, upward_grad, preferred_element_type=jnp.float32
    )
    normed_two_grad = jnp.einsum(
        BACK, upward_grad, up_weight, preferred_element_type=jnp.float32
    )
    primal_two, norm_back = jax.vjp(
        normalize, hidden, mlp_gain.astype(jnp.float32), mlp_shift.astype(jnp.float32)
    )
    hidden_grad, mlp_gain_grad, mlp_shift_grad = norm_back(normed_two_grad)
    attn_grad = (change_grad + hidden_grad).astype(jnp.bfloat16)
    out_weight_grad = jnp.einsum(
        TERM, attended, attn_grad, preferred_element_type=jnp.float32
    )
    attended_grad = jnp.einsum(
        BACK, attn_grad, out_weight, preferred_element_type=jnp.float32
    ).astype(jnp.bfloat16)
    attended_grad = attended_grad.reshape(group_size, capacity, HEADS, HEAD_DIM)
    queries = projected[:, :, 0]
    key_rows = projected[:, :, 1]
    value_rows = projected[:, :, 2]
    score_scale = HEAD_DIM ** (-0.5)
    key_live = live_mask[:, None, None, :] > 0
    scores = (
        jnp.einsum(SCORE, queries, key_rows, preferred_element_type=jnp.float32)
        * score_scale
    )
    scores = jnp.where(key_live, scores, -1000000000.0)
    prob_wide = jnp.exp(scores - log_total)
    prob_low = prob_wide.astype(jnp.bfloat16)
    value_grad = jnp.einsum(
        KEYS, prob_low, attended_grad, preferred_element_type=jnp.float32
    )
    prob_grad = jnp.einsum(
        SCORE, attended_grad, value_rows, preferred_element_type=jnp.float32
    )
    score_grad = prob_wide * (prob_grad - jnp.sum(prob_wide * prob_grad, axis=-1, keepdims=True))
    score_grad = jnp.where(key_live, score_grad.astype(jnp.bfloat16), 0.0) * score_scale
    query_grad = jnp.einsum(
        QUERY, score_grad, key_rows, preferred_element_type=jnp.float32
    )
    key_grad = jnp.einsum(
        KEYS, score_grad, queries, preferred_element_type=jnp.float32
    )
    projected_grad = jnp.stack([query_grad, key_grad, value_grad], axis=2).astype(jnp.bfloat16)
    projected_grad = projected_grad.reshape(group_size, capacity, 3 * HEADS * HEAD_DIM)
    qkv_weight_grad = jnp.einsum(
        TERM, normed, projected_grad, preferred_element_type=jnp.float32
    )
    normed_grad = jnp.einsum(
        BACK, projected_grad, qkv_weight, preferred_element_type=jnp.float32
    )
    primal_one, first_back = jax.vjp(
        normalize, chosen_wide, attn_gain.astype(jnp.float32), attn_shift.astype(jnp.float32)
    )
    chosen_grad, attn_gain_grad, attn_shift_grad = first_back(normed_grad)
    chosen_grad = (
        chosen_grad + hidden_grad + logit_grad[:, :, None] * router_weight.astype(jnp.float32)
    )
    router_weight_grad = jnp.einsum(
        "bc,bcd->d", logit_grad, chosen_wide, precision=lax.Precision.HIGHEST
    )
    image_rows = jnp.arange(group_size)[:, None]
    token_grad = out_grad.at[image_rows, selected].add(chosen_grad).astype(jnp.bfloat16)
    grad_terms = (
        attn_gain_grad,
        attn_shift_grad,
        mlp_gain_grad,
        mlp_shift_grad,
        router_weight_grad,
        qkv_weight_grad,
        out_weight_grad,
        up_weight_grad,
        up_bias_grad,
        down_weight_grad,
        down_bias_grad,
    )
    return (token_grad, grad_terms)


def on_device(
    tokens,
    lengths,
    selected,
    cotangent,
    attn_gain,
    attn_shift,
    mlp_gain,
    mlp_shift,
    router_weight,
    qkv_weight,
    out_weight,
    up_weight,
    up_bias,
    down_weight,
    down_bias,
):
    outputs = []
    token_grads = []
    totals = None
    for micro_step in range(MICRO):
        forward_weights = (
            lax.all_gather(attn_gain, BOTH, axis=0, tiled=True),
            lax.all_gather(attn_shift, BOTH, axis=0, tiled=True),
            lax.all_gather(mlp_gain, BOTH, axis=0, tiled=True),
            lax.all_gather(mlp_shift, BOTH, axis=0, tiled=True),
            lax.all_gather(router_weight, BOTH, axis=0, tiled=True),
            lax.all_gather(qkv_weight, BOTH, axis=0, tiled=True),
            lax.all_gather(out_weight, BOTH, axis=0, tiled=True),
            lax.all_gather(up_weight, BOTH, axis=0, tiled=True),
            lax.all_gather(up_bias, BOTH, axis=0, tiled=True),
            lax.all_gather(down_weight, BOTH, axis=0, tiled=True),
            lax.all_gather(down_bias, BOTH, axis=0, tiled=True),
        )
        output, kept_values = forward_pass(
            tokens[micro_step], lengths[micro_step], selected[micro_step], forward_weights
        )
        backward_weights = (
            lax.all_gather(attn_gain, BOTH, axis=0, tiled=True),
            lax.all_gather(attn_shift, BOTH, axis=0, tiled=True),
            lax.all_gather(mlp_gain, BOTH, axis=0, tiled=True),
            lax.all_gather(mlp_shift, BOTH, axis=0, tiled=True),
            lax.all_gather(router_weight, BOTH, axis=0, tiled=True),
            lax.all_gather(qkv_weight, BOTH, axis=0, tiled=True),
            lax.all_gather(out_weight, BOTH, axis=0, tiled=True),
            lax.all_gather(up_weight, BOTH, axis=0, tiled=True),
            lax.all_gather(up_bias, BOTH, axis=0, tiled=True),
            lax.all_gather(down_weight, BOTH, axis=0, tiled=True),
            lax.all_gather(down_bias, BOTH, axis=0, tiled=True),
        )
        token_grad, grad_terms = backward_pass(
            cotangent[micro_step], selected[micro_step], backward_weights, kept_values
        )
        grad_terms = (
            lax.psum_scatter(grad_terms[0], BOTH, scatter_dimension=0, tiled=True),
            lax.psum_scatter(grad_terms[1], BOTH, scatter_dimension=0, tiled=True),
            lax.psum_scatter(grad_terms[2], BOTH, scatter_dimension=0, tiled=True),
            lax.psum_scatter(grad_terms[3], BOTH, scatter_dimension=0, tiled=True),
            lax.psum_scatter(grad_terms[4], BOTH, scatter_dimension=0, tiled=True),
            lax.psum_scatter(grad_terms[5], BOTH, scatter_dimension=0, tiled=True),
            lax.psum_scatter(grad_terms[6], BOTH, scatter_dimension=0, tiled=True),
            lax.psum_scatter(grad_terms[7], BOTH, scatter_dimension=0, tiled=True),
            lax.psum_scatter(grad_terms[8], BOTH, scatter_dimension=0, tiled=True),
            lax.psum_scatter(grad_terms[9], BOTH, scatter_dimension=0, tiled=True),
            lax.psum_scatter(grad_terms[10], BOTH, scatter_dimension=0, tiled=True),
        )
        totals = grad_terms if totals is None else jax.tree.map(jnp.add, totals, grad_terms)
        outputs.append(output)
        token_grads.append(token_grad)
    return (
        jnp.stack(outputs),
        jnp.stack(token_grads),
        totals[0],
        totals[1],
        totals[2],
        totals[3],
        totals[4],
        totals[5],
        totals[6],
        totals[7],
        totals[8],
        totals[9],
        totals[10],
    )


def solution(mesh):
    fits = dict(mesh.shape) == {"dp": 16, "shard": 2}
    return jax.shard_map(
        on_device_fast if fits else on_device,
        mesh=mesh,
        in_specs=(
            P(None, BOTH, None, None),
            P(None, BOTH),
            P(None, BOTH, None),
            P(None, BOTH, None, None),
            P(BOTH),
            P(BOTH),
            P(BOTH),
            P(BOTH),
            P(BOTH),
            P(BOTH, None),
            P(BOTH, None),
            P(BOTH, None),
            P(BOTH),
            P(BOTH, None),
            P(BOTH),
        ),
        out_specs=(
            P(None, BOTH, None, None),
            P(None, BOTH, None, None),
            P(BOTH),
            P(BOTH),
            P(BOTH),
            P(BOTH),
            P(BOTH),
            P(BOTH, None),
            P(BOTH, None),
            P(BOTH, None),
            P(BOTH),
            P(BOTH, None),
            P(BOTH),
        ),
        check_vma=False,
    )
```
